128 devices in a mesh: row: 16 (over x, z), col: 8 (over y, core).
Axes of the slice: x: 4, y: 4, z: 4, core: 2. Of those that a mesh axis runs over, the one named last changes fastest.
Arguments:
- amplitudes: float32 [48, 6, 8, 1296], P('row', None, 'col'), may hold values from -6 to 6
- vvvv: float32 [8, 1296, 10368], P('col', 'row'), may hold values from -0.0625 to 0.0625
- ovov: float32 [1728, 8, 216], P('row', 'col'), may hold values from -0.4375 to 0.4375
- eps_occ: float32 [8, 6], replicated, may hold values from -1 to -0.25
- eps_vir: float32 [8, 36], replicated, may hold values from 0.25 to 1.5
- occ_count: int32 [8], replicated, may hold values from 4 to 6, as said below
- vir_count: int32 [8], replicated, may hold values from 1 to 36, 256 in all
Outputs:
- updated: float32 [48, 6, 8, 1296], P('row', None, 'col')
The draws below stay inside these ranges and needn't reach their ends.
Inputs may be any that keep to these rules, and one draw needn't show every extreme that they name: `occ_count`: every irrep has more than half of its 6 occupied slots live; one irrep has exactly 6. `vir_count`: the entries sum to 256; one of them is exactly 36.
All inputs are finite; a program needn't handle non-finite values.
Results may differ from the reference program's by a relative error of at most 0.00005.
Values sent between devices are 32-bit elements; how exact they have to be, the bound alone decides.
No kernel may reach another device: no remote copies, remote signals or barrier semaphores. Data moves between devices by JAX's collectives and lax.ppermute only.
A program may use at most 128 MiB of HBM per device.

```python
import math
import jax
import jax.numpy as jnp
import numpy as np
from jax import lax

NIRR = 8
NVIR = 256
CAPO = 6
CAPV = 36
PAIRS = 1296
OROWS = 48
KC = 216


def draw_occ_count(key, part):
    key = jax.random.fold_in(key, 11)
    count_key, full_key = jax.random.split(key)
    counts = jax.random.randint(count_key, (NIRR,), CAPO // 2 + 1, CAPO + 1)
    full_irrep = jax.random.randint(full_key, (), 0, NIRR)
    return jnp.where(jnp.arange(NIRR) == full_irrep, CAPO, counts).astype(jnp.int32)


def steps_of(key, extent, pieces, low, largest):
    level, own = 1.0, jax.random.fold_in(key, 6)
    for axis_at, parts in pieces:
        steps = jnp.exp(jax.random.uniform(jax.random.fold_in(own, axis_at), (parts,), jnp.float32, low / len(pieces), largest / len(pieces)))
        level = level * jnp.repeat(steps, extent[axis_at] // parts).reshape([-1 if axis == axis_at else 1 for axis in range(len(extent))])
    return level


def profile(number_of, total, reach, slope):
    loads = [(1 << 20) // math.isqrt(rank ** slope) + 1 for rank in range(2, number_of + 1)]
    spare, given = total - reach - (number_of - 1), [1] * (number_of - 1)
    while spare > 0:
        movable = [i for i in range(number_of - 1) if given[i] < reach]
        mass, remaining = sum([loads[i] for i in movable]), spare
        for i in movable:
            more = min(reach - given[i], max(1, remaining * loads[i] // mass), spare)
            given[i] = given[i] + more
            spare = spare - more
    return np.array([reach] + given)


def uneven_parts(own_key, number_of, total, bound, lean):
    if number_of == 2:
        one = jax.random.randint(own_key, (), max(1, total - bound), min(bound, total - 1) + 1)
        return jnp.stack([one, total - one])
    tallies = jnp.asarray(profile(number_of, total, bound, lean), jnp.int32)
    twos = (number_of - 1) // 2
    giver, receiver = tallies[1:1 + 2 * twos:2], tallies[2:2 + 2 * twos:2]
    room = jnp.minimum(giver - 1, bound - receiver)
    shifted = jax.random.randint(jax.random.fold_in(own_key, 1), (twos,), 0, 1 << 20) % (room + 1)
    tallies = tallies.at[1:1 + 2 * twos:2].set(giver - shifted).at[2:2 + 2 * twos:2].set(receiver + shifted)
    return tallies[jax.random.permutation(jax.random.fold_in(own_key, 2), number_of)]


def scatter_about(rng, shape, width, bound, shards=(), kind=jnp.bfloat16):
    result = jax.random.normal(rng, shape, jnp.float32) * width
    if len(shards) > 0:
        result = steps_of(rng, shape, shards, -0.22, 0.18) * result
    return jnp.clip(result, min=-bound, max=bound).astype(kind)


def setup_inputs(seed: int = 0) -> dict:
    key_list = jax.random.split(jax.random.key(seed), 8)
    return {
        "amplitudes": scatter_about(key_list[0], (OROWS, CAPO, NIRR, PAIRS), 1.0, 6.0, ((0, 16), (2, 8)), jnp.float32),
        "vvvv": scatter_about(key_list[1], (NIRR, PAIRS, NIRR * PAIRS), (NIRR * PAIRS) ** -0.5, 0.0625, ((0, 8), (1, 16)), jnp.float32),
        "ovov": scatter_about(key_list[2], (NIRR * KC, NIRR, KC), KC ** -0.5, 0.4375, ((0, 16), (1, 8)), jnp.float32),
        "eps_occ": jnp.clip(jax.random.uniform(key_list[3], (NIRR, CAPO), jnp.float32, -1.0, -0.25), -1.0, -0.25),
        "eps_vir": jnp.clip(jax.random.uniform(key_list[4], (NIRR, CAPV), jnp.float32, 0.25, 1.5), 0.25, 1.5),
        "occ_count": draw_occ_count(jax.random.fold_in(key_list[7], 71), 0),
        "vir_count": uneven_parts(key_list[6], NIRR, NVIR, CAPV, 0).astype(jnp.int32),
    }


def slot_masks(occ_count, vir_count):
    occ_live = (jnp.arange(CAPO)[None, :] < occ_count[:, None]).astype(jnp.float32)
    vir_live = (jnp.arange(CAPV)[None, :] < vir_count[:, None]).astype(jnp.float32)
    return occ_live, vir_live


def reference(amplitudes, vvvv, ovov, eps_occ, eps_vir, occ_count, vir_count):
    occ_live, vir_live = slot_masks(occ_count, vir_count)
    live_mask = (occ_live[:, :, None, None, None, None] * occ_live[:, None, :, None, None, None]
                 * vir_live[None, None, None, :, :, None] * vir_live[None, None, None, :, None, :])
    amplitude_live = amplitudes.reshape(NIRR, CAPO, CAPO, NIRR, CAPV, CAPV) * live_mask
    flat_amps = amplitude_live.reshape(NIRR * CAPO * CAPO, NIRR * CAPV * CAPV)

    def ladder_block(integral_block):
        return jnp.dot(flat_amps, integral_block.T, precision=lax.Precision.HIGHEST,
                       preferred_element_type=jnp.float32)

    ladder = lax.map(ladder_block, vvvv)
    ladder = jnp.transpose(ladder, (1, 0, 2)).reshape(NIRR, CAPO, CAPO, NIRR, CAPV, CAPV)
    cycle_integral = ovov.reshape(NIRR, CAPO, CAPV, NIRR, CAPO, CAPV)
    cycle_term = jnp.einsum('hikgac,hkcgjb->hijgab', amplitude_live, cycle_integral, precision=lax.Precision.HIGHEST)
    energy_gap = (eps_occ[:, :, None, None, None, None] + eps_occ[:, None, :, None, None, None]
                  - eps_vir[None, None, None, :, :, None] - eps_vir[None, None, None, :, None, :])
    updated = live_mask * (ladder + cycle_term) / energy_gap
    return updated.reshape(NIRR * CAPO, CAPO, NIRR, CAPV * CAPV)
```

```python
import jax
import jax.numpy as jnp
from jax import lax
from jax.experimental import pallas as pl
from jax.experimental.pallas import tpu as pltpu
from jax.sharding import Mesh, PartitionSpec as P

AXES = ("x", "z", "y", "core")
SHIFTS = (1, -1, 2)
STEPS = (0, 1, -1, 2)
LANES = 128
TILES = 11
WINDOW = TILES * LANES
PAIR_WINDOW = 21 * LANES
MAIN = 8 * TILES
SHARD = 104
PAIR = 200
QUAD = 2 * PAIR
F32 = jnp.float32
BF16 = jnp.bfloat16
ANY = pl.BlockSpec(memory_space=pl.ANY)
SMEM = pl.BlockSpec(memory_space=pltpu.SMEM)
VMEM = pl.BlockSpec(memory_space=pltpu.VMEM)
PARAMS = pltpu.CompilerParams(vmem_limit_bytes=50 * 1024 * 1024)


def shift(value, axis_of_core0, axis_of_core1, step):
    pairs = []
    for x in range(4):
        for z in range(4):
            for y in range(4):
                for core in range(2):
                    here = {"x": x, "z": z, "y": y, "core": core}
                    there = dict(here)
                    axis = axis_of_core1 if core else axis_of_core0
                    there[axis] = (there[axis] + step) % 4
                    place = [((p["x"] * 4 + p["z"]) * 4 + p["y"]) * 2 + p["core"] for p in (here, there)]
                    pairs.append(tuple(place))
    return lax.ppermute(value, AXES, pairs)


def swap_core(value):
    return lax.ppermute(value, "core", [(0, 1), (1, 0)])


def pack_shard(place, occ, vir, amp, keep, send, wide):
    x, z, y, core = place[0], place[1], place[2], place[3]
    row_place = x * 4 + z
    occ_here = occ[row_place >> 1]
    first = 3 * (row_place & 1)
    irrep = 2 * y + core
    vir_here = vir[irrep]
    wide[...] = jnp.zeros_like(wide)
    for row in range(18):
        wide[row : row + 1, 0:1296] = amp[row // 6, row % 6]
    lane = lax.broadcasted_iota(jnp.int32, wide.shape, 1)
    row = lax.broadcasted_iota(jnp.int32, wide.shape, 0)
    a = jnp.floor((lane.astype(F32) + 0.5) * (1.0 / 36.0)).astype(jnp.int32)
    b = lane - 36 * a
    i_low = (row * 43) >> 8
    j = row - 6 * i_low
    i = i_low + first
    live = (a < vir_here) & (b < vir_here) & (i < occ_here) & (j < occ_here)
    moved = pltpu.roll(jnp.where(live, wide[...], 0.0), 16 * irrep, 1)

    def write(ref, half):
        for t in range(TILES):
            columns = slice(t * LANES, (t + 1) * LANES)
            ref[8 * t : 8 * t + 8, :] = moved[8 * half : 8 * half + 8, columns]
            ref[MAIN + t : MAIN + t + 1, :] = moved[16 + half : 17 + half, columns]
        ref[MAIN + TILES : SHARD, :] = jnp.zeros((SHARD - MAIN - TILES, LANES), F32)

    @pl.when(core == 0)
    def _():
        write(keep, 0)
        write(send, 1)

    @pl.when(core == 1)
    def _():
        write(keep, 1)
        write(send, 0)


def pack_pair(own, other, out):
    out[0:MAIN, :] = own[0:MAIN, :]
    out[MAIN : 2 * MAIN, :] = other[0:MAIN, :]
    out[2 * MAIN : 2 * MAIN + TILES, :] = own[MAIN : MAIN + TILES, :]
    out[2 * MAIN + TILES : 2 * MAIN + 2 * TILES, :] = other[MAIN : MAIN + TILES, :]
    out[2 * MAIN + 2 * TILES : PAIR, :] = jnp.zeros((2, LANES), F32)


def join(*refs):
    out = refs[-1]
    at = 0
    for ref in refs[:-1]:
        rows = ref.shape[0]
        out[at : at + rows, :] = ref[...]
        at += rows


def join_call(*arrays):
    rows = sum(array.shape[0] for array in arrays)
    return pl.pallas_call(
        join,
        out_shape=jax.ShapeDtypeStruct((rows, LANES), F32),
        in_specs=[VMEM] * len(arrays),
        out_specs=VMEM,
        compiler_params=PARAMS,
    )(*arrays)


def cut_windows(place, integrals, gate, up, down, sems):
    y = place[2]
    copies = []
    for at, (ref, step) in enumerate(((up, 1), (down, 3))):
        start = pl.multiple_of(((y + step) & 3) * 2560, LANES)
        copies.append(
            pltpu.make_async_copy(integrals.at[:, :, pl.ds(start, PAIR_WINDOW)], ref, sems.at[at])
        )
    for copy in copies:
        copy.start()
    for copy in copies:
        copy.wait()


def split_turned(block, wide, high, low, first, column):
    wide[0:81, :] = block
    turned = wide[...].T
    upper = turned.astype(BF16)
    high[first : first + WINDOW, column : column + LANES] = upper
    low[first : first + WINDOW, column : column + LANES] = (turned - upper.astype(F32)).astype(BF16)


def turn_local(place, own, other, high, low, wide):
    y, core = place[2], place[3]
    wide[...] = jnp.zeros_like(wide)
    for pair in range(2):
        chip = (y + 2 * pair) & 3
        for side in range(2):
            irrep = 2 * chip + (core if side == 0 else 1 - core)
            start = pl.multiple_of(irrep * 1280, LANES)
            for column, ref in enumerate((own, other)):
                split_turned(
                    ref[:, pl.ds(start, WINDOW)], wide, high, low,
                    (2 * pair + side) * WINDOW, column * LANES,
                )


def turn_moved(place, own, other, high, low, wide):
    core = place[3]
    wide[...] = jnp.zeros_like(wide)
    for side in range(2):
        start = pl.multiple_of((core if side == 0 else 1 - core) * 1280, LANES)
        for column, ref in enumerate((own, other)):
            split_turned(
                ref[:, pl.ds(start, WINDOW)], wide, high, low, side * WINDOW, column * LANES
            )


def turn_call(kernel, place, own, other, depth):
    return pl.pallas_call(
        kernel,
        out_shape=[jax.ShapeDtypeStruct((depth, 2 * LANES), BF16)] * 2,
        in_specs=[SMEM, VMEM, VMEM],
        out_specs=[VMEM, VMEM],
        scratch_shapes=[pltpu.VMEM((LANES, WINDOW), F32)],
        compiler_params=PARAMS,
    )(place, own, other)


def multiply(b0, b1, b2, b3, local_high, local_low, up_high, up_low, down_high, down_low,
             local_sum, up_sum, down_sum, extra):
    blocks = (b0, b1, b2, b3)
    depth = 2 * WINDOW
    for pair in range(2):
        for t in range(2 * TILES):
            row = PAIR * pair + 2 * MAIN + t
            at = (pair * 2 * TILES + t) * LANES
            for d, block in enumerate(blocks):
                extra[4 * d : 4 * d + 4, at : at + LANES] = block[pl.ds(row, 4, stride=QUAD), :]
    total = None
    for pair in range(2):
        rows = []
        for block in blocks:
            for e in range(4):
                base = e * QUAD + pair * PAIR
                rows.append(
                    jnp.concatenate(
                        [block[base + 8 * t : base + 8 * t + 8, :] for t in range(2 * TILES)], axis=1
                    )
                )
        rows.append(extra[:, pair * depth : (pair + 1) * depth])
        left = jnp.concatenate(rows, axis=0)
        high = left.astype(BF16)
        low = (left - high.astype(F32)).astype(BF16)

        def product(right_high, right_low):
            dot = lambda p, q: jnp.dot(p, q, preferred_element_type=F32)
            return dot(high, right_high) + (dot(low, right_high) + dot(high, right_low))

        here = product(
            local_high[pair * depth : (pair + 1) * depth, :],
            local_low[pair * depth : (pair + 1) * depth, :],
        )
        total = here if total is None else total + here
        if pair == 0:
            up_sum[...] = product(up_high[...], up_low[...])
            down_sum[...] = product(down_high[...], down_low[...])
    local_sum[...] = total


def address(place, local_sum, up_sum, down_sum, out):
    x, z, core = place[0], place[1], place[3]
    total = local_sum[...] + up_sum[...] + down_sum[...]
    lane = lax.broadcasted_iota(jnp.int32, (8, LANES), 1)
    row = lax.broadcasted_iota(jnp.int32, (8, LANES), 0)
    for side in range(2):
        columns = slice(side * LANES, (side + 1) * LANES)
        last = total[128:144, columns]
        last_a = pltpu.roll(last, 81, 1)
        last_b = pltpu.roll(last, 34, 1)
        core_there = core if side == 0 else 1 - core
        for d in range(4):
            for e in range(4):
                s = 4 * d + e
                x_step = jnp.where(core == 0, STEPS[e], STEPS[d])
                z_step = jnp.where(core == 0, STEPS[d], STEPS[e])
                there = ((x - x_step) & 3) * 4 + ((z - z_step) & 3)
                main = total[8 * s : 8 * s + 8, columns]
                tail = jnp.where(row == 0, last_a[s : s + 1, :], last_b[s : s + 1, :])
                out[there * 2 + core_there] = jnp.where(lane < 81, main, tail)


def finish(sums, scale, offset, out, wide):
    wide[...] = jnp.zeros_like(wide)
    lane8 = lax.broadcasted_iota(jnp.int32, (1, LANES), 1)
    lane = lax.broadcasted_iota(jnp.int32, (24, LANES), 1)
    for r in range(16):
        mains, lasts = [], []
        for core in range(2):
            block = sums[2 * r + core]
            mains.append(block)
            lasts.append(
                jnp.where(lane8 < 47, pltpu.roll(block, 47, 1)[0:1, :], pltpu.roll(block, 94, 1)[1:2, :])
            )
        stack = jnp.concatenate(mains + lasts + [jnp.zeros((6, LANES), F32)], axis=0)
        tile, start = divmod(81 * r, LANES)
        turned = pltpu.roll(stack, start, 1) if start else stack
        here = slice(tile * LANES, (tile + 1) * LANES)
        wide[:, here] = jnp.where((lane >= start) & (lane < start + 81), turned, wide[:, here])
        if start + 81 > LANES:
            after = slice((tile + 1) * LANES, (tile + 2) * LANES)
            wide[:, after] = jnp.where(lane < start + 81 - LANES, turned, wide[:, after])
    out[...] = wide[0:18, 0:1296] * scale[...] + offset[...]


def local_terms(amplitudes, ovov, eps_occ, eps_vir, occ_count, vir_count, x, z, y, core):
    row_place = x * 4 + z
    col_place = y * 2 + core
    occ_slots, vir_slots = eps_occ.shape[1], eps_vir.shape[1]
    occ_live = (jnp.arange(occ_slots)[None, :] < occ_count[:, None]).astype(F32)
    vir_live = (jnp.arange(vir_slots)[None, :] < vir_count[:, None]).astype(F32)
    shell = row_place // 2
    first = row_place * 3
    occ_rows = lax.dynamic_slice_in_dim(occ_live.reshape(-1), first, 3)
    energy_rows = lax.dynamic_slice_in_dim(eps_occ.reshape(-1), first, 3)
    occ_cols = lax.dynamic_slice_in_dim(occ_live, shell, 1, 0)[0]
    energy_cols = lax.dynamic_slice_in_dim(eps_occ, shell, 1, 0)[0]
    vir_here = lax.dynamic_slice_in_dim(vir_live, col_place, 1, 0)[0]
    vir_energy = lax.dynamic_slice_in_dim(eps_vir, col_place, 1, 0)[0]
    mask = (
        occ_rows[:, None, None, None]
        * occ_cols[None, :, None, None]
        * vir_here[None, None, :, None]
        * vir_here[None, None, None, :]
    )
    live = amplitudes.reshape(3, occ_slots, vir_slots, vir_slots) * mask
    partner = lax.ppermute(ovov, "z", [(0, 1), (1, 0), (2, 3), (3, 2)])
    panel = jnp.where(
        row_place % 2 == 0,
        jnp.concatenate([ovov, partner], 0),
        jnp.concatenate([partner, ovov], 0),
    )
    panel = panel.reshape(occ_slots, vir_slots, occ_slots, vir_slots)
    cycle = jnp.einsum("ikac,kcjb->ijab", live, panel, precision=lax.Precision.HIGHEST)
    gap = (
        energy_rows[:, None, None, None]
        + energy_cols[None, :, None, None]
        - vir_energy[None, None, :, None]
        - vir_energy[None, None, None, :]
    )
    scale = mask / gap
    return scale.reshape(18, 1296), (scale * cycle).reshape(18, 1296)


def on_device(amplitudes, vvvv, ovov, eps_occ, eps_vir, occ_count, vir_count):
    x, z, y, core = (lax.axis_index(name) for name in AXES)
    place = jnp.stack([x, z, y, core]).astype(jnp.int32)
    integrals = vvvv.reshape(81, 1, 10368)
    flat = vvvv.reshape(81, 10368)

    keep, send = pl.pallas_call(
        pack_shard,
        out_shape=[jax.ShapeDtypeStruct((SHARD, LANES), F32)] * 2,
        in_specs=[SMEM, SMEM, SMEM, VMEM],
        out_specs=[VMEM, VMEM],
        scratch_shapes=[pltpu.VMEM((24, WINDOW), F32)],
        compiler_params=PARAMS,
    )(place, occ_count, vir_count, amplitudes)
    got = swap_core(send)
    pair = pl.pallas_call(
        pack_pair,
        out_shape=jax.ShapeDtypeStruct((PAIR, LANES), F32),
        in_specs=[VMEM, VMEM],
        out_specs=VMEM,
        compiler_params=PARAMS,
    )(keep, got)
    far = shift(pair, "y", "y", 2)
    quad = join_call(pair, far)

    up, down = pl.pallas_call(
        cut_windows,
        out_shape=[jax.ShapeDtypeStruct((81, 1, PAIR_WINDOW), F32)] * 2,
        in_specs=[SMEM, ANY, ANY],
        out_specs=[ANY, ANY],
        scratch_shapes=[pltpu.SemaphoreType.DMA((2,))],
        compiler_params=PARAMS,
    )(place, integrals, far)
    from_below = shift(up, "y", "y", 1)
    from_above = shift(down, "y", "y", -1)

    near = join_call(quad, *[shift(quad, "x", "z", step) for step in SHIFTS])
    blocks = [near] + [shift(near, "z", "x", step) for step in SHIFTS]

    other = swap_core(integrals).reshape(81, 10368)
    below_other = swap_core(from_below)
    above_other = swap_core(from_above)
    local_high, local_low = turn_call(turn_local, place, flat, other, 4 * WINDOW)
    moved = lambda a, b: turn_call(
        turn_moved, place, a.reshape(81, PAIR_WINDOW), b.reshape(81, PAIR_WINDOW), 2 * WINDOW
    )
    below_high, below_low = moved(from_below, below_other)
    above_high, above_low = moved(from_above, above_other)

    local_sum, below_sum, above_sum = pl.pallas_call(
        multiply,
        out_shape=[jax.ShapeDtypeStruct((144, 2 * LANES), F32)] * 3,
        in_specs=[VMEM] * 10,
        out_specs=[VMEM] * 3,
        scratch_shapes=[pltpu.VMEM((16, 4 * WINDOW), F32)],
        compiler_params=PARAMS,
    )(*blocks, local_high, local_low, below_high, below_low, above_high, above_low)
    up_back = shift(below_sum, "y", "y", -1)
    down_back = shift(above_sum, "y", "y", 1)
    packed = pl.pallas_call(
        address,
        out_shape=jax.ShapeDtypeStruct((32, 8, LANES), F32),
        in_specs=[SMEM, VMEM, VMEM, VMEM],
        out_specs=VMEM,
        compiler_params=PARAMS,
    )(place, local_sum, up_back, down_back)
    ladder = lax.all_to_all(packed, ("x", "z", "core"), 0, 0, tiled=True)

    scale, offset = local_terms(
        amplitudes, ovov, eps_occ, eps_vir, occ_count, vir_count, x, z, y, core
    )
    result = pl.pallas_call(
        finish,
        out_shape=jax.ShapeDtypeStruct((18, 1296), F32),
        in_specs=[VMEM, VMEM, VMEM],
        out_specs=VMEM,
        scratch_shapes=[pltpu.VMEM((24, WINDOW), F32)],
        compiler_params=PARAMS,
    )(ladder, scale, offset)
    return result.reshape(3, 6, 1, 1296)


def solution(mesh):
    fine = Mesh(mesh.devices.reshape(4, 4, 4, 2), AXES)
    rows, cols = ("x", "z"), ("y", "core")
    return jax.shard_map(
        on_device,
        mesh=fine,
        in_specs=(P(rows, None, cols, None), P(cols, rows, None), P(rows, cols, None), P(), P(), P(), P()),
        out_specs=P(rows, None, cols, None),
        check_vma=False,
    )
```

```python
import jax
import jax.numpy as jnp
from jax import lax
from jax.experimental import pallas as pl
from jax.experimental.pallas import tpu as pltpu
from jax.sharding import Mesh, PartitionSpec as P

AXES = ("x", "z", "y", "core")
SHIFTS = (1, -1, 2)
STEPS = (0, 1, -1, 2)
LANES = 128
TILES = 11
WINDOW = TILES * LANES
SPAN = 21
DEPTH = SPAN * LANES
MAIN = 8 * TILES
SHARD = 104
PMAIN = 8 * SPAN
PAIR = 192
QUAD = 2 * PAIR
PSLOT = 88
PROWS = SPAN * PSLOT
F32 = jnp.float32
BF16 = jnp.bfloat16
ANY = pl.BlockSpec(memory_space=pl.ANY)
HBM = pl.BlockSpec(memory_space=pltpu.HBM)
VMEM = pl.BlockSpec(memory_space=pltpu.VMEM)
SMALL = pltpu.CompilerParams(vmem_limit_bytes=8 * 1024 * 1024)
LARGE = pltpu.CompilerParams(vmem_limit_bytes=28 * 1024 * 1024)


def ring(value, axes, step, cross=False):
    pairs = []
    for x in range(4):
        for z in range(4):
            for y in range(4):
                for core in range(2):
                    here = {"x": x, "z": z, "y": y, "core": core}
                    there = dict(here)
                    there[axes[core]] = (there[axes[core]] + step) % 4
                    if cross:
                        there["core"] = 1 - core
                    pairs.append(
                        tuple(((p["x"] * 4 + p["z"]) * 4 + p["y"]) * 2 + p["core"] for p in (here, there))
                    )
    return lax.ppermute(value, AXES, pairs)


def swap_core(value):
    return lax.ppermute(value, "core", [(0, 1), (1, 0)])


def places():
    return tuple(lax.axis_index(name) for name in AXES)


def lane_orbitals(shape):
    lane = lax.broadcasted_iota(jnp.int32, shape, 1)
    a = jnp.floor((lane.astype(F32) + 0.5) * (1.0 / 36.0)).astype(jnp.int32)
    return a, lane - 36 * a


def cut_step(integrals, witness, up, down, home, sems):
    y = lax.axis_index("y")
    cuts = []
    for at, (ref, first, step) in enumerate(((up, 0, 1), (down, 0, 3), (home, 0, 0), (home, SPAN, 2))):
        base = ((y + step) & 3) * 20
        for t in range(SPAN):
            start = pl.multiple_of((base + t) * LANES, LANES)
            cuts.append(
                pltpu.make_async_copy(
                    integrals.at[:, :, pl.ds(start, LANES)], ref.at[first + t, 0:81], sems.at[at, t]
                )
            )
    for copy in cuts:
        copy.start()
    for ref, tiles in ((up, SPAN), (down, SPAN), (home, 2 * SPAN)):
        ref[:, 81:PSLOT] = jnp.zeros((tiles, PSLOT - 81, 1, LANES), F32)
    for copy in cuts:
        copy.wait()


def open_step(occ_ref, vir_ref, amp_ref, keep, send, wide, amp, occ, vir, sems):
    x, z, y, core = places()
    copies = [
        pltpu.make_async_copy(source, target, sems.at[at])
        for at, (source, target) in enumerate(((occ_ref, occ), (vir_ref, vir), (amp_ref, amp)))
    ]
    for copy in copies:
        copy.start()
    wide[...] = jnp.zeros_like(wide)
    for copy in copies:
        copy.wait()
    for row in range(18):
        wide[row : row + 1, 0:1296] = amp[row // 6, row % 6]
    row_place = x * 4 + z
    occ_here = occ[row_place >> 1]
    first = 3 * (row_place & 1)
    irrep = 2 * y + core
    vir_here = vir[irrep]
    a, b = lane_orbitals(wide.shape)
    row = lax.broadcasted_iota(jnp.int32, wide.shape, 0)
    i_low = (row * 43) >> 8
    j = row - 6 * i_low
    live = (a < vir_here) & (b < vir_here) & (i_low + first < occ_here) & (j < occ_here)
    moved = pltpu.roll(jnp.where(live, wide[...], 0.0), 16 * irrep, 1)

    def write(ref, half):
        for t in range(TILES):
            columns = slice(t * LANES, (t + 1) * LANES)
            ref[8 * t : 8 * t + 8, :] = moved[8 * half : 8 * half + 8, columns]
            ref[MAIN + t : MAIN + t + 1, :] = moved[16 + half : 17 + half, columns]
        ref[MAIN + TILES : SHARD, :] = jnp.zeros((SHARD - MAIN - TILES, LANES), F32)

    @pl.when(core == 0)
    def _():
        write(keep, 0)
        write(send, 1)

    @pl.when(core == 1)
    def _():
        write(keep, 1)
        write(send, 0)


def merge_irreps(even, odd, out, at):
    gap = SPAN - TILES
    out[at : at + 8 * gap, :] = even[0 : 8 * gap, :]
    out[at + 8 * gap : at + MAIN, :] = even[8 * gap : MAIN, :] + odd[0:8, :]
    out[at + MAIN : at + PMAIN, :] = odd[8:MAIN, :]
    extra = at + PMAIN
    out[extra : extra + gap, :] = even[MAIN : MAIN + gap, :]
    out[extra + gap : extra + TILES, :] = even[MAIN + gap : MAIN + TILES, :] + odd[MAIN : MAIN + 1, :]
    out[extra + TILES : extra + SPAN, :] = odd[MAIN + 1 : MAIN + TILES, :]
    out[extra + SPAN : at + PAIR, :] = jnp.zeros((PAIR - PMAIN - SPAN, LANES), F32)


def merge_quad(keep, got, far_keep, far_got, out):
    core = lax.axis_index("core")

    @pl.when(core == 0)
    def _():
        merge_irreps(keep, got, out, 0)
        merge_irreps(far_keep, far_got, out, PAIR)

    @pl.when(core == 1)
    def _():
        merge_irreps(got, keep, out, 0)
        merge_irreps(far_got, far_keep, out, PAIR)


def gather_four(b0, b1, b2, b3, near, far):
    for at, block in enumerate((b0, b1, b2, b3)):
        near[at * PAIR : (at + 1) * PAIR, :] = block[0:PAIR, :]
        far[at * PAIR : (at + 1) * PAIR, :] = block[PAIR:QUAD, :]


def nothing(*refs):
    pass


def hold(a, b, *witnesses):
    return pl.pallas_call(
        nothing,
        out_shape=[jax.ShapeDtypeStruct(v.shape, v.dtype) for v in (a, b)],
        in_specs=[ANY] * (2 + len(witnesses)),
        out_specs=[ANY] * 2,
        input_output_aliases={0: 0, 1: 1},
        compiler_params=SMALL,
    )(a, b, *witnesses)


def left_side(blocks, extra):
    for t in range(SPAN):
        for d, block in enumerate(blocks):
            extra[4 * d : 4 * d + 4, t * LANES : (t + 1) * LANES] = block[pl.ds(PMAIN + t, 4, stride=PAIR), :]
    rows = []
    for block in blocks:
        for e in range(4):
            rows.append(
                jnp.concatenate(
                    [block[e * PAIR + 8 * t : e * PAIR + 8 * t + 8, :] for t in range(SPAN)], axis=1
                )
            )
    return split(jnp.concatenate(rows + [extra[...]], axis=0))


def split(value):
    high = value.astype(BF16)
    return high, (value - high.astype(F32)).astype(BF16)


def tiles_side(ref, first):
    return jnp.concatenate(
        [ref[(first + t) * PSLOT : (first + t + 1) * PSLOT, :] for t in range(SPAN)], axis=1
    )


def last_by_last(p, q):
    return lax.dot_general(p, q, (((1,), (1,)), ((), ())), preferred_element_type=F32)


def multiply_near(b0, b1, b2, b3, home, home_other, below, below_other, above, above_other,
                  here_sum, below_sum, above_sum, extra, turned):
    high, low = left_side((b0, b1, b2, b3), extra)
    sides = [tiles_side(ref, 0) for ref in (home, home_other, below, below_other, above, above_other)]
    v_high, v_low = split(jnp.concatenate(sides, axis=0))
    total = last_by_last(v_high, high) + (last_by_last(v_low, high) + last_by_last(v_high, low))
    turned[...] = jnp.zeros_like(turned)
    for at, ref in enumerate((here_sum, below_sum, above_sum)):
        for side in range(2):
            rows = slice((2 * at + side) * PSLOT, (2 * at + side + 1) * PSLOT)
            turned[0:PSLOT, 0:144] = total[rows, :]
            ref[:, side * LANES : (side + 1) * LANES] = turned[...].T[0:144, :]


def multiply_far(b0, b1, b2, b3, home, home_other, here_sum, back_a, back_b, out, extra):
    x, z, y, core = places()
    high, low = left_side((b0, b1, b2, b3), extra)
    partial = here_sum[...] + back_a[...] + back_b[...]
    row = lax.broadcasted_iota(jnp.int32, (8, LANES), 0)
    lane = lax.broadcasted_iota(jnp.int32, (8, LANES), 1)
    pad = jnp.zeros((LANES - PSLOT, DEPTH), BF16)
    sides = [split(tiles_side(ref, SPAN)) for ref in (home, home_other)]
    v_high = jnp.concatenate([sides[0][0], pad, sides[1][0], pad], axis=0)
    v_low = jnp.concatenate([sides[0][1], pad, sides[1][1], pad], axis=0)
    total = partial + (
        last_by_last(high, v_high) + (last_by_last(low, v_high) + last_by_last(high, v_low))
    )
    for side in range(2):
        columns = slice(side * LANES, (side + 1) * LANES)
        last = total[128:144, columns]
        last_a = pltpu.roll(last, 81, 1)
        last_b = pltpu.roll(last, 34, 1)
        core_there = core if side == 0 else 1 - core
        for d in range(4):
            for e in range(4):
                s = 4 * d + e
                x_step = jnp.where(core == 0, STEPS[e], STEPS[d])
                z_step = jnp.where(core == 0, STEPS[d], STEPS[e])
                there = ((x - x_step) & 3) * 4 + ((z - z_step) & 3)
                main = total[8 * s : 8 * s + 8, columns]
                tail = jnp.where(row == 0, last_a[s : s + 1, :], last_b[s : s + 1, :])
                out[there * 2 + core_there] = jnp.where(lane < 81, main, tail)


def local_step(occ_ref, vir_ref, eps_occ_ref, eps_vir_ref, amp_ref, witness,
               scale, live, amp, occ, vir, eps_occ, eps_vir, sems):
    x, z, y, core = places()
    copies = [
        pltpu.make_async_copy(source, target, sems.at[at])
        for at, (source, target) in enumerate(
            ((occ_ref, occ), (vir_ref, vir), (eps_occ_ref, eps_occ), (eps_vir_ref, eps_vir), (amp_ref, amp))
        )
    ]
    for copy in copies:
        copy.start()
    for copy in copies:
        copy.wait()
    row_place = x * 4 + z
    shell = row_place >> 1
    first = 3 * (row_place & 1)
    irrep = 2 * y + core
    a, b = lane_orbitals((1, 1296))
    energy_a = jnp.zeros((1, 1296), F32)
    energy_b = jnp.zeros((1, 1296), F32)
    for slot in range(36):
        value = eps_vir[irrep, slot]
        energy_a = jnp.where(a == slot, value, energy_a)
        energy_b = jnp.where(b == slot, value, energy_b)
    lane_live = (a < vir[irrep]) & (b < vir[irrep])
    occ_here = occ[shell]
    for r in range(18):
        i, j = first + r // 6, r % 6
        here = lane_live & (i < occ_here) & (j < occ_here)
        gap = eps_occ[shell, i] + eps_occ[shell, j] - energy_a - energy_b
        scale[r : r + 1, :] = jnp.where(here, 1.0, 0.0) / gap
        live[r : r + 1, :] = jnp.where(here, amp[r // 6, r % 6], 0.0)


def finish(sums, scale, cycle, out, wide):
    wide[...] = jnp.zeros_like(wide)
    lane8 = lax.broadcasted_iota(jnp.int32, (1, LANES), 1)
    lane = lax.broadcasted_iota(jnp.int32, (24, LANES), 1)
    for r in range(16):
        mains, lasts = [], []
        for core in range(2):
            block = sums[2 * r + core]
            mains.append(block)
            lasts.append(
                jnp.where(lane8 < 47, pltpu.roll(block, 47, 1)[0:1, :], pltpu.roll(block, 94, 1)[1:2, :])
            )
        stack = jnp.concatenate(mains + lasts + [jnp.zeros((6, LANES), F32)], axis=0)
        tile, start = divmod(81 * r, LANES)
        turned = pltpu.roll(stack, start, 1) if start else stack
        here = slice(tile * LANES, (tile + 1) * LANES)
        wide[:, here] = jnp.where((lane >= start) & (lane < start + 81), turned, wide[:, here])
        if start + 81 > LANES:
            after = slice((tile + 1) * LANES, (tile + 2) * LANES)
            wide[:, after] = jnp.where(lane < start + 81 - LANES, turned, wide[:, after])
    out[...] = (wide[0:18, 0:1296] + cycle[...]) * scale[...]


def cycle_term(live, ovov, row_place):
    partner = lax.ppermute(ovov, "z", [(0, 1), (1, 0), (2, 3), (3, 2)])
    panel = jnp.where(
        row_place % 2 == 0,
        jnp.concatenate([ovov, partner], 0),
        jnp.concatenate([partner, ovov], 0),
    )
    panel = panel.reshape(6, 36, 6, 36)
    cycle = jnp.einsum(
        "ikac,kcjb->ijab", live.reshape(3, 6, 36, 36), panel, precision=lax.Precision.HIGHEST
    )
    return cycle.reshape(18, 1296)


def on_device(amplitudes, vvvv, ovov, eps_occ, eps_vir, occ_count, vir_count):
    x, z, y, core = places()
    shape = jax.ShapeDtypeStruct
    keep, send = pl.pallas_call(
        open_step,
        out_shape=[shape((SHARD, LANES), F32)] * 2,
        in_specs=[HBM] * 3,
        out_specs=[VMEM] * 2,
        scratch_shapes=[
            pltpu.VMEM((24, WINDOW), F32),
            pltpu.VMEM((3, 6, 1, 1296), F32),
            pltpu.SMEM((8,), jnp.int32),
            pltpu.SMEM((8,), jnp.int32),
            pltpu.SemaphoreType.DMA((3,)),
        ],
        compiler_params=SMALL,
    )(occ_count, vir_count, amplitudes)
    got = swap_core(send)
    far_keep = ring(keep, "yy", 2)
    far_got = ring(send, "yy", 2, cross=True)
    up, down, home = pl.pallas_call(
        cut_step,
        out_shape=[shape((SPAN, PSLOT, 1, LANES), F32)] * 2 + [shape((2 * SPAN, PSLOT, 1, LANES), F32)],
        in_specs=[HBM, ANY],
        out_specs=[VMEM] * 3,
        scratch_shapes=[pltpu.SemaphoreType.DMA((4, SPAN))],
        compiler_params=SMALL,
        cost_estimate=pl.CostEstimate(flops=0, bytes_accessed=7000000, transcendentals=0),
    )(vvvv.reshape(81, 1, 10368), send)
    home = home.reshape(2 * PROWS, LANES)
    home_other = swap_core(home)
    up, down = hold(up.reshape(PROWS, LANES), down.reshape(PROWS, LANES), far_keep, far_got)
    quad = pl.pallas_call(
        merge_quad,
        out_shape=shape((QUAD, LANES), F32),
        in_specs=[VMEM] * 4,
        out_specs=VMEM,
        compiler_params=SMALL,
    )(keep, got, far_keep, far_got)
    below = ring(up, "yy", 1)
    above = ring(down, "yy", -1)

    near, far = pl.pallas_call(
        gather_four,
        out_shape=[shape((4 * PAIR, LANES), F32)] * 2,
        in_specs=[VMEM] * 4,
        out_specs=[VMEM] * 2,
        compiler_params=SMALL,
    )(quad, *[ring(quad, "xz", step) for step in SHIFTS])
    near_blocks = [near] + [ring(near, "zx", step) for step in SHIFTS]
    far_blocks = [far] + [ring(far, "zx", step) for step in SHIFTS]

    below, above = hold(below, above, *near_blocks[1:])
    below_other, above_other = swap_core(below), swap_core(above)

    scale, live = pl.pallas_call(
        local_step,
        out_shape=[shape((18, 1296), F32)] * 2,
        in_specs=[HBM] * 5 + [ANY],
        out_specs=[VMEM] * 2,
        scratch_shapes=[
            pltpu.VMEM((3, 6, 1, 1296), F32),
            pltpu.SMEM((8,), jnp.int32),
            pltpu.SMEM((8,), jnp.int32),
            pltpu.SMEM((8, 6), F32),
            pltpu.SMEM((8, 36), F32),
            pltpu.SemaphoreType.DMA((5,)),
        ],
        compiler_params=SMALL,
    )(occ_count, vir_count, eps_occ, eps_vir, amplitudes, near)
    cycle = cycle_term(live, ovov, x * 4 + z)

    sums = [shape((144, 2 * LANES), F32)] * 3
    here_sum, below_sum, above_sum = pl.pallas_call(
        multiply_near,
        out_shape=sums,
        in_specs=[VMEM] * 10,
        out_specs=[VMEM] * 3,
        scratch_shapes=[pltpu.VMEM((16, DEPTH), F32), pltpu.VMEM((LANES, 2 * LANES), F32)],
        compiler_params=LARGE,
    )(*near_blocks, home, home_other, below, below_other, above, above_other)
    back_a = ring(below_sum, "yy", -1)
    back_b = ring(above_sum, "yy", 1)
    packed = pl.pallas_call(
        multiply_far,
        out_shape=shape((32, 8, LANES), F32),
        in_specs=[VMEM] * 9,
        out_specs=VMEM,
        scratch_shapes=[pltpu.VMEM((16, DEPTH), F32)],
        compiler_params=LARGE,
    )(*far_blocks, home, home_other, here_sum, back_a, back_b)
    ladder = lax.all_to_all(packed, ("x", "z", "core"), 0, 0, tiled=True)
    result = pl.pallas_call(
        finish,
        out_shape=shape((18, 1296), F32),
        in_specs=[VMEM] * 3,
        out_specs=VMEM,
        scratch_shapes=[pltpu.VMEM((24, WINDOW), F32)],
        compiler_params=SMALL,
    )(ladder, scale, cycle)
    return result.reshape(3, 6, 1, 1296)


def solution(mesh):
    fine = Mesh(mesh.devices.reshape(4, 4, 4, 2), AXES)
    rows, cols = ("x", "z"), ("y", "core")
    return jax.shard_map(
        on_device,
        mesh=fine,
        in_specs=(P(rows, None, cols, None), P(cols, rows, None), P(rows, cols, None), P(), P(), P(), P()),
        out_specs=P(rows, None, cols, None),
        check_vma=False,
    )
```

```python
import jax
import jax.numpy as jnp
from jax import lax
from jax.experimental import pallas as pl
from jax.experimental.pallas import tpu as pltpu
from jax.sharding import Mesh, PartitionSpec as P

AXES = ("x", "z", "y", "core")
SHIFTS = ((1, 1), (-1, -1), (2, 2))
STEPS = (0, 1, -1, 2)
LANES = 128
TILES = 11
WINDOW = TILES * LANES
SPAN = 21
DEPTH = SPAN * LANES
MAIN = 8 * TILES
SHARD = 104
PMAIN = 8 * SPAN
PAIR = 192
QUAD = 2 * PAIR
PSLOT = 88
PROWS = SPAN * PSLOT
F32 = jnp.float32
BF16 = jnp.bfloat16
ANY = pl.BlockSpec(memory_space=pl.ANY)
HBM = pl.BlockSpec(memory_space=pltpu.HBM)
VMEM = pl.BlockSpec(memory_space=pltpu.VMEM)
HUGE = pltpu.CompilerParams(vmem_limit_bytes=56 * 1024 * 1024)
SMALL = pltpu.CompilerParams(vmem_limit_bytes=8 * 1024 * 1024)
LARGE = pltpu.CompilerParams(vmem_limit_bytes=28 * 1024 * 1024)


def ring(value, axes, steps):
    pairs = []
    for x in range(4):
        for z in range(4):
            for y in range(4):
                for core in range(2):
                    here = {"x": x, "z": z, "y": y, "core": core}
                    there = dict(here)
                    there[axes[core]] = (there[axes[core]] + steps[core]) % 4
                    pairs.append(
                        tuple(((p["x"] * 4 + p["z"]) * 4 + p["y"]) * 2 + p["core"] for p in (here, there))
                    )
    return lax.ppermute(value, AXES, pairs)


def swap_core(value):
    return lax.ppermute(value, "core", [(0, 1), (1, 0)])


def places():
    return tuple(lax.axis_index(name) for name in AXES)


def lane_orbitals(shape):
    lane = lax.broadcasted_iota(jnp.int32, shape, 1)
    a = jnp.floor((lane.astype(F32) + 0.5) * (1.0 / 36.0)).astype(jnp.int32)
    return a, lane - 36 * a


def window_copies(integrals, ref, sems, base):
    copies = []
    for t in range(SPAN):
        start = pl.multiple_of((base + t) * LANES, LANES)
        copies.append(
            pltpu.make_async_copy(integrals.at[:, :, pl.ds(start, LANES)], ref.at[t, 0:81], sems.at[t])
        )
    return copies


def cut_home(integrals, integrals_other, witness, near, near_other, far, far_other, sems):
    y = lax.axis_index("y")
    copies = []
    plan = ((integrals, near, 0), (integrals_other, near_other, 0), (integrals, far, 2), (integrals_other, far_other, 2))
    for at, (source, ref, step) in enumerate(plan):
        copies += window_copies(source, ref, sems.at[at], ((y + step) & 3) * 20)
    for copy in copies:
        copy.start()
    for copy in copies:
        copy.wait()


def open_step(occ_ref, vir_ref, amp_ref, integrals, keep, send, first_v, second_v,
              wide, amp, occ, vir, sems, cut_sems):
    x, z, y, core = places()
    copies = [
        pltpu.make_async_copy(source, target, sems.at[at])
        for at, (source, target) in enumerate(((occ_ref, occ), (vir_ref, vir), (amp_ref, amp)))
    ]
    cuts = window_copies(integrals, first_v, cut_sems.at[0], ((y + 1 + 2 * core) & 3) * 20)
    cuts += window_copies(integrals, second_v, cut_sems.at[1], ((y + 3 - 2 * core) & 3) * 20)
    for copy in copies + cuts:
        copy.start()
    wide[...] = jnp.zeros_like(wide)
    for copy in copies:
        copy.wait()
    for row in range(18):
        wide[row : row + 1, 0:1296] = amp[row // 6, row % 6]
    row_place = x * 4 + z
    occ_here = occ[row_place >> 1]
    first = 3 * (row_place & 1)
    irrep = 2 * y + core
    vir_here = vir[irrep]
    a, b = lane_orbitals(wide.shape)
    row = lax.broadcasted_iota(jnp.int32, wide.shape, 0)
    i_low = (row * 43) >> 8
    j = row - 6 * i_low
    live = (a < vir_here) & (b < vir_here) & (i_low + first < occ_here) & (j < occ_here)
    moved = pltpu.roll(jnp.where(live, wide[...], 0.0), 16 * irrep, 1)

    def write(ref, half):
        for t in range(TILES):
            columns = slice(t * LANES, (t + 1) * LANES)
            ref[8 * t : 8 * t + 8, :] = moved[8 * half : 8 * half + 8, columns]
            ref[MAIN + t : MAIN + t + 1, :] = moved[16 + half : 17 + half, columns]
        ref[MAIN + TILES : SHARD, :] = jnp.zeros((SHARD - MAIN - TILES, LANES), F32)

    @pl.when(core == 0)
    def _():
        write(keep, 0)
        write(send, 1)

    @pl.when(core == 1)
    def _():
        write(keep, 1)
        write(send, 0)

    for copy in cuts:
        copy.wait()


def merge_irreps(even, odd, out, at):
    gap = SPAN - TILES
    out[at : at + 8 * gap, :] = even[0 : 8 * gap, :]
    out[at + 8 * gap : at + MAIN, :] = even[8 * gap : MAIN, :] + odd[0:8, :]
    out[at + MAIN : at + PMAIN, :] = odd[8:MAIN, :]
    extra = at + PMAIN
    out[extra : extra + gap, :] = even[MAIN : MAIN + gap, :]
    out[extra + gap : extra + TILES, :] = even[MAIN + gap : MAIN + TILES, :] + odd[MAIN : MAIN + 1, :]
    out[extra + TILES : extra + SPAN, :] = odd[MAIN + 1 : MAIN + TILES, :]
    out[extra + SPAN : at + PAIR, :] = jnp.zeros((PAIR - PMAIN - SPAN, LANES), F32)


def merge_pair(keep, got, witness, out):
    core = lax.axis_index("core")

    @pl.when(core == 0)
    def _():
        merge_irreps(keep, got, out, 0)

    @pl.when(core == 1)
    def _():
        merge_irreps(got, keep, out, 0)


def join_pairs(near, far, out):
    out[0:PAIR, :] = near[...]
    out[PAIR:QUAD, :] = far[...]


def gather_four(b0, b1, b2, b3, witness, near, far):
    for at, block in enumerate((b0, b1, b2, b3)):
        near[at * PAIR : (at + 1) * PAIR, :] = block[0:PAIR, :]
        far[at * PAIR : (at + 1) * PAIR, :] = block[PAIR:QUAD, :]


def nothing(*refs):
    pass


def hold(a, b, *witnesses):
    return pl.pallas_call(
        nothing,
        out_shape=[jax.ShapeDtypeStruct(v.shape, v.dtype) for v in (a, b)],
        in_specs=[ANY] * (2 + len(witnesses)),
        out_specs=[ANY] * 2,
        input_output_aliases={0: 0, 1: 1},
        compiler_params=SMALL,
    )(a, b, *witnesses)


def left_side(blocks, extra):
    for t in range(SPAN):
        for d, block in enumerate(blocks):
            extra[4 * d : 4 * d + 4, t * LANES : (t + 1) * LANES] = block[pl.ds(PMAIN + t, 4, stride=PAIR), :]
    rows = []
    for block in blocks:
        for e in range(4):
            rows.append(
                jnp.concatenate(
                    [block[e * PAIR + 8 * t : e * PAIR + 8 * t + 8, :] for t in range(SPAN)], axis=1
                )
            )
    return split(jnp.concatenate(rows + [extra[...]], axis=0))


def split(value):
    high = value.astype(BF16)
    return high, (value - high.astype(F32)).astype(BF16)


def tiles_side(ref):
    return jnp.concatenate([ref[t * PSLOT : (t + 1) * PSLOT, :] for t in range(SPAN)], axis=1)


def last_by_last(p, q):
    return lax.dot_general(p, q, (((1,), (1,)), ((), ())), preferred_element_type=F32)


def multiply_near(b0, b1, b2, b3, home, home_other, below, below_other, above, above_other,
                  here_sum, below_sum, above_sum, extra, turned):
    high, low = left_side((b0, b1, b2, b3), extra)
    sides = [tiles_side(ref) for ref in (home, home_other, below, below_other, above, above_other)]
    v_high, v_low = split(jnp.concatenate(sides, axis=0))
    total = last_by_last(v_high, high) + (last_by_last(v_low, high) + last_by_last(v_high, low))
    turned[...] = jnp.zeros_like(turned)
    for at, ref in enumerate((here_sum, below_sum, above_sum)):
        for side in range(2):
            rows = slice((2 * at + side) * PSLOT, (2 * at + side + 1) * PSLOT)
            turned[0:PSLOT, 0:144] = total[rows, :]
            ref[:, side * LANES : (side + 1) * LANES] = turned[...].T[0:144, :]


def multiply_far(b0, b1, b2, b3, home, home_other, here_sum, back_a, back_b, out, extra):
    x, z, y, core = places()
    high, low = left_side((b0, b1, b2, b3), extra)
    partial = here_sum[...] + back_a[...] + back_b[...]
    row = lax.broadcasted_iota(jnp.int32, (8, LANES), 0)
    lane = lax.broadcasted_iota(jnp.int32, (8, LANES), 1)
    pad = jnp.zeros((LANES - PSLOT, DEPTH), BF16)
    sides = [split(tiles_side(ref)) for ref in (home, home_other)]
    v_high = jnp.concatenate([sides[0][0], pad, sides[1][0], pad], axis=0)
    v_low = jnp.concatenate([sides[0][1], pad, sides[1][1], pad], axis=0)
    total = partial + (
        last_by_last(high, v_high) + (last_by_last(low, v_high) + last_by_last(high, v_low))
    )
    for side in range(2):
        columns = slice(side * LANES, (side + 1) * LANES)
        last = total[128:144, columns]
        last_a = pltpu.roll(last, 81, 1)
        last_b = pltpu.roll(last, 34, 1)
        core_there = core if side == 0 else 1 - core
        for d in range(4):
            for e in range(4):
                s = 4 * d + e
                x_step = jnp.where(core == 0, STEPS[e], STEPS[d])
                z_step = jnp.where(core == 0, STEPS[d], STEPS[e])
                there = ((x - x_step) & 3) * 4 + ((z - z_step) & 3)
                main = total[8 * s : 8 * s + 8, columns]
                tail = jnp.where(row == 0, last_a[s : s + 1, :], last_b[s : s + 1, :])
                out[there * 2 + core_there] = jnp.where(lane < 81, main, tail)


def local_step(occ_ref, vir_ref, eps_occ_ref, eps_vir_ref, amp_ref, ovov, partner,
               scale, cycle, amp, occ, vir, eps_occ, eps_vir, left_a, left_b, panel_a, panel_b, sems):
    x, z, y, core = places()
    copies = [
        pltpu.make_async_copy(source, target, sems.at[at])
        for at, (source, target) in enumerate(
            ((occ_ref, occ), (vir_ref, vir), (eps_occ_ref, eps_occ), (eps_vir_ref, eps_vir), (amp_ref, amp))
        )
    ]
    for copy in copies:
        copy.start()
    panel_a[...] = jnp.zeros_like(panel_a)
    panel_b[...] = jnp.zeros_like(panel_b)
    left_a[...] = jnp.zeros_like(left_a)
    left_b[...] = jnp.zeros_like(left_b)
    lower = (z & 1) == 0
    for r in range(108):
        own, other = ovov[r], partner[r]
        panel_a[r : r + 1, 0:216] = jnp.where(lower, own, other)
        panel_b[r : r + 1, 0:216] = jnp.where(lower, other, own)
    for copy in copies:
        copy.wait()
    row_place = x * 4 + z
    shell = row_place >> 1
    first = 3 * (row_place & 1)
    irrep = 2 * y + core
    a, b = lane_orbitals((1, 1296))
    energy_a = jnp.zeros((1, 1296), F32)
    energy_b = jnp.zeros((1, 1296), F32)
    for slot in range(36):
        value = eps_vir[irrep, slot]
        energy_a = jnp.where(a == slot, value, energy_a)
        energy_b = jnp.where(b == slot, value, energy_b)
    lane_live = (a < vir[irrep]) & (b < vir[irrep])
    occ_here = occ[shell]
    for r in range(18):
        low, k = r // 6, r % 6
        i = first + low
        here = lane_live & (i < occ_here) & (k < occ_here)
        gap = eps_occ[shell, i] + eps_occ[shell, k] - energy_a - energy_b
        scale[r : r + 1, :] = jnp.where(here, 1.0, 0.0) / gap
        live = jnp.where(here, amp[low, k], 0.0)
        left, column = (left_a, 36 * k) if k < 3 else (left_b, 36 * (k - 3))
        for slot in range(36):
            left[36 * low + slot : 36 * low + slot + 1, column : column + 36] = live[
                :, 36 * slot : 36 * slot + 36
            ]
    dot = lambda p, q: jnp.dot(p, q, preferred_element_type=F32)
    total = None
    for left, panel in ((left_a, panel_a), (left_b, panel_b)):
        p_high, p_low = split(left[:, 0:112])
        q_high, q_low = split(panel[...])
        part = dot(p_high, q_high) + (dot(p_low, q_high) + dot(p_high, q_low))
        total = part if total is None else total + part
    for low in range(3):
        for j in range(6):
            r = 6 * low + j
            for slot in range(36):
                cycle[r : r + 1, 36 * slot : 36 * slot + 36] = total[
                    36 * low + slot : 36 * low + slot + 1, 36 * j : 36 * j + 36
                ]


def finish(sums, scale, cycle, out, wide):
    wide[...] = jnp.zeros_like(wide)
    lane8 = lax.broadcasted_iota(jnp.int32, (1, LANES), 1)
    lane = lax.broadcasted_iota(jnp.int32, (24, LANES), 1)
    for r in range(16):
        mains, lasts = [], []
        for core in range(2):
            block = sums[2 * r + core]
            mains.append(block)
            lasts.append(
                jnp.where(lane8 < 47, pltpu.roll(block, 47, 1)[0:1, :], pltpu.roll(block, 94, 1)[1:2, :])
            )
        stack = jnp.concatenate(mains + lasts + [jnp.zeros((6, LANES), F32)], axis=0)
        tile, start = divmod(81 * r, LANES)
        turned = pltpu.roll(stack, start, 1) if start else stack
        here = slice(tile * LANES, (tile + 1) * LANES)
        wide[:, here] = jnp.where((lane >= start) & (lane < start + 81), turned, wide[:, here])
        if start + 81 > LANES:
            after = slice((tile + 1) * LANES, (tile + 2) * LANES)
            wide[:, after] = jnp.where(lane < start + 81 - LANES, turned, wide[:, after])
    out[...] = (wide[0:18, 0:1296] + cycle[...]) * scale[...]


def on_device(amplitudes, vvvv, ovov, eps_occ, eps_vir, occ_count, vir_count):
    x, z, y, core = places()
    shape = jax.ShapeDtypeStruct
    integrals = vvvv.reshape(81, 1, 10368)
    window = shape((SPAN, PSLOT, 1, LANES), F32)
    flat = lambda value: value.reshape(PROWS, LANES)
    keep, send, first_v, second_v = pl.pallas_call(
        open_step,
        out_shape=[shape((SHARD, LANES), F32)] * 2 + [window] * 2,
        in_specs=[HBM] * 4,
        out_specs=[VMEM] * 2 + [ANY] * 2,
        scratch_shapes=[
            pltpu.VMEM((24, WINDOW), F32),
            pltpu.VMEM((3, 6, 1, 1296), F32),
            pltpu.SMEM((8,), jnp.int32),
            pltpu.SMEM((8,), jnp.int32),
            pltpu.SemaphoreType.DMA((3,)),
            pltpu.SemaphoreType.DMA((2, SPAN)),
        ],
        compiler_params=HUGE,
    )(occ_count, vir_count, amplitudes, integrals)
    got = swap_core(send)
    integrals_other = swap_core(integrals)
    partner = lax.ppermute(ovov, "z", [(0, 1), (1, 0), (2, 3), (3, 2)])
    pair = pl.pallas_call(
        merge_pair,
        out_shape=shape((PAIR, LANES), F32),
        in_specs=[VMEM] * 2 + [ANY],
        out_specs=VMEM,
        compiler_params=SMALL,
    )(keep, got, partner)
    far_pair = ring(pair, "yy", (2, 2))
    quad = pl.pallas_call(
        join_pairs,
        out_shape=shape((QUAD, LANES), F32),
        in_specs=[VMEM] * 2,
        out_specs=VMEM,
        compiler_params=SMALL,
    )(pair, far_pair)
    first_v, second_v = hold(
        flat(first_v), flat(second_v), far_pair
    )
    moved_a = ring(first_v, "yy", (1, -1))
    moved_b = ring(second_v, "yy", (-1, 1))

    near, far = pl.pallas_call(
        gather_four,
        out_shape=[shape((4 * PAIR, LANES), F32)] * 2,
        in_specs=[VMEM] * 4 + [ANY],
        out_specs=[VMEM] * 2,
        compiler_params=SMALL,
    )(quad, *[ring(quad, "xz", step) for step in SHIFTS], integrals_other)
    near_blocks = [near] + [ring(near, "zx", step) for step in SHIFTS]
    far_blocks = [far] + [ring(far, "zx", step) for step in SHIFTS]

    moved_a, moved_b = hold(moved_a, moved_b, *near_blocks[1:])
    swapped_a, swapped_b = swap_core(moved_a), swap_core(moved_b)
    homes = pl.pallas_call(
        cut_home,
        out_shape=[window] * 4,
        in_specs=[HBM, HBM, ANY],
        out_specs=[VMEM] * 4,
        scratch_shapes=[pltpu.SemaphoreType.DMA((4, SPAN))],
        compiler_params=SMALL,
        cost_estimate=pl.CostEstimate(flops=0, bytes_accessed=7000000, transcendentals=0),
    )(integrals, integrals_other, near_blocks[1])
    near_v, near_v_other, far_v, far_v_other = (flat(value) for value in homes)

    scale, cycle = pl.pallas_call(
        local_step,
        out_shape=[shape((18, 1296), F32)] * 2,
        in_specs=[HBM] * 5 + [VMEM] * 2,
        out_specs=[VMEM] * 2,
        scratch_shapes=[
            pltpu.VMEM((3, 6, 1, 1296), F32),
            pltpu.SMEM((8,), jnp.int32),
            pltpu.SMEM((8,), jnp.int32),
            pltpu.SMEM((8, 6), F32),
            pltpu.SMEM((8, 36), F32),
            pltpu.VMEM((112, 256), F32),
            pltpu.VMEM((112, 256), F32),
            pltpu.VMEM((112, 256), F32),
            pltpu.VMEM((112, 256), F32),
            pltpu.SemaphoreType.DMA((5,)),
        ],
        compiler_params=SMALL,
        cost_estimate=pl.CostEstimate(flops=100000000, bytes_accessed=1000000, transcendentals=0),
    )(occ_count, vir_count, eps_occ, eps_vir, amplitudes, ovov, partner)

    sums = [shape((144, 2 * LANES), F32)] * 3
    here_sum, below_sum, above_sum = pl.pallas_call(
        multiply_near,
        out_shape=sums,
        in_specs=[VMEM] * 10,
        out_specs=[VMEM] * 3,
        scratch_shapes=[pltpu.VMEM((16, DEPTH), F32), pltpu.VMEM((LANES, 2 * LANES), F32)],
        compiler_params=LARGE,
    )(*near_blocks, near_v, near_v_other, moved_a, swapped_b, moved_b, swapped_a)
    back_a = ring(below_sum, "yy", (-1, 1))
    back_b = ring(above_sum, "yy", (1, -1))
    packed = pl.pallas_call(
        multiply_far,
        out_shape=shape((32, 8, LANES), F32),
        in_specs=[VMEM] * 9,
        out_specs=VMEM,
        scratch_shapes=[pltpu.VMEM((16, DEPTH), F32)],
        compiler_params=LARGE,
    )(*far_blocks, far_v, far_v_other, here_sum, back_a, back_b)
    ladder = lax.all_to_all(packed, ("x", "z", "core"), 0, 0, tiled=True)
    result = pl.pallas_call(
        finish,
        out_shape=shape((18, 1296), F32),
        in_specs=[VMEM] * 3,
        out_specs=VMEM,
        scratch_shapes=[pltpu.VMEM((24, WINDOW), F32)],
        compiler_params=SMALL,
    )(ladder, scale, cycle)
    return result.reshape(3, 6, 1, 1296)


def solution(mesh):
    fine = Mesh(mesh.devices.reshape(4, 4, 4, 2), AXES)
    rows, cols = ("x", "z"), ("y", "core")
    return jax.shard_map(
        on_device,
        mesh=fine,
        in_specs=(P(rows, None, cols, None), P(cols, rows, None), P(rows, cols, None), P(), P(), P(), P()),
        out_specs=P(rows, None, cols, None),
        check_vma=False,
    )
```

```python
import jax
import jax.numpy as jnp
from jax import lax
from jax.experimental import pallas as pl
from jax.experimental.pallas import tpu as pltpu
from jax.sharding import Mesh, PartitionSpec as P

AXES = ("x", "z", "y", "core")
SHIFTS = ((1, 1), (-1, -1), (2, 2))
STEPS = (0, 1, -1, 2)
LANES = 128
TILES = 11
WINDOW = TILES * LANES
SPAN = 21
DEPTH = SPAN * LANES
MAIN = 8 * TILES
SHARD = 104
PMAIN = 8 * SPAN
PAIR = 192
QUAD = 2 * PAIR
PSLOT = 88
PROWS = SPAN * PSLOT
F32 = jnp.float32
BF16 = jnp.bfloat16
ANY = pl.BlockSpec(memory_space=pl.ANY)
HBM = pl.BlockSpec(memory_space=pltpu.HBM)
VMEM = pl.BlockSpec(memory_space=pltpu.VMEM)
HUGE = pltpu.CompilerParams(vmem_limit_bytes=56 * 1024 * 1024)
SMALL = pltpu.CompilerParams(vmem_limit_bytes=8 * 1024 * 1024)
LARGE = pltpu.CompilerParams(vmem_limit_bytes=28 * 1024 * 1024)


def ring(value, axes, steps):
    pairs = []
    for x in range(4):
        for z in range(4):
            for y in range(4):
                for core in range(2):
                    here = {"x": x, "z": z, "y": y, "core": core}
                    there = dict(here)
                    there[axes[core]] = (there[axes[core]] + steps[core]) % 4
                    pairs.append(
                        tuple(((p["x"] * 4 + p["z"]) * 4 + p["y"]) * 2 + p["core"] for p in (here, there))
                    )
    return lax.ppermute(value, AXES, pairs)


def swap_core(value):
    return lax.ppermute(value, "core", [(0, 1), (1, 0)])


def places():
    return tuple(lax.axis_index(name) for name in AXES)


def lane_orbitals(shape):
    lane = lax.broadcasted_iota(jnp.int32, shape, 1)
    a = jnp.floor((lane.astype(F32) + 0.5) * (1.0 / 36.0)).astype(jnp.int32)
    return a, lane - 36 * a


def window_copies(integrals, ref, first, sems, base):
    copies = []
    for t in range(SPAN):
        start = pl.multiple_of((base + t) * LANES, LANES)
        copies.append(
            pltpu.make_async_copy(integrals.at[:, :, pl.ds(start, LANES)], ref.at[first + t, 0:81], sems.at[t])
        )
    return copies


def open_step(occ_ref, vir_ref, amp_ref, integrals, keep, send, first_v, second_v, home,
              wide, amp, occ, vir, sems, cut_sems):
    x, z, y, core = places()
    copies = [
        pltpu.make_async_copy(source, target, sems.at[at])
        for at, (source, target) in enumerate(((occ_ref, occ), (vir_ref, vir), (amp_ref, amp)))
    ]
    cuts = window_copies(integrals, first_v, 0, cut_sems.at[0], ((y + 1 + 2 * core) & 3) * 20)
    cuts += window_copies(integrals, second_v, 0, cut_sems.at[1], ((y + 3 - 2 * core) & 3) * 20)
    cuts += window_copies(integrals, home, 0, cut_sems.at[2], y * 20)
    cuts += window_copies(integrals, home, SPAN, cut_sems.at[3], ((y + 2) & 3) * 20)
    for copy in copies + cuts:
        copy.start()
    wide[...] = jnp.zeros_like(wide)
    for copy in copies:
        copy.wait()
    for row in range(18):
        wide[row : row + 1, 0:1296] = amp[row // 6, row % 6]
    row_place = x * 4 + z
    occ_here = occ[row_place >> 1]
    first = 3 * (row_place & 1)
    irrep = 2 * y + core
    vir_here = vir[irrep]
    a, b = lane_orbitals(wide.shape)
    row = lax.broadcasted_iota(jnp.int32, wide.shape, 0)
    i_low = (row * 43) >> 8
    j = row - 6 * i_low
    live = (a < vir_here) & (b < vir_here) & (i_low + first < occ_here) & (j < occ_here)
    moved = pltpu.roll(jnp.where(live, wide[...], 0.0), 16 * irrep, 1)

    def write(ref, half):
        for t in range(TILES):
            columns = slice(t * LANES, (t + 1) * LANES)
            ref[8 * t : 8 * t + 8, :] = moved[8 * half : 8 * half + 8, columns]
            ref[MAIN + t : MAIN + t + 1, :] = moved[16 + half : 17 + half, columns]
        ref[MAIN + TILES : SHARD, :] = jnp.zeros((SHARD - MAIN - TILES, LANES), F32)

    @pl.when(core == 0)
    def _():
        write(keep, 0)
        write(send, 1)

    @pl.when(core == 1)
    def _():
        write(keep, 1)
        write(send, 0)

    for copy in cuts:
        copy.wait()


def merge_irreps(even, odd, out, at):
    gap = SPAN - TILES
    out[at : at + 8 * gap, :] = even[0 : 8 * gap, :]
    out[at + 8 * gap : at + MAIN, :] = even[8 * gap : MAIN, :] + odd[0:8, :]
    out[at + MAIN : at + PMAIN, :] = odd[8:MAIN, :]
    extra = at + PMAIN
    out[extra : extra + gap, :] = even[MAIN : MAIN + gap, :]
    out[extra + gap : extra + TILES, :] = even[MAIN + gap : MAIN + TILES, :] + odd[MAIN : MAIN + 1, :]
    out[extra + TILES : extra + SPAN, :] = odd[MAIN + 1 : MAIN + TILES, :]
    out[extra + SPAN : at + PAIR, :] = jnp.zeros((PAIR - PMAIN - SPAN, LANES), F32)


def merge_pair(keep, got, witness, out):
    core = lax.axis_index("core")

    @pl.when(core == 0)
    def _():
        merge_irreps(keep, got, out, 0)

    @pl.when(core == 1)
    def _():
        merge_irreps(got, keep, out, 0)


def join_pairs(near, far, witness, out):
    out[0:PAIR, :] = near[...]
    out[PAIR:QUAD, :] = far[...]


def gather_four(b0, b1, b2, b3, near, far):
    for at, block in enumerate((b0, b1, b2, b3)):
        near[at * PAIR : (at + 1) * PAIR, :] = block[0:PAIR, :]
        far[at * PAIR : (at + 1) * PAIR, :] = block[PAIR:QUAD, :]


def nothing(*refs):
    pass


def hold(a, b, *witnesses):
    return pl.pallas_call(
        nothing,
        out_shape=[jax.ShapeDtypeStruct(v.shape, v.dtype) for v in (a, b)],
        in_specs=[ANY] * (2 + len(witnesses)),
        out_specs=[ANY] * 2,
        input_output_aliases={0: 0, 1: 1},
        compiler_params=SMALL,
    )(a, b, *witnesses)


def left_side(blocks, extra):
    for t in range(SPAN):
        for d, block in enumerate(blocks):
            extra[4 * d : 4 * d + 4, t * LANES : (t + 1) * LANES] = block[pl.ds(PMAIN + t, 4, stride=PAIR), :]
    rows = []
    for block in blocks:
        for e in range(4):
            rows.append(
                jnp.concatenate(
                    [block[e * PAIR + 8 * t : e * PAIR + 8 * t + 8, :] for t in range(SPAN)], axis=1
                )
            )
    return split(jnp.concatenate(rows + [extra[...]], axis=0))


def split(value):
    high = value.astype(BF16)
    return high, (value - high.astype(F32)).astype(BF16)


def tiles_side(ref, first):
    return jnp.concatenate(
        [ref[(first + t) * PSLOT : (first + t + 1) * PSLOT, :] for t in range(SPAN)], axis=1
    )


def last_by_last(p, q):
    return lax.dot_general(p, q, (((1,), (1,)), ((), ())), preferred_element_type=F32)


def multiply_near(b0, b1, b2, b3, home, home_other, below, below_other, above, above_other,
                  here_sum, below_sum, above_sum, extra, turned):
    high, low = left_side((b0, b1, b2, b3), extra)
    sides = [tiles_side(ref, 0) for ref in (home, home_other, below, below_other, above, above_other)]
    v_high, v_low = split(jnp.concatenate(sides, axis=0))
    total = last_by_last(v_high, high) + (last_by_last(v_low, high) + last_by_last(v_high, low))
    turned[...] = jnp.zeros_like(turned)
    for at, ref in enumerate((here_sum, below_sum, above_sum)):
        for side in range(2):
            rows = slice((2 * at + side) * PSLOT, (2 * at + side + 1) * PSLOT)
            turned[0:PSLOT, 0:144] = total[rows, :]
            ref[:, side * LANES : (side + 1) * LANES] = turned[...].T[0:144, :]


def multiply_far(b0, b1, b2, b3, home, home_other, here_sum, back_a, back_b, out, extra):
    x, z, y, core = places()
    high, low = left_side((b0, b1, b2, b3), extra)
    partial = here_sum[...] + back_a[...] + back_b[...]
    row = lax.broadcasted_iota(jnp.int32, (8, LANES), 0)
    lane = lax.broadcasted_iota(jnp.int32, (8, LANES), 1)
    pad = jnp.zeros((LANES - PSLOT, DEPTH), BF16)
    sides = [split(tiles_side(ref, SPAN)) for ref in (home, home_other)]
    v_high = jnp.concatenate([sides[0][0], pad, sides[1][0], pad], axis=0)
    v_low = jnp.concatenate([sides[0][1], pad, sides[1][1], pad], axis=0)
    total = partial + (
        last_by_last(high, v_high) + (last_by_last(low, v_high) + last_by_last(high, v_low))
    )
    for side in range(2):
        columns = slice(side * LANES, (side + 1) * LANES)
        last = total[128:144, columns]
        last_a = pltpu.roll(last, 81, 1)
        last_b = pltpu.roll(last, 34, 1)
        core_there = core if side == 0 else 1 - core
        for d in range(4):
            for e in range(4):
                s = 4 * d + e
                x_step = jnp.where(core == 0, STEPS[e], STEPS[d])
                z_step = jnp.where(core == 0, STEPS[d], STEPS[e])
                there = ((x - x_step) & 3) * 4 + ((z - z_step) & 3)
                main = total[8 * s : 8 * s + 8, columns]
                tail = jnp.where(row == 0, last_a[s : s + 1, :], last_b[s : s + 1, :])
                out[there * 2 + core_there] = jnp.where(lane < 81, main, tail)


def local_step(occ_ref, vir_ref, eps_occ_ref, eps_vir_ref, amp_ref, ovov, partner,
               scale, cycle, amp, occ, vir, eps_occ, eps_vir, left_a, left_b, panel_a, panel_b, sems):
    x, z, y, core = places()
    copies = [
        pltpu.make_async_copy(source, target, sems.at[at])
        for at, (source, target) in enumerate(
            ((occ_ref, occ), (vir_ref, vir), (eps_occ_ref, eps_occ), (eps_vir_ref, eps_vir), (amp_ref, amp))
        )
    ]
    for copy in copies:
        copy.start()
    panel_a[...] = jnp.zeros_like(panel_a)
    panel_b[...] = jnp.zeros_like(panel_b)
    left_a[...] = jnp.zeros_like(left_a)
    left_b[...] = jnp.zeros_like(left_b)
    lower = (z & 1) == 0
    for r in range(108):
        own, other = ovov[r], partner[r]
        panel_a[r : r + 1, 0:216] = jnp.where(lower, own, other)
        panel_b[r : r + 1, 0:216] = jnp.where(lower, other, own)
    for copy in copies:
        copy.wait()
    row_place = x * 4 + z
    shell = row_place >> 1
    first = 3 * (row_place & 1)
    irrep = 2 * y + core
    a, b = lane_orbitals((1, 1296))
    energy_a = jnp.zeros((1, 1296), F32)
    energy_b = jnp.zeros((1, 1296), F32)
    for slot in range(36):
        value = eps_vir[irrep, slot]
        energy_a = jnp.where(a == slot, value, energy_a)
        energy_b = jnp.where(b == slot, value, energy_b)
    lane_live = (a < vir[irrep]) & (b < vir[irrep])
    occ_here = occ[shell]
    for r in range(18):
        low, k = r // 6, r % 6
        i = first + low
        here = lane_live & (i < occ_here) & (k < occ_here)
        gap = eps_occ[shell, i] + eps_occ[shell, k] - energy_a - energy_b
        scale[r : r + 1, :] = jnp.where(here, 1.0, 0.0) / gap
        live = jnp.where(here, amp[low, k], 0.0)
        left, column = (left_a, 36 * k) if k < 3 else (left_b, 36 * (k - 3))
        for slot in range(36):
            left[36 * low + slot : 36 * low + slot + 1, column : column + 36] = live[
                :, 36 * slot : 36 * slot + 36
            ]
    dot = lambda p, q: jnp.dot(p, q, preferred_element_type=F32)
    total = None
    for left, panel in ((left_a, panel_a), (left_b, panel_b)):
        p_high, p_low = split(left[:, 0:112])
        q_high, q_low = split(panel[...])
        part = dot(p_high, q_high) + (dot(p_low, q_high) + dot(p_high, q_low))
        total = part if total is None else total + part
    for low in range(3):
        for j in range(6):
            r = 6 * low + j
            for slot in range(36):
                cycle[r : r + 1, 36 * slot : 36 * slot + 36] = total[
                    36 * low + slot : 36 * low + slot + 1, 36 * j : 36 * j + 36
                ]


def finish(sums, scale, cycle, out, wide):
    wide[...] = jnp.zeros_like(wide)
    lane8 = lax.broadcasted_iota(jnp.int32, (1, LANES), 1)
    lane = lax.broadcasted_iota(jnp.int32, (24, LANES), 1)
    for r in range(16):
        mains, lasts = [], []
        for core in range(2):
            block = sums[2 * r + core]
            mains.append(block)
            lasts.append(
                jnp.where(lane8 < 47, pltpu.roll(block, 47, 1)[0:1, :], pltpu.roll(block, 94, 1)[1:2, :])
            )
        stack = jnp.concatenate(mains + lasts + [jnp.zeros((6, LANES), F32)], axis=0)
        tile, start = divmod(81 * r, LANES)
        turned = pltpu.roll(stack, start, 1) if start else stack
        here = slice(tile * LANES, (tile + 1) * LANES)
        wide[:, here] = jnp.where((lane >= start) & (lane < start + 81), turned, wide[:, here])
        if start + 81 > LANES:
            after = slice((tile + 1) * LANES, (tile + 2) * LANES)
            wide[:, after] = jnp.where(lane < start + 81 - LANES, turned, wide[:, after])
    total = (wide[0:18, 0:1296] + cycle[...]) * scale[...]
    for r in range(18):
        out[r // 6, r % 6] = total[r : r + 1, :]


def on_device(amplitudes, vvvv, ovov, eps_occ, eps_vir, occ_count, vir_count):
    x, z, y, core = places()
    shape = jax.ShapeDtypeStruct
    integrals = vvvv.reshape(81, 1, 10368)
    window = shape((SPAN, PSLOT, 1, LANES), F32)
    flat = lambda value: value.reshape(PROWS, LANES)
    keep, send, first_v, second_v, home = pl.pallas_call(
        open_step,
        out_shape=[shape((SHARD, LANES), F32)] * 2 + [window] * 2
        + [shape((2 * SPAN, PSLOT, 1, LANES), F32)],
        in_specs=[HBM] * 4,
        out_specs=[VMEM] * 2 + [ANY] * 3,
        scratch_shapes=[
            pltpu.VMEM((24, WINDOW), F32),
            pltpu.VMEM((3, 6, 1, 1296), F32),
            pltpu.SMEM((8,), jnp.int32),
            pltpu.SMEM((8,), jnp.int32),
            pltpu.SemaphoreType.DMA((3,)),
            pltpu.SemaphoreType.DMA((4, SPAN)),
        ],
        compiler_params=HUGE,
    )(occ_count, vir_count, amplitudes, integrals)
    got = swap_core(send)
    home = home.reshape(2 * PROWS, LANES)
    home_other = swap_core(home)
    partner = lax.ppermute(ovov, "z", [(0, 1), (1, 0), (2, 3), (3, 2)])
    pair = pl.pallas_call(
        merge_pair,
        out_shape=shape((PAIR, LANES), F32),
        in_specs=[VMEM] * 2 + [ANY],
        out_specs=VMEM,
        compiler_params=SMALL,
    )(keep, got, partner)
    far_pair = ring(pair, "yy", (2, 2))
    quad = pl.pallas_call(
        join_pairs,
        out_shape=shape((QUAD, LANES), F32),
        in_specs=[VMEM] * 2 + [ANY],
        out_specs=VMEM,
        compiler_params=SMALL,
    )(pair, far_pair, home_other)
    first_v, second_v = hold(
        flat(first_v), flat(second_v), far_pair
    )
    moved_a = ring(first_v, "yy", (1, -1))
    moved_b = ring(second_v, "yy", (-1, 1))

    near, far = pl.pallas_call(
        gather_four,
        out_shape=[shape((4 * PAIR, LANES), F32)] * 2,
        in_specs=[VMEM] * 4,
        out_specs=[VMEM] * 2,
        compiler_params=SMALL,
    )(quad, *[ring(quad, "xz", step) for step in SHIFTS])
    near_blocks = [near] + [ring(near, "zx", step) for step in SHIFTS]
    far_blocks = [far] + [ring(far, "zx", step) for step in SHIFTS]

    moved_a, moved_b = hold(moved_a, moved_b, *near_blocks[1:])
    swapped_a, swapped_b = swap_core(moved_a), swap_core(moved_b)

    scale, cycle = pl.pallas_call(
        local_step,
        out_shape=[shape((18, 1296), F32)] * 2,
        in_specs=[HBM] * 5 + [VMEM] * 2,
        out_specs=[VMEM] * 2,
        scratch_shapes=[
            pltpu.VMEM((3, 6, 1, 1296), F32),
            pltpu.SMEM((8,), jnp.int32),
            pltpu.SMEM((8,), jnp.int32),
            pltpu.SMEM((8, 6), F32),
            pltpu.SMEM((8, 36), F32),
            pltpu.VMEM((112, 256), F32),
            pltpu.VMEM((112, 256), F32),
            pltpu.VMEM((112, 256), F32),
            pltpu.VMEM((112, 256), F32),
            pltpu.SemaphoreType.DMA((5,)),
        ],
        compiler_params=SMALL,
        cost_estimate=pl.CostEstimate(flops=100000000, bytes_accessed=1000000, transcendentals=0),
    )(occ_count, vir_count, eps_occ, eps_vir, amplitudes, ovov, partner)

    sums = [shape((144, 2 * LANES), F32)] * 3
    here_sum, below_sum, above_sum = pl.pallas_call(
        multiply_near,
        out_shape=sums,
        in_specs=[VMEM] * 10,
        out_specs=[VMEM] * 3,
        scratch_shapes=[pltpu.VMEM((16, DEPTH), F32), pltpu.VMEM((LANES, 2 * LANES), F32)],
        compiler_params=LARGE,
    )(*near_blocks, home, home_other, moved_a, swapped_b, moved_b, swapped_a)
    back_a = ring(below_sum, "yy", (-1, 1))
    back_b = ring(above_sum, "yy", (1, -1))
    packed = pl.pallas_call(
        multiply_far,
        out_shape=shape((32, 8, LANES), F32),
        in_specs=[VMEM] * 9,
        out_specs=VMEM,
        scratch_shapes=[pltpu.VMEM((16, DEPTH), F32)],
        compiler_params=LARGE,
    )(*far_blocks, home, home_other, here_sum, back_a, back_b)
    ladder = lax.all_to_all(packed, ("x", "z", "core"), 0, 0, tiled=True)
    return pl.pallas_call(
        finish,
        out_shape=shape((3, 6, 1, 1296), F32),
        in_specs=[VMEM] * 3,
        out_specs=VMEM,
        scratch_shapes=[pltpu.VMEM((24, WINDOW), F32)],
        compiler_params=SMALL,
    )(ladder, scale, cycle)


def solution(mesh):
    fine = Mesh(mesh.devices.reshape(4, 4, 4, 2), AXES)
    rows, cols = ("x", "z"), ("y", "core")
    return jax.shard_map(
        on_device,
        mesh=fine,
        in_specs=(P(rows, None, cols, None), P(cols, rows, None), P(rows, cols, None), P(), P(), P(), P()),
        out_specs=P(rows, None, cols, None),
        check_vma=False,
    )
```

```python
import jax
import jax.numpy as jnp
from jax import lax
from jax.experimental import pallas as pl
from jax.experimental.pallas import tpu as pltpu
from jax.sharding import Mesh, PartitionSpec as P

AXES = ("x", "z", "y", "core")
SHIFTS = ((1, 1), (-1, -1), (2, 2))
STEPS = (0, 1, -1, 2)
LANES = 128
TILES = 11
WINDOW = TILES * LANES
SPAN = 21
DEPTH = SPAN * LANES
MAIN = 8 * TILES
SHARD = 104
PMAIN = 8 * SPAN
PAIR = 192
QUAD = 2 * PAIR
PSLOT = 88
PROWS = SPAN * PSLOT
F32 = jnp.float32
BF16 = jnp.bfloat16
ANY = pl.BlockSpec(memory_space=pl.ANY)
HBM = pl.BlockSpec(memory_space=pltpu.HBM)
VMEM = pl.BlockSpec(memory_space=pltpu.VMEM)
HUGE = pltpu.CompilerParams(vmem_limit_bytes=56 * 1024 * 1024)
SMALL = pltpu.CompilerParams(vmem_limit_bytes=8 * 1024 * 1024)
LARGE = pltpu.CompilerParams(vmem_limit_bytes=28 * 1024 * 1024)


def ring(value, axes, steps):
    pairs = []
    for x in range(4):
        for z in range(4):
            for y in range(4):
                for core in range(2):
                    here = {"x": x, "z": z, "y": y, "core": core}
                    there = dict(here)
                    there[axes[core]] = (there[axes[core]] + steps[core]) % 4
                    pairs.append(
                        tuple(((p["x"] * 4 + p["z"]) * 4 + p["y"]) * 2 + p["core"] for p in (here, there))
                    )
    return lax.ppermute(value, AXES, pairs)


def swap_core(value):
    return lax.ppermute(value, "core", [(0, 1), (1, 0)])


def places():
    return tuple(lax.axis_index(name) for name in AXES)


def lane_orbitals(shape):
    lane = lax.broadcasted_iota(jnp.int32, shape, 1)
    a = jnp.floor((lane.astype(F32) + 0.5) * (1.0 / 36.0)).astype(jnp.int32)
    return a, lane - 36 * a


def window_copies(integrals, ref, first, sems, base):
    copies = []
    for t in range(SPAN):
        start = pl.multiple_of((base + t) * LANES, LANES)
        copies.append(
            pltpu.make_async_copy(integrals.at[:, :, pl.ds(start, LANES)], ref.at[first + t, 0:81], sems.at[t])
        )
    return copies


def open_step(occ_ref, vir_ref, amp_ref, integrals, keep, send, first_v, second_v, home,
              wide, amp, occ, vir, sems, cut_sems):
    x, z, y, core = places()
    copies = [
        pltpu.make_async_copy(source, target, sems.at[at])
        for at, (source, target) in enumerate(((occ_ref, occ), (vir_ref, vir), (amp_ref, amp)))
    ]
    cuts = window_copies(integrals, first_v, 0, cut_sems.at[0], ((y + 1 + 2 * core) & 3) * 20)
    cuts += window_copies(integrals, second_v, 0, cut_sems.at[1], ((y + 3 - 2 * core) & 3) * 20)
    cuts += window_copies(integrals, home, 0, cut_sems.at[2], y * 20)
    cuts += window_copies(integrals, home, SPAN, cut_sems.at[3], ((y + 2) & 3) * 20)
    for copy in copies + cuts:
        copy.start()
    wide[...] = jnp.zeros_like(wide)
    for copy in copies:
        copy.wait()
    for row in range(18):
        wide[row : row + 1, 0:1296] = amp[row // 6, row % 6]
    row_place = x * 4 + z
    occ_here = occ[row_place >> 1]
    first = 3 * (row_place & 1)
    irrep = 2 * y + core
    vir_here = vir[irrep]
    a, b = lane_orbitals(wide.shape)
    row = lax.broadcasted_iota(jnp.int32, wide.shape, 0)
    i_low = (row * 43) >> 8
    j = row - 6 * i_low
    live = (a < vir_here) & (b < vir_here) & (i_low + first < occ_here) & (j < occ_here)
    moved = pltpu.roll(jnp.where(live, wide[...], 0.0), 16 * irrep, 1)

    def write(ref, half):
        for t in range(TILES):
            columns = slice(t * LANES, (t + 1) * LANES)
            ref[8 * t : 8 * t + 8, :] = moved[8 * half : 8 * half + 8, columns]
            ref[MAIN + t : MAIN + t + 1, :] = moved[16 + half : 17 + half, columns]
        ref[MAIN + TILES : SHARD, :] = jnp.zeros((SHARD - MAIN - TILES, LANES), F32)

    @pl.when(core == 0)
    def _():
        write(keep, 0)
        write(send, 1)

    @pl.when(core == 1)
    def _():
        write(keep, 1)
        write(send, 0)

    for copy in cuts:
        copy.wait()


def merge_irreps(even, odd, out, at):
    gap = SPAN - TILES
    out[at : at + 8 * gap, :] = even[0 : 8 * gap, :]
    out[at + 8 * gap : at + MAIN, :] = even[8 * gap : MAIN, :] + odd[0:8, :]
    out[at + MAIN : at + PMAIN, :] = odd[8:MAIN, :]
    extra = at + PMAIN
    out[extra : extra + gap, :] = even[MAIN : MAIN + gap, :]
    out[extra + gap : extra + TILES, :] = even[MAIN + gap : MAIN + TILES, :] + odd[MAIN : MAIN + 1, :]
    out[extra + TILES : extra + SPAN, :] = odd[MAIN + 1 : MAIN + TILES, :]
    out[extra + SPAN : at + PAIR, :] = jnp.zeros((PAIR - PMAIN - SPAN, LANES), F32)


def merge_pair(keep, got, witness, out):
    core = lax.axis_index("core")

    @pl.when(core == 0)
    def _():
        merge_irreps(keep, got, out, 0)

    @pl.when(core == 1)
    def _():
        merge_irreps(got, keep, out, 0)


def join_pairs(near, far, witness, out):
    out[0:PAIR, :] = near[...]
    out[PAIR:QUAD, :] = far[...]


def gather_four(b0, b1, b2, b3, near, far):
    for at, block in enumerate((b0, b1, b2, b3)):
        near[at * PAIR : (at + 1) * PAIR, :] = block[0:PAIR, :]
        far[at * PAIR : (at + 1) * PAIR, :] = block[PAIR:QUAD, :]


def nothing(*refs):
    pass


def hold(a, b, *witnesses):
    return pl.pallas_call(
        nothing,
        out_shape=[jax.ShapeDtypeStruct(v.shape, v.dtype) for v in (a, b)],
        in_specs=[ANY] * (2 + len(witnesses)),
        out_specs=[ANY] * 2,
        input_output_aliases={0: 0, 1: 1},
        compiler_params=SMALL,
    )(a, b, *witnesses)


def left_side(blocks, extra):
    for t in range(SPAN):
        for d, block in enumerate(blocks):
            extra[4 * d : 4 * d + 4, t * LANES : (t + 1) * LANES] = block[pl.ds(PMAIN + t, 4, stride=PAIR), :]
    rows = []
    for block in blocks:
        for e in range(4):
            rows.append(
                jnp.concatenate(
                    [block[e * PAIR + 8 * t : e * PAIR + 8 * t + 8, :] for t in range(SPAN)], axis=1
                )
            )
    return split(jnp.concatenate(rows + [extra[...]], axis=0))


def split(value):
    high = value.astype(BF16)
    return high, (value - high.astype(F32)).astype(BF16)


def tiles_side(ref, first):
    return jnp.concatenate(
        [ref[(first + t) * PSLOT : (first + t + 1) * PSLOT, :] for t in range(SPAN)], axis=1
    )


def last_by_last(p, q):
    return lax.dot_general(p, q, (((1,), (1,)), ((), ())), preferred_element_type=F32)


def multiply_near(b0, b1, b2, b3, home, home_other, below, below_other, above, above_other,
                  here_sum, below_sum, above_sum, extra, turned):
    high, low = left_side((b0, b1, b2, b3), extra)
    sides = [tiles_side(ref, 0) for ref in (home, home_other, below, below_other, above, above_other)]
    v_high, v_low = split(jnp.concatenate(sides, axis=0))
    total = last_by_last(v_high, high) + (last_by_last(v_low, high) + last_by_last(v_high, low))
    turned[...] = jnp.zeros_like(turned)
    for at, ref in enumerate((here_sum, below_sum, above_sum)):
        for side in range(2):
            rows = slice((2 * at + side) * PSLOT, (2 * at + side + 1) * PSLOT)
            turned[0:PSLOT, 0:144] = total[rows, :]
            ref[:, side * LANES : (side + 1) * LANES] = turned[...].T[0:144, :]


def multiply_far(b0, b1, b2, b3, home, home_other, here_sum, back_a, back_b, out, extra):
    x, z, y, core = places()
    high, low = left_side((b0, b1, b2, b3), extra)
    partial = here_sum[...] + back_a[...] + back_b[...]
    row = lax.broadcasted_iota(jnp.int32, (8, LANES), 0)
    lane = lax.broadcasted_iota(jnp.int32, (8, LANES), 1)
    pad = jnp.zeros((LANES - PSLOT, DEPTH), BF16)
    sides = [split(tiles_side(ref, SPAN)) for ref in (home, home_other)]
    v_high = jnp.concatenate([sides[0][0], pad, sides[1][0], pad], axis=0)
    v_low = jnp.concatenate([sides[0][1], pad, sides[1][1], pad], axis=0)
    total = partial + (
        last_by_last(high, v_high) + (last_by_last(low, v_high) + last_by_last(high, v_low))
    )
    for side in range(2):
        columns = slice(side * LANES, (side + 1) * LANES)
        last = total[128:144, columns]
        last_a = pltpu.roll(last, 81, 1)
        last_b = pltpu.roll(last, 34, 1)
        core_there = core if side == 0 else 1 - core
        for d in range(4):
            for e in range(4):
                s = 4 * d + e
                x_step = jnp.where(core == 0, STEPS[e], STEPS[d])
                z_step = jnp.where(core == 0, STEPS[d], STEPS[e])
                there = ((x - x_step) & 3) * 4 + ((z - z_step) & 3)
                main = total[8 * s : 8 * s + 8, columns]
                tail = jnp.where(row == 0, last_a[s : s + 1, :], last_b[s : s + 1, :])
                out[there * 2 + core_there] = jnp.where(lane < 81, main, tail)


def local_step(occ_ref, vir_ref, eps_occ_ref, eps_vir_ref, amp_ref, ovov, partner,
               scale, cycle, amp, occ, vir, eps_occ, eps_vir, left_a, left_b, panel_a, panel_b, sems):
    x, z, y, core = places()
    copies = [
        pltpu.make_async_copy(source, target, sems.at[at])
        for at, (source, target) in enumerate(
            ((occ_ref, occ), (vir_ref, vir), (eps_occ_ref, eps_occ), (eps_vir_ref, eps_vir), (amp_ref, amp))
        )
    ]
    for copy in copies:
        copy.start()
    panel_a[...] = jnp.zeros_like(panel_a)
    panel_b[...] = jnp.zeros_like(panel_b)
    left_a[...] = jnp.zeros_like(left_a)
    left_b[...] = jnp.zeros_like(left_b)
    lower = (z & 1) == 0
    for r in range(108):
        own, other = ovov[r], partner[r]
        panel_a[r : r + 1, 0:216] = jnp.where(lower, own, other)
        panel_b[r : r + 1, 0:216] = jnp.where(lower, other, own)
    for copy in copies:
        copy.wait()
    row_place = x * 4 + z
    shell = row_place >> 1
    first = 3 * (row_place & 1)
    irrep = 2 * y + core
    a, b = lane_orbitals((1, 1296))
    energy_a = jnp.zeros((1, 1296), F32)
    energy_b = jnp.zeros((1, 1296), F32)
    for slot in range(36):
        value = eps_vir[irrep, slot]
        energy_a = jnp.where(a == slot, value, energy_a)
        energy_b = jnp.where(b == slot, value, energy_b)
    lane_live = (a < vir[irrep]) & (b < vir[irrep])
    occ_here = occ[shell]
    for r in range(18):
        low, k = r // 6, r % 6
        i = first + low
        here = lane_live & (i < occ_here) & (k < occ_here)
        gap = eps_occ[shell, i] + eps_occ[shell, k] - energy_a - energy_b
        scale[r : r + 1, :] = jnp.where(here, 1.0, 0.0) / gap
        live = jnp.where(here, amp[low, k], 0.0)
        left, column = (left_a, 36 * k) if k < 3 else (left_b, 36 * (k - 3))
        for slot in range(36):
            left[36 * low + slot : 36 * low + slot + 1, column : column + 36] = live[
                :, 36 * slot : 36 * slot + 36
            ]
    dot = lambda p, q: jnp.dot(p, q, preferred_element_type=F32)
    total = None
    for left, panel in ((left_a, panel_a), (left_b, panel_b)):
        p_high, p_low = split(left[:, 0:112])
        q_high, q_low = split(panel[...])
        part = dot(p_high, q_high) + (dot(p_low, q_high) + dot(p_high, q_low))
        total = part if total is None else total + part
    for low in range(3):
        for j in range(6):
            r = 6 * low + j
            for slot in range(36):
                cycle[r : r + 1, 36 * slot : 36 * slot + 36] = total[
                    36 * low + slot : 36 * low + slot + 1, 36 * j : 36 * j + 36
                ]


def finish(sums, scale, cycle, out, wide):
    wide[...] = jnp.zeros_like(wide)
    lane8 = lax.broadcasted_iota(jnp.int32, (1, LANES), 1)
    lane = lax.broadcasted_iota(jnp.int32, (24, LANES), 1)
    for r in range(16):
        mains, lasts = [], []
        for core in range(2):
            block = sums[2 * r + core]
            mains.append(block)
            lasts.append(
                jnp.where(lane8 < 47, pltpu.roll(block, 47, 1)[0:1, :], pltpu.roll(block, 94, 1)[1:2, :])
            )
        stack = jnp.concatenate(mains + lasts + [jnp.zeros((6, LANES), F32)], axis=0)
        tile, start = divmod(81 * r, LANES)
        turned = pltpu.roll(stack, start, 1) if start else stack
        here = slice(tile * LANES, (tile + 1) * LANES)
        wide[:, here] = jnp.where((lane >= start) & (lane < start + 81), turned, wide[:, here])
        if start + 81 > LANES:
            after = slice((tile + 1) * LANES, (tile + 2) * LANES)
            wide[:, after] = jnp.where(lane < start + 81 - LANES, turned, wide[:, after])
    total = (wide[0:18, 0:1296] + cycle[...]) * scale[...]
    for r in range(18):
        out[r // 6, r % 6] = total[r : r + 1, :]


def on_device(amplitudes, vvvv, ovov, eps_occ, eps_vir, occ_count, vir_count):
    x, z, y, core = places()
    shape = jax.ShapeDtypeStruct
    integrals = vvvv.reshape(81, 1, 10368)
    window = shape((SPAN, PSLOT, 1, LANES), F32)
    flat = lambda value: value.reshape(PROWS, LANES)
    keep, send, first_v, second_v, home = pl.pallas_call(
        open_step,
        out_shape=[shape((SHARD, LANES), F32)] * 2 + [window] * 2
        + [shape((2 * SPAN, PSLOT, 1, LANES), F32)],
        in_specs=[HBM] * 4,
        out_specs=[VMEM] * 5,
        scratch_shapes=[
            pltpu.VMEM((24, WINDOW), F32),
            pltpu.VMEM((3, 6, 1, 1296), F32),
            pltpu.SMEM((8,), jnp.int32),
            pltpu.SMEM((8,), jnp.int32),
            pltpu.SemaphoreType.DMA((3,)),
            pltpu.SemaphoreType.DMA((4, SPAN)),
        ],
        compiler_params=HUGE,
    )(occ_count, vir_count, amplitudes, integrals)
    got = swap_core(send)
    home = home.reshape(2 * PROWS, LANES)
    home_other = swap_core(home)
    partner = lax.ppermute(ovov, "z", [(0, 1), (1, 0), (2, 3), (3, 2)])
    pair = pl.pallas_call(
        merge_pair,
        out_shape=shape((PAIR, LANES), F32),
        in_specs=[VMEM] * 2 + [ANY],
        out_specs=VMEM,
        compiler_params=SMALL,
    )(keep, got, partner)
    far_pair = ring(pair, "yy", (2, 2))
    quad = pl.pallas_call(
        join_pairs,
        out_shape=shape((QUAD, LANES), F32),
        in_specs=[VMEM] * 2 + [ANY],
        out_specs=VMEM,
        compiler_params=SMALL,
    )(pair, far_pair, home_other)
    first_v, second_v = hold(
        flat(first_v), flat(second_v), far_pair
    )
    moved_a = ring(first_v, "yy", (1, -1))
    moved_b = ring(second_v, "yy", (-1, 1))

    near, far = pl.pallas_call(
        gather_four,
        out_shape=[shape((4 * PAIR, LANES), F32)] * 2,
        in_specs=[VMEM] * 4,
        out_specs=[VMEM] * 2,
        compiler_params=SMALL,
    )(quad, *[ring(quad, "xz", step) for step in SHIFTS])
    near_blocks = [near] + [ring(near, "zx", step) for step in SHIFTS]
    far_blocks = [far] + [ring(far, "zx", step) for step in SHIFTS]

    moved_a, moved_b = hold(moved_a, moved_b, *near_blocks[1:])
    swapped_a, swapped_b = swap_core(moved_a), swap_core(moved_b)

    scale, cycle = pl.pallas_call(
        local_step,
        out_shape=[shape((18, 1296), F32)] * 2,
        in_specs=[HBM] * 5 + [VMEM] * 2,
        out_specs=[VMEM] * 2,
        scratch_shapes=[
            pltpu.VMEM((3, 6, 1, 1296), F32),
            pltpu.SMEM((8,), jnp.int32),
            pltpu.SMEM((8,), jnp.int32),
            pltpu.SMEM((8, 6), F32),
            pltpu.SMEM((8, 36), F32),
            pltpu.VMEM((112, 256), F32),
            pltpu.VMEM((112, 256), F32),
            pltpu.VMEM((112, 256), F32),
            pltpu.VMEM((112, 256), F32),
            pltpu.SemaphoreType.DMA((5,)),
        ],
        compiler_params=SMALL,
        cost_estimate=pl.CostEstimate(flops=100000000, bytes_accessed=1000000, transcendentals=0),
    )(occ_count, vir_count, eps_occ, eps_vir, amplitudes, ovov, partner)

    sums = [shape((144, 2 * LANES), F32)] * 3
    here_sum, below_sum, above_sum = pl.pallas_call(
        multiply_near,
        out_shape=sums,
        in_specs=[VMEM] * 10,
        out_specs=[VMEM] * 3,
        scratch_shapes=[pltpu.VMEM((16, DEPTH), F32), pltpu.VMEM((LANES, 2 * LANES), F32)],
        compiler_params=LARGE,
    )(*near_blocks, home, home_other, moved_a, swapped_b, moved_b, swapped_a)
    back_a = ring(below_sum, "yy", (-1, 1))
    back_b = ring(above_sum, "yy", (1, -1))
    packed = pl.pallas_call(
        multiply_far,
        out_shape=shape((32, 8, LANES), F32),
        in_specs=[VMEM] * 9,
        out_specs=VMEM,
        scratch_shapes=[pltpu.VMEM((16, DEPTH), F32)],
        compiler_params=LARGE,
    )(*far_blocks, home, home_other, here_sum, back_a, back_b)
    ladder = lax.all_to_all(packed, ("x", "z", "core"), 0, 0, tiled=True)
    return pl.pallas_call(
        finish,
        out_shape=shape((3, 6, 1, 1296), F32),
        in_specs=[VMEM] * 3,
        out_specs=VMEM,
        scratch_shapes=[pltpu.VMEM((24, WINDOW), F32)],
        compiler_params=SMALL,
    )(ladder, scale, cycle)


def solution(mesh):
    fine = Mesh(mesh.devices.reshape(4, 4, 4, 2), AXES)
    rows, cols = ("x", "z"), ("y", "core")
    return jax.shard_map(
        on_device,
        mesh=fine,
        in_specs=(P(rows, None, cols, None), P(cols, rows, None), P(rows, cols, None), P(), P(), P(), P()),
        out_specs=P(rows, None, cols, None),
        check_vma=False,
    )
```

```python
import jax
import jax.numpy as jnp
from jax import lax
from jax.experimental import pallas as pl
from jax.experimental.pallas import tpu as pltpu
from jax.sharding import Mesh, PartitionSpec as P

AXES = ("x", "z", "y", "core")
SHIFTS = ((1, 1), (-1, -1), (2, 2))
STEPS = (0, 1, -1, 2)
LANES = 128
TILES = 11
WINDOW = TILES * LANES
SPAN = 21
DEPTH = SPAN * LANES
MAIN = 8 * TILES
SHARD = 104
PMAIN = 8 * SPAN
PAIR = 192
QUAD = 2 * PAIR
PSLOT = 88
PROWS = SPAN * PSLOT
F32 = jnp.float32
BF16 = jnp.bfloat16
ANY = pl.BlockSpec(memory_space=pl.ANY)
HBM = pl.BlockSpec(memory_space=pltpu.HBM)
VMEM = pl.BlockSpec(memory_space=pltpu.VMEM)
HUGE = pltpu.CompilerParams(vmem_limit_bytes=56 * 1024 * 1024)
SMALL = pltpu.CompilerParams(vmem_limit_bytes=8 * 1024 * 1024)
LARGE = pltpu.CompilerParams(vmem_limit_bytes=28 * 1024 * 1024)


def ring(value, axes, steps):
    pairs = []
    for x in range(4):
        for z in range(4):
            for y in range(4):
                for core in range(2):
                    here = {"x": x, "z": z, "y": y, "core": core}
                    there = dict(here)
                    there[axes[core]] = (there[axes[core]] + steps[core]) % 4
                    pairs.append(
                        tuple(((p["x"] * 4 + p["z"]) * 4 + p["y"]) * 2 + p["core"] for p in (here, there))
                    )
    return lax.ppermute(value, AXES, pairs)


def swap_core(value):
    return lax.ppermute(value, "core", [(0, 1), (1, 0)])


def places():
    return tuple(lax.axis_index(name) for name in AXES)


def lane_orbitals(shape):
    lane = lax.broadcasted_iota(jnp.int32, shape, 1)
    a = jnp.floor((lane.astype(F32) + 0.5) * (1.0 / 36.0)).astype(jnp.int32)
    return a, lane - 36 * a


def window_copies(integrals, ref, first, sems, base):
    copies = []
    for t in range(SPAN):
        start = pl.multiple_of((base + t) * LANES, LANES)
        copies.append(
            pltpu.make_async_copy(integrals.at[:, :, pl.ds(start, LANES)], ref.at[first + t, 0:81], sems.at[t])
        )
    return copies


def open_step(occ_ref, vir_ref, amp_ref, integrals, keep_out, send_out, first_out, second_out, home_out,
              wide, amp, occ, vir, keep, send, first_v, second_v, home, sems, cut_sems, out_sems):
    x, z, y, core = places()
    copies = [
        pltpu.make_async_copy(source, target, sems.at[at])
        for at, (source, target) in enumerate(((occ_ref, occ), (vir_ref, vir), (amp_ref, amp)))
    ]
    groups = [
        window_copies(integrals, first_v, 0, cut_sems.at[0], ((y + 1 + 2 * core) & 3) * 20),
        window_copies(integrals, second_v, 0, cut_sems.at[1], ((y + 3 - 2 * core) & 3) * 20),
        window_copies(integrals, home, 0, cut_sems.at[2], y * 20),
        window_copies(integrals, home, SPAN, cut_sems.at[3], ((y + 2) & 3) * 20),
    ]
    outs = [
        pltpu.make_async_copy(source, target, out_sems.at[at])
        for at, (source, target) in enumerate(
            (
                (first_v, first_out),
                (second_v, second_out),
                (home.at[0:SPAN], home_out.at[0:SPAN]),
                (home.at[SPAN : 2 * SPAN], home_out.at[SPAN : 2 * SPAN]),
                (keep, keep_out),
                (send, send_out),
            )
        )
    ]
    for copy in copies:
        copy.start()
    for group in groups:
        for copy in group:
            copy.start()
    wide[...] = jnp.zeros_like(wide)
    for copy in copies:
        copy.wait()
    for row in range(18):
        wide[row : row + 1, 0:1296] = amp[row // 6, row % 6]
    row_place = x * 4 + z
    occ_here = occ[row_place >> 1]
    first = 3 * (row_place & 1)
    irrep = 2 * y + core
    vir_here = vir[irrep]
    a, b = lane_orbitals(wide.shape)
    row = lax.broadcasted_iota(jnp.int32, wide.shape, 0)
    i_low = (row * 43) >> 8
    j = row - 6 * i_low
    live = (a < vir_here) & (b < vir_here) & (i_low + first < occ_here) & (j < occ_here)
    moved = pltpu.roll(jnp.where(live, wide[...], 0.0), 16 * irrep, 1)

    def write(ref, half):
        for t in range(TILES):
            columns = slice(t * LANES, (t + 1) * LANES)
            ref[8 * t : 8 * t + 8, :] = moved[8 * half : 8 * half + 8, columns]
            ref[MAIN + t : MAIN + t + 1, :] = moved[16 + half : 17 + half, columns]
        ref[MAIN + TILES : SHARD, :] = jnp.zeros((SHARD - MAIN - TILES, LANES), F32)

    @pl.when(core == 0)
    def _():
        write(keep, 0)
        write(send, 1)

    @pl.when(core == 1)
    def _():
        write(keep, 1)
        write(send, 0)

    for copy in outs[4:]:
        copy.start()
    for group, out in zip(groups, outs):
        for copy in group:
            copy.wait()
        out.start()
    for copy in outs:
        copy.wait()


def merge_irreps(even, odd, out, at):
    gap = SPAN - TILES
    out[at : at + 8 * gap, :] = even[0 : 8 * gap, :]
    out[at + 8 * gap : at + MAIN, :] = even[8 * gap : MAIN, :] + odd[0:8, :]
    out[at + MAIN : at + PMAIN, :] = odd[8:MAIN, :]
    extra = at + PMAIN
    out[extra : extra + gap, :] = even[MAIN : MAIN + gap, :]
    out[extra + gap : extra + TILES, :] = even[MAIN + gap : MAIN + TILES, :] + odd[MAIN : MAIN + 1, :]
    out[extra + TILES : extra + SPAN, :] = odd[MAIN + 1 : MAIN + TILES, :]
    out[extra + SPAN : at + PAIR, :] = jnp.zeros((PAIR - PMAIN - SPAN, LANES), F32)


def merge_pair(keep, got, out):
    core = lax.axis_index("core")

    @pl.when(core == 0)
    def _():
        merge_irreps(keep, got, out, 0)

    @pl.when(core == 1)
    def _():
        merge_irreps(got, keep, out, 0)


def join_pairs(near, far, home_other, out):
    out[0:PAIR, :] = near[...]
    out[PAIR:QUAD, :] = far[...]


def gather_four(b0, b1, b2, b3, near, far):
    for at, block in enumerate((b0, b1, b2, b3)):
        near[at * PAIR : (at + 1) * PAIR, :] = block[0:PAIR, :]
        far[at * PAIR : (at + 1) * PAIR, :] = block[PAIR:QUAD, :]


def nothing(*refs):
    pass


def hold(a, b, *witnesses):
    return pl.pallas_call(
        nothing,
        out_shape=[jax.ShapeDtypeStruct(v.shape, v.dtype) for v in (a, b)],
        in_specs=[ANY] * (2 + len(witnesses)),
        out_specs=[ANY] * 2,
        input_output_aliases={0: 0, 1: 1},
        compiler_params=SMALL,
    )(a, b, *witnesses)


def left_side(blocks, extra):
    for t in range(SPAN):
        for d, block in enumerate(blocks):
            extra[4 * d : 4 * d + 4, t * LANES : (t + 1) * LANES] = block[pl.ds(PMAIN + t, 4, stride=PAIR), :]
    rows = []
    for block in blocks:
        for e in range(4):
            rows.append(
                jnp.concatenate(
                    [block[e * PAIR + 8 * t : e * PAIR + 8 * t + 8, :] for t in range(SPAN)], axis=1
                )
            )
    return split(jnp.concatenate(rows + [extra[...]], axis=0))


def split(value):
    high = value.astype(BF16)
    return high, (value - high.astype(F32)).astype(BF16)


def tiles_side(ref, first):
    return jnp.concatenate(
        [ref[(first + t) * PSLOT : (first + t + 1) * PSLOT, :] for t in range(SPAN)], axis=1
    )


def last_by_last(p, q):
    return lax.dot_general(p, q, (((1,), (1,)), ((), ())), preferred_element_type=F32)


def multiply_near(b0, b1, b2, b3, home, home_other, below, below_other, above, above_other,
                  here_sum, below_sum, above_sum, extra, turned):
    high, low = left_side((b0, b1, b2, b3), extra)
    sides = [tiles_side(ref, 0) for ref in (home, home_other, below, below_other, above, above_other)]
    v_high, v_low = split(jnp.concatenate(sides, axis=0))
    total = last_by_last(v_high, high) + (last_by_last(v_low, high) + last_by_last(v_high, low))
    turned[...] = jnp.zeros_like(turned)
    for at, ref in enumerate((here_sum, below_sum, above_sum)):
        for side in range(2):
            rows = slice((2 * at + side) * PSLOT, (2 * at + side + 1) * PSLOT)
            turned[0:PSLOT, 0:144] = total[rows, :]
            ref[:, side * LANES : (side + 1) * LANES] = turned[...].T[0:144, :]


def multiply_far(b0, b1, b2, b3, home, home_other, here_sum, back_a, back_b, out, extra):
    x, z, y, core = places()
    high, low = left_side((b0, b1, b2, b3), extra)
    partial = here_sum[...] + back_a[...] + back_b[...]
    row = lax.broadcasted_iota(jnp.int32, (8, LANES), 0)
    lane = lax.broadcasted_iota(jnp.int32, (8, LANES), 1)
    pad = jnp.zeros((LANES - PSLOT, DEPTH), BF16)
    sides = [split(tiles_side(ref, SPAN)) for ref in (home, home_other)]
    v_high = jnp.concatenate([sides[0][0], pad, sides[1][0], pad], axis=0)
    v_low = jnp.concatenate([sides[0][1], pad, sides[1][1], pad], axis=0)
    total = partial + (
        last_by_last(high, v_high) + (last_by_last(low, v_high) + last_by_last(high, v_low))
    )
    for side in range(2):
        columns = slice(side * LANES, (side + 1) * LANES)
        last = total[128:144, columns]
        last_a = pltpu.roll(last, 81, 1)
        last_b = pltpu.roll(last, 34, 1)
        core_there = core if side == 0 else 1 - core
        for d in range(4):
            for e in range(4):
                s = 4 * d + e
                x_step = jnp.where(core == 0, STEPS[e], STEPS[d])
                z_step = jnp.where(core == 0, STEPS[d], STEPS[e])
                there = ((x - x_step) & 3) * 4 + ((z - z_step) & 3)
                main = total[8 * s : 8 * s + 8, columns]
                tail = jnp.where(row == 0, last_a[s : s + 1, :], last_b[s : s + 1, :])
                out[there * 2 + core_there] = jnp.where(lane < 81, main, tail)


def local_step(occ_ref, vir_ref, eps_occ_ref, eps_vir_ref, amp_ref, ovov, partner,
               scale, cycle, amp, occ, vir, eps_occ, eps_vir, left_a, left_b, panel_a, panel_b, sems):
    x, z, y, core = places()
    copies = [
        pltpu.make_async_copy(source, target, sems.at[at])
        for at, (source, target) in enumerate(
            ((occ_ref, occ), (vir_ref, vir), (eps_occ_ref, eps_occ), (eps_vir_ref, eps_vir), (amp_ref, amp))
        )
    ]
    for copy in copies:
        copy.start()
    panel_a[...] = jnp.zeros_like(panel_a)
    panel_b[...] = jnp.zeros_like(panel_b)
    left_a[...] = jnp.zeros_like(left_a)
    left_b[...] = jnp.zeros_like(left_b)
    lower = (z & 1) == 0
    for r in range(108):
        own, other = ovov[r], partner[r]
        panel_a[r : r + 1, 0:216] = jnp.where(lower, own, other)
        panel_b[r : r + 1, 0:216] = jnp.where(lower, other, own)
    for copy in copies:
        copy.wait()
    row_place = x * 4 + z
    shell = row_place >> 1
    first = 3 * (row_place & 1)
    irrep = 2 * y + core
    a, b = lane_orbitals((1, 1296))
    energy_a = jnp.zeros((1, 1296), F32)
    energy_b = jnp.zeros((1, 1296), F32)
    for slot in range(36):
        value = eps_vir[irrep, slot]
        energy_a = jnp.where(a == slot, value, energy_a)
        energy_b = jnp.where(b == slot, value, energy_b)
    lane_live = (a < vir[irrep]) & (b < vir[irrep])
    occ_here = occ[shell]
    for r in range(18):
        low, k = r // 6, r % 6
        i = first + low
        here = lane_live & (i < occ_here) & (k < occ_here)
        gap = eps_occ[shell, i] + eps_occ[shell, k] - energy_a - energy_b
        scale[r : r + 1, :] = jnp.where(here, 1.0, 0.0) / gap
        live = jnp.where(here, amp[low, k], 0.0)
        left, column = (left_a, 36 * k) if k < 3 else (left_b, 36 * (k - 3))
        for slot in range(36):
            left[36 * low + slot : 36 * low + slot + 1, column : column + 36] = live[
                :, 36 * slot : 36 * slot + 36
            ]
    dot = lambda p, q: jnp.dot(p, q, preferred_element_type=F32)
    total = None
    for left, panel in ((left_a, panel_a), (left_b, panel_b)):
        p_high, p_low = split(left[:, 0:112])
        q_high, q_low = split(panel[...])
        part = dot(p_high, q_high) + (dot(p_low, q_high) + dot(p_high, q_low))
        total = part if total is None else total + part
    for low in range(3):
        for j in range(6):
            r = 6 * low + j
            for slot in range(36):
                cycle[r : r + 1, 36 * slot : 36 * slot + 36] = total[
                    36 * low + slot : 36 * low + slot + 1, 36 * j : 36 * j + 36
                ]


def finish(sums, scale, cycle, out, wide):
    wide[...] = jnp.zeros_like(wide)
    lane8 = lax.broadcasted_iota(jnp.int32, (1, LANES), 1)
    lane = lax.broadcasted_iota(jnp.int32, (24, LANES), 1)
    for r in range(16):
        mains, lasts = [], []
        for core in range(2):
            block = sums[2 * r + core]
            mains.append(block)
            lasts.append(
                jnp.where(lane8 < 47, pltpu.roll(block, 47, 1)[0:1, :], pltpu.roll(block, 94, 1)[1:2, :])
            )
        stack = jnp.concatenate(mains + lasts + [jnp.zeros((6, LANES), F32)], axis=0)
        tile, start = divmod(81 * r, LANES)
        turned = pltpu.roll(stack, start, 1) if start else stack
        here = slice(tile * LANES, (tile + 1) * LANES)
        wide[:, here] = jnp.where((lane >= start) & (lane < start + 81), turned, wide[:, here])
        if start + 81 > LANES:
            after = slice((tile + 1) * LANES, (tile + 2) * LANES)
            wide[:, after] = jnp.where(lane < start + 81 - LANES, turned, wide[:, after])
    total = (wide[0:18, 0:1296] + cycle[...]) * scale[...]
    for r in range(18):
        out[r // 6, r % 6] = total[r : r + 1, :]


def on_device(amplitudes, vvvv, ovov, eps_occ, eps_vir, occ_count, vir_count):
    x, z, y, core = places()
    shape = jax.ShapeDtypeStruct
    integrals = vvvv.reshape(81, 1, 10368)
    window = shape((SPAN, PSLOT, 1, LANES), F32)
    flat = lambda value: value.reshape(PROWS, LANES)
    keep, send, first_v, second_v, home = pl.pallas_call(
        open_step,
        out_shape=[shape((SHARD, LANES), F32)] * 2 + [window] * 2
        + [shape((2 * SPAN, PSLOT, 1, LANES), F32)],
        in_specs=[HBM] * 4,
        out_specs=[ANY] * 5,
        scratch_shapes=[
            pltpu.VMEM((24, WINDOW), F32),
            pltpu.VMEM((3, 6, 1, 1296), F32),
            pltpu.SMEM((8,), jnp.int32),
            pltpu.SMEM((8,), jnp.int32),
            pltpu.VMEM((SHARD, LANES), F32),
            pltpu.VMEM((SHARD, LANES), F32),
            pltpu.VMEM((SPAN, PSLOT, 1, LANES), F32),
            pltpu.VMEM((SPAN, PSLOT, 1, LANES), F32),
            pltpu.VMEM((2 * SPAN, PSLOT, 1, LANES), F32),
            pltpu.SemaphoreType.DMA((3,)),
            pltpu.SemaphoreType.DMA((4, SPAN)),
            pltpu.SemaphoreType.DMA((6,)),
        ],
        compiler_params=HUGE,
    )(occ_count, vir_count, amplitudes, integrals)
    got = swap_core(send)
    home = home.reshape(2 * PROWS, LANES)
    home_other = swap_core(home)
    partner = lax.ppermute(ovov, "z", [(0, 1), (1, 0), (2, 3), (3, 2)])
    pair = pl.pallas_call(
        merge_pair,
        out_shape=shape((PAIR, LANES), F32),
        in_specs=[VMEM] * 2,
        out_specs=VMEM,
        compiler_params=SMALL,
    )(keep, got)
    far_pair = ring(pair, "yy", (2, 2))
    quad = pl.pallas_call(
        join_pairs,
        out_shape=shape((QUAD, LANES), F32),
        in_specs=[VMEM] * 2 + [ANY],
        out_specs=VMEM,
        compiler_params=SMALL,
    )(pair, far_pair, home_other)
    first_v, second_v = hold(
        flat(first_v), flat(second_v), far_pair, partner
    )
    moved_a = ring(first_v, "yy", (1, -1))
    moved_b = ring(second_v, "yy", (-1, 1))

    near, far = pl.pallas_call(
        gather_four,
        out_shape=[shape((4 * PAIR, LANES), F32)] * 2,
        in_specs=[VMEM] * 4,
        out_specs=[VMEM] * 2,
        compiler_params=SMALL,
    )(quad, *[ring(quad, "xz", step) for step in SHIFTS])
    near_blocks = [near] + [ring(near, "zx", step) for step in SHIFTS]
    far_blocks = [far] + [ring(far, "zx", step) for step in SHIFTS]

    moved_a, moved_b = hold(moved_a, moved_b, *near_blocks[1:])
    swapped_a, swapped_b = swap_core(moved_a), swap_core(moved_b)

    scale, cycle = pl.pallas_call(
        local_step,
        out_shape=[shape((18, 1296), F32)] * 2,
        in_specs=[HBM] * 5 + [VMEM] * 2,
        out_specs=[VMEM] * 2,
        scratch_shapes=[
            pltpu.VMEM((3, 6, 1, 1296), F32),
            pltpu.SMEM((8,), jnp.int32),
            pltpu.SMEM((8,), jnp.int32),
            pltpu.SMEM((8, 6), F32),
            pltpu.SMEM((8, 36), F32),
            pltpu.VMEM((112, 256), F32),
            pltpu.VMEM((112, 256), F32),
            pltpu.VMEM((112, 256), F32),
            pltpu.VMEM((112, 256), F32),
            pltpu.SemaphoreType.DMA((5,)),
        ],
        compiler_params=SMALL,
        cost_estimate=pl.CostEstimate(flops=100000000, bytes_accessed=1000000, transcendentals=0),
    )(occ_count, vir_count, eps_occ, eps_vir, amplitudes, ovov, partner)

    sums = [shape((144, 2 * LANES), F32)] * 3
    here_sum, below_sum, above_sum = pl.pallas_call(
        multiply_near,
        out_shape=sums,
        in_specs=[VMEM] * 10,
        out_specs=[VMEM] * 3,
        scratch_shapes=[pltpu.VMEM((16, DEPTH), F32), pltpu.VMEM((LANES, 2 * LANES), F32)],
        compiler_params=LARGE,
    )(*near_blocks, home, home_other, moved_a, swapped_b, moved_b, swapped_a)
    back_a = ring(below_sum, "yy", (-1, 1))
    back_b = ring(above_sum, "yy", (1, -1))
    packed = pl.pallas_call(
        multiply_far,
        out_shape=shape((32, 8, LANES), F32),
        in_specs=[VMEM] * 9,
        out_specs=VMEM,
        scratch_shapes=[pltpu.VMEM((16, DEPTH), F32)],
        compiler_params=LARGE,
    )(*far_blocks, home, home_other, here_sum, back_a, back_b)
    ladder = lax.all_to_all(packed, ("x", "z", "core"), 0, 0, tiled=True)
    return pl.pallas_call(
        finish,
        out_shape=shape((3, 6, 1, 1296), F32),
        in_specs=[VMEM] * 3,
        out_specs=VMEM,
        scratch_shapes=[pltpu.VMEM((24, WINDOW), F32)],
        compiler_params=SMALL,
    )(ladder, scale, cycle)


def solution(mesh):
    fine = Mesh(mesh.devices.reshape(4, 4, 4, 2), AXES)
    rows, cols = ("x", "z"), ("y", "core")
    return jax.shard_map(
        on_device,
        mesh=fine,
        in_specs=(P(rows, None, cols, None), P(cols, rows, None), P(rows, cols, None), P(), P(), P(), P()),
        out_specs=P(rows, None, cols, None),
        check_vma=False,
    )
```

```python
import jax
import jax.numpy as jnp
from jax import lax
from jax.experimental import pallas as pl
from jax.experimental.pallas import tpu as pltpu
from jax.sharding import Mesh, PartitionSpec as P

AXES = ("x", "z", "y", "core")
SHIFTS = ((1, 1), (-1, -1), (2, 2))
STEPS = (0, 1, -1, 2)
LANES = 128
TILES = 11
WINDOW = TILES * LANES
SPAN = 21
DEPTH = SPAN * LANES
MAIN = 8 * TILES
SHARD = 104
PMAIN = 8 * SPAN
PAIR = 192
QUAD = 2 * PAIR
PSLOT = 88
PROWS = SPAN * PSLOT
F32 = jnp.float32
BF16 = jnp.bfloat16
ANY = pl.BlockSpec(memory_space=pl.ANY)
HBM = pl.BlockSpec(memory_space=pltpu.HBM)
VMEM = pl.BlockSpec(memory_space=pltpu.VMEM)
HUGE = pltpu.CompilerParams(vmem_limit_bytes=56 * 1024 * 1024)
SMALL = pltpu.CompilerParams(vmem_limit_bytes=8 * 1024 * 1024)
LARGE = pltpu.CompilerParams(vmem_limit_bytes=28 * 1024 * 1024)


def ring(value, axes, steps):
    pairs = []
    for x in range(4):
        for z in range(4):
            for y in range(4):
                for core in range(2):
                    here = {"x": x, "z": z, "y": y, "core": core}
                    there = dict(here)
                    there[axes[core]] = (there[axes[core]] + steps[core]) % 4
                    pairs.append(
                        tuple(((p["x"] * 4 + p["z"]) * 4 + p["y"]) * 2 + p["core"] for p in (here, there))
                    )
    return lax.ppermute(value, AXES, pairs)


def swap_core(value):
    return lax.ppermute(value, "core", [(0, 1), (1, 0)])


def places():
    return tuple(lax.axis_index(name) for name in AXES)


def lane_orbitals(shape):
    lane = lax.broadcasted_iota(jnp.int32, shape, 1)
    a = jnp.floor((lane.astype(F32) + 0.5) * (1.0 / 36.0)).astype(jnp.int32)
    return a, lane - 36 * a


def window_copies(integrals, ref, first, sems, base):
    copies = []
    for t in range(SPAN):
        start = pl.multiple_of((base + t) * LANES, LANES)
        copies.append(
            pltpu.make_async_copy(integrals.at[:, :, pl.ds(start, LANES)], ref.at[first + t, 0:81], sems.at[t])
        )
    return copies


def open_step(occ_ref, vir_ref, amp_ref, integrals, keep_out, send_out, first_out, second_out, home_out,
              wide, amp, occ, vir, keep, send, first_v, second_v, home, sems, cut_sems, out_sems):
    x, z, y, core = places()
    copies = [
        pltpu.make_async_copy(source, target, sems.at[at])
        for at, (source, target) in enumerate(((occ_ref, occ), (vir_ref, vir), (amp_ref, amp)))
    ]
    groups = [
        window_copies(integrals, first_v, 0, cut_sems.at[0], ((y + 1 + 2 * core) & 3) * 20),
        window_copies(integrals, second_v, 0, cut_sems.at[1], ((y + 3 - 2 * core) & 3) * 20),
        window_copies(integrals, home, 0, cut_sems.at[2], y * 20),
        window_copies(integrals, home, SPAN, cut_sems.at[3], ((y + 2) & 3) * 20),
    ]
    outs = [
        pltpu.make_async_copy(source, target, out_sems.at[at])
        for at, (source, target) in enumerate(
            (
                (first_v, first_out),
                (second_v, second_out),
                (home.at[0:SPAN], home_out.at[0:SPAN]),
                (home.at[SPAN : 2 * SPAN], home_out.at[SPAN : 2 * SPAN]),
                (keep, keep_out),
                (send, send_out),
            )
        )
    ]
    for copy in copies:
        copy.start()
    for group in groups:
        for copy in group:
            copy.start()
    wide[...] = jnp.zeros_like(wide)
    for copy in copies:
        copy.wait()
    for row in range(18):
        wide[row : row + 1, 0:1296] = amp[row // 6, row % 6]
    row_place = x * 4 + z
    occ_here = occ[row_place >> 1]
    first = 3 * (row_place & 1)
    irrep = 2 * y + core
    vir_here = vir[irrep]
    a, b = lane_orbitals(wide.shape)
    row = lax.broadcasted_iota(jnp.int32, wide.shape, 0)
    i_low = (row * 43) >> 8
    j = row - 6 * i_low
    live = (a < vir_here) & (b < vir_here) & (i_low + first < occ_here) & (j < occ_here)
    moved = pltpu.roll(jnp.where(live, wide[...], 0.0), 16 * irrep, 1)

    def write(ref, half):
        for t in range(TILES):
            columns = slice(t * LANES, (t + 1) * LANES)
            ref[8 * t : 8 * t + 8, :] = moved[8 * half : 8 * half + 8, columns]
            ref[MAIN + t : MAIN + t + 1, :] = moved[16 + half : 17 + half, columns]
        ref[MAIN + TILES : SHARD, :] = jnp.zeros((SHARD - MAIN - TILES, LANES), F32)

    @pl.when(core == 0)
    def _():
        write(keep, 0)
        write(send, 1)

    @pl.when(core == 1)
    def _():
        write(keep, 1)
        write(send, 0)

    for copy in outs[4:]:
        copy.start()
    for group, out in zip(groups, outs):
        for copy in group:
            copy.wait()
        out.start()
    for copy in outs:
        copy.wait()


def merge_irreps(even, odd, out, at):
    gap = SPAN - TILES
    out[at : at + 8 * gap, :] = even[0 : 8 * gap, :]
    out[at + 8 * gap : at + MAIN, :] = even[8 * gap : MAIN, :] + odd[0:8, :]
    out[at + MAIN : at + PMAIN, :] = odd[8:MAIN, :]
    extra = at + PMAIN
    out[extra : extra + gap, :] = even[MAIN : MAIN + gap, :]
    out[extra + gap : extra + TILES, :] = even[MAIN + gap : MAIN + TILES, :] + odd[MAIN : MAIN + 1, :]
    out[extra + TILES : extra + SPAN, :] = odd[MAIN + 1 : MAIN + TILES, :]
    out[extra + SPAN : at + PAIR, :] = jnp.zeros((PAIR - PMAIN - SPAN, LANES), F32)


def merge_pair(keep, got, home, out, home_out):
    core = lax.axis_index("core")

    @pl.when(core == 0)
    def _():
        merge_irreps(keep, got, out, 0)

    @pl.when(core == 1)
    def _():
        merge_irreps(got, keep, out, 0)


def join_pairs(near, far, home_other, out):
    out[0:PAIR, :] = near[...]
    out[PAIR:QUAD, :] = far[...]


def gather_four(b0, b1, b2, b3, near, far):
    for at, block in enumerate((b0, b1, b2, b3)):
        near[at * PAIR : (at + 1) * PAIR, :] = block[0:PAIR, :]
        far[at * PAIR : (at + 1) * PAIR, :] = block[PAIR:QUAD, :]


def nothing(*refs):
    pass


def hold(values, *witnesses):
    kept = range(len(values))
    return pl.pallas_call(
        nothing,
        out_shape=[jax.ShapeDtypeStruct(value.shape, value.dtype) for value in values],
        in_specs=[ANY] * (len(values) + len(witnesses)),
        out_specs=[ANY] * len(values),
        input_output_aliases={at: at for at in kept},
        compiler_params=SMALL,
    )(*values, *witnesses)


def left_side(blocks, extra):
    for t in range(SPAN):
        for d, block in enumerate(blocks):
            extra[4 * d : 4 * d + 4, t * LANES : (t + 1) * LANES] = block[pl.ds(PMAIN + t, 4, stride=PAIR), :]
    rows = []
    for block in blocks:
        for e in range(4):
            rows.append(
                jnp.concatenate(
                    [block[e * PAIR + 8 * t : e * PAIR + 8 * t + 8, :] for t in range(SPAN)], axis=1
                )
            )
    return split(jnp.concatenate(rows + [extra[...]], axis=0))


def split(value):
    high = value.astype(BF16)
    return high, (value - high.astype(F32)).astype(BF16)


def tiles_side(ref, first):
    return jnp.concatenate(
        [ref[(first + t) * PSLOT : (first + t + 1) * PSLOT, :] for t in range(SPAN)], axis=1
    )


def last_by_last(p, q):
    return lax.dot_general(p, q, (((1,), (1,)), ((), ())), preferred_element_type=F32)


def multiply_near(b0, b1, b2, b3, home, home_other, below, below_other, above, above_other,
                  here_sum, below_sum, above_sum, extra, turned):
    high, low = left_side((b0, b1, b2, b3), extra)
    sides = [tiles_side(ref, 0) for ref in (home, home_other, below, below_other, above, above_other)]
    v_high, v_low = split(jnp.concatenate(sides, axis=0))
    total = last_by_last(v_high, high) + (last_by_last(v_low, high) + last_by_last(v_high, low))
    turned[...] = jnp.zeros_like(turned)
    for at, ref in enumerate((here_sum, below_sum, above_sum)):
        for side in range(2):
            rows = slice((2 * at + side) * PSLOT, (2 * at + side + 1) * PSLOT)
            turned[0:PSLOT, 0:144] = total[rows, :]
            ref[:, side * LANES : (side + 1) * LANES] = turned[...].T[0:144, :]


def multiply_far(b0, b1, b2, b3, home, home_other, here_sum, back_a, back_b, out, extra):
    x, z, y, core = places()
    high, low = left_side((b0, b1, b2, b3), extra)
    partial = here_sum[...] + back_a[...] + back_b[...]
    row = lax.broadcasted_iota(jnp.int32, (8, LANES), 0)
    lane = lax.broadcasted_iota(jnp.int32, (8, LANES), 1)
    pad = jnp.zeros((LANES - PSLOT, DEPTH), BF16)
    sides = [split(tiles_side(ref, SPAN)) for ref in (home, home_other)]
    v_high = jnp.concatenate([sides[0][0], pad, sides[1][0], pad], axis=0)
    v_low = jnp.concatenate([sides[0][1], pad, sides[1][1], pad], axis=0)
    total = partial + (
        last_by_last(high, v_high) + (last_by_last(low, v_high) + last_by_last(high, v_low))
    )
    for side in range(2):
        columns = slice(side * LANES, (side + 1) * LANES)
        last = total[128:144, columns]
        last_a = pltpu.roll(last, 81, 1)
        last_b = pltpu.roll(last, 34, 1)
        core_there = core if side == 0 else 1 - core
        for d in range(4):
            for e in range(4):
                s = 4 * d + e
                x_step = jnp.where(core == 0, STEPS[e], STEPS[d])
                z_step = jnp.where(core == 0, STEPS[d], STEPS[e])
                there = ((x - x_step) & 3) * 4 + ((z - z_step) & 3)
                main = total[8 * s : 8 * s + 8, columns]
                tail = jnp.where(row == 0, last_a[s : s + 1, :], last_b[s : s + 1, :])
                out[there * 2 + core_there] = jnp.where(lane < 81, main, tail)


def local_step(occ_ref, vir_ref, eps_occ_ref, eps_vir_ref, amp_ref, ovov, partner,
               scale, cycle, amp, occ, vir, eps_occ, eps_vir, left_a, left_b, panel_a, panel_b, sems):
    x, z, y, core = places()
    copies = [
        pltpu.make_async_copy(source, target, sems.at[at])
        for at, (source, target) in enumerate(
            ((occ_ref, occ), (vir_ref, vir), (eps_occ_ref, eps_occ), (eps_vir_ref, eps_vir), (amp_ref, amp))
        )
    ]
    for copy in copies:
        copy.start()
    panel_a[...] = jnp.zeros_like(panel_a)
    panel_b[...] = jnp.zeros_like(panel_b)
    left_a[...] = jnp.zeros_like(left_a)
    left_b[...] = jnp.zeros_like(left_b)
    lower = (z & 1) == 0
    for r in range(108):
        own, other = ovov[r], partner[r]
        panel_a[r : r + 1, 0:216] = jnp.where(lower, own, other)
        panel_b[r : r + 1, 0:216] = jnp.where(lower, other, own)
    for copy in copies:
        copy.wait()
    row_place = x * 4 + z
    shell = row_place >> 1
    first = 3 * (row_place & 1)
    irrep = 2 * y + core
    a, b = lane_orbitals((1, 1296))
    energy_a = jnp.zeros((1, 1296), F32)
    energy_b = jnp.zeros((1, 1296), F32)
    for slot in range(36):
        value = eps_vir[irrep, slot]
        energy_a = jnp.where(a == slot, value, energy_a)
        energy_b = jnp.where(b == slot, value, energy_b)
    lane_live = (a < vir[irrep]) & (b < vir[irrep])
    occ_here = occ[shell]
    for r in range(18):
        low, k = r // 6, r % 6
        i = first + low
        here = lane_live & (i < occ_here) & (k < occ_here)
        gap = eps_occ[shell, i] + eps_occ[shell, k] - energy_a - energy_b
        scale[r : r + 1, :] = jnp.where(here, 1.0, 0.0) / gap
        live = jnp.where(here, amp[low, k], 0.0)
        left, column = (left_a, 36 * k) if k < 3 else (left_b, 36 * (k - 3))
        for slot in range(36):
            left[36 * low + slot : 36 * low + slot + 1, column : column + 36] = live[
                :, 36 * slot : 36 * slot + 36
            ]
    dot = lambda p, q: jnp.dot(p, q, preferred_element_type=F32)
    total = None
    for left, panel in ((left_a, panel_a), (left_b, panel_b)):
        p_high, p_low = split(left[:, 0:112])
        q_high, q_low = split(panel[...])
        part = dot(p_high, q_high) + (dot(p_low, q_high) + dot(p_high, q_low))
        total = part if total is None else total + part
    for low in range(3):
        for j in range(6):
            r = 6 * low + j
            for slot in range(36):
                cycle[r : r + 1, 36 * slot : 36 * slot + 36] = total[
                    36 * low + slot : 36 * low + slot + 1, 36 * j : 36 * j + 36
                ]


def finish(sums, scale, cycle, out, wide):
    wide[...] = jnp.zeros_like(wide)
    lane8 = lax.broadcasted_iota(jnp.int32, (1, LANES), 1)
    lane = lax.broadcasted_iota(jnp.int32, (24, LANES), 1)
    for r in range(16):
        mains, lasts = [], []
        for core in range(2):
            block = sums[2 * r + core]
            mains.append(block)
            lasts.append(
                jnp.where(lane8 < 47, pltpu.roll(block, 47, 1)[0:1, :], pltpu.roll(block, 94, 1)[1:2, :])
            )
        stack = jnp.concatenate(mains + lasts + [jnp.zeros((6, LANES), F32)], axis=0)
        tile, start = divmod(81 * r, LANES)
        turned = pltpu.roll(stack, start, 1) if start else stack
        here = slice(tile * LANES, (tile + 1) * LANES)
        wide[:, here] = jnp.where((lane >= start) & (lane < start + 81), turned, wide[:, here])
        if start + 81 > LANES:
            after = slice((tile + 1) * LANES, (tile + 2) * LANES)
            wide[:, after] = jnp.where(lane < start + 81 - LANES, turned, wide[:, after])
    total = (wide[0:18, 0:1296] + cycle[...]) * scale[...]
    for r in range(18):
        out[r // 6, r % 6] = total[r : r + 1, :]


def on_device(amplitudes, vvvv, ovov, eps_occ, eps_vir, occ_count, vir_count):
    x, z, y, core = places()
    shape = jax.ShapeDtypeStruct
    integrals = vvvv.reshape(81, 1, 10368)
    window = shape((SPAN, PSLOT, 1, LANES), F32)
    flat = lambda value: value.reshape(PROWS, LANES)
    keep, send, first_v, second_v, home = pl.pallas_call(
        open_step,
        out_shape=[shape((SHARD, LANES), F32)] * 2 + [window] * 2
        + [shape((2 * SPAN, PSLOT, 1, LANES), F32)],
        in_specs=[HBM] * 4,
        out_specs=[ANY] * 5,
        scratch_shapes=[
            pltpu.VMEM((24, WINDOW), F32),
            pltpu.VMEM((3, 6, 1, 1296), F32),
            pltpu.SMEM((8,), jnp.int32),
            pltpu.SMEM((8,), jnp.int32),
            pltpu.VMEM((SHARD, LANES), F32),
            pltpu.VMEM((SHARD, LANES), F32),
            pltpu.VMEM((SPAN, PSLOT, 1, LANES), F32),
            pltpu.VMEM((SPAN, PSLOT, 1, LANES), F32),
            pltpu.VMEM((2 * SPAN, PSLOT, 1, LANES), F32),
            pltpu.SemaphoreType.DMA((3,)),
            pltpu.SemaphoreType.DMA((4, SPAN)),
            pltpu.SemaphoreType.DMA((6,)),
        ],
        compiler_params=HUGE,
    )(occ_count, vir_count, amplitudes, integrals)
    got = swap_core(send)
    moved_a = ring(flat(first_v), "yy", (1, -1))
    partner = lax.ppermute(ovov, "z", [(0, 1), (1, 0), (2, 3), (3, 2)])
    home = home.reshape(2 * PROWS, LANES)
    pair, home = pl.pallas_call(
        merge_pair,
        out_shape=[shape((PAIR, LANES), F32), shape(home.shape, F32)],
        in_specs=[VMEM] * 2 + [ANY],
        out_specs=[VMEM, ANY],
        input_output_aliases={2: 1},
        compiler_params=SMALL,
    )(keep, got, home)
    home_other = swap_core(home)
    far_pair = ring(pair, "yy", (2, 2))
    quad = pl.pallas_call(
        join_pairs,
        out_shape=shape((QUAD, LANES), F32),
        in_specs=[VMEM] * 2 + [ANY],
        out_specs=VMEM,
        compiler_params=SMALL,
    )(pair, far_pair, home_other)
    (second_v,) = hold([flat(second_v)], far_pair, partner)
    moved_b = ring(second_v, "yy", (-1, 1))

    near, far = pl.pallas_call(
        gather_four,
        out_shape=[shape((4 * PAIR, LANES), F32)] * 2,
        in_specs=[VMEM] * 4,
        out_specs=[VMEM] * 2,
        compiler_params=SMALL,
    )(quad, *[ring(quad, "xz", step) for step in SHIFTS])
    near_blocks = [near] + [ring(near, "zx", step) for step in SHIFTS]
    far_blocks = [far] + [ring(far, "zx", step) for step in SHIFTS]

    moved_a, moved_b = hold([moved_a, moved_b], *near_blocks[1:])
    swapped_a, swapped_b = swap_core(moved_a), swap_core(moved_b)

    scale, cycle = pl.pallas_call(
        local_step,
        out_shape=[shape((18, 1296), F32)] * 2,
        in_specs=[HBM] * 5 + [VMEM] * 2,
        out_specs=[VMEM] * 2,
        scratch_shapes=[
            pltpu.VMEM((3, 6, 1, 1296), F32),
            pltpu.SMEM((8,), jnp.int32),
            pltpu.SMEM((8,), jnp.int32),
            pltpu.SMEM((8, 6), F32),
            pltpu.SMEM((8, 36), F32),
            pltpu.VMEM((112, 256), F32),
            pltpu.VMEM((112, 256), F32),
            pltpu.VMEM((112, 256), F32),
            pltpu.VMEM((112, 256), F32),
            pltpu.SemaphoreType.DMA((5,)),
        ],
        compiler_params=SMALL,
        cost_estimate=pl.CostEstimate(flops=100000000, bytes_accessed=1000000, transcendentals=0),
    )(occ_count, vir_count, eps_occ, eps_vir, amplitudes, ovov, partner)

    sums = [shape((144, 2 * LANES), F32)] * 3
    here_sum, below_sum, above_sum = pl.pallas_call(
        multiply_near,
        out_shape=sums,
        in_specs=[VMEM] * 10,
        out_specs=[VMEM] * 3,
        scratch_shapes=[pltpu.VMEM((16, DEPTH), F32), pltpu.VMEM((LANES, 2 * LANES), F32)],
        compiler_params=LARGE,
    )(*near_blocks, home, home_other, moved_a, swapped_b, moved_b, swapped_a)
    back_a = ring(below_sum, "yy", (-1, 1))
    back_b = ring(above_sum, "yy", (1, -1))
    packed = pl.pallas_call(
        multiply_far,
        out_shape=shape((32, 8, LANES), F32),
        in_specs=[VMEM] * 9,
        out_specs=VMEM,
        scratch_shapes=[pltpu.VMEM((16, DEPTH), F32)],
        compiler_params=LARGE,
    )(*far_blocks, home, home_other, here_sum, back_a, back_b)
    ladder = lax.all_to_all(packed, ("x", "z", "core"), 0, 0, tiled=True)
    return pl.pallas_call(
        finish,
        out_shape=shape((3, 6, 1, 1296), F32),
        in_specs=[VMEM] * 3,
        out_specs=VMEM,
        scratch_shapes=[pltpu.VMEM((24, WINDOW), F32)],
        compiler_params=SMALL,
    )(ladder, scale, cycle)


def solution(mesh):
    fine = Mesh(mesh.devices.reshape(4, 4, 4, 2), AXES)
    rows, cols = ("x", "z"), ("y", "core")
    return jax.shard_map(
        on_device,
        mesh=fine,
        in_specs=(P(rows, None, cols, None), P(cols, rows, None), P(rows, cols, None), P(), P(), P(), P()),
        out_specs=P(rows, None, cols, None),
        check_vma=False,
    )
```

```python
import jax
import jax.numpy as jnp
from jax import lax
from jax.experimental import pallas as pl
from jax.experimental.pallas import tpu as pltpu
from jax.sharding import Mesh, PartitionSpec as P

AXES = ("x", "z", "y", "core")
SHIFTS = ((1, 1), (-1, -1), (2, 2))
STEPS = (0, 1, -1, 2)
LANES = 128
TILES = 11
WINDOW = TILES * LANES
SPAN = 21
DEPTH = SPAN * LANES
MAIN = 8 * TILES
SHARD = 104
PMAIN = 8 * SPAN
PAIR = 192
QUAD = 2 * PAIR
PSLOT = 88
PROWS = SPAN * PSLOT
F32 = jnp.float32
BF16 = jnp.bfloat16
ANY = pl.BlockSpec(memory_space=pl.ANY)
HBM = pl.BlockSpec(memory_space=pltpu.HBM)
VMEM = pl.BlockSpec(memory_space=pltpu.VMEM)
HUGE = pltpu.CompilerParams(vmem_limit_bytes=56 * 1024 * 1024)
SMALL = pltpu.CompilerParams(vmem_limit_bytes=8 * 1024 * 1024)
LARGE = pltpu.CompilerParams(vmem_limit_bytes=28 * 1024 * 1024)


def ring(value, axes, steps):
    pairs = []
    for x in range(4):
        for z in range(4):
            for y in range(4):
                for core in range(2):
                    here = {"x": x, "z": z, "y": y, "core": core}
                    there = dict(here)
                    there[axes[core]] = (there[axes[core]] + steps[core]) % 4
                    pairs.append(
                        tuple(((p["x"] * 4 + p["z"]) * 4 + p["y"]) * 2 + p["core"] for p in (here, there))
                    )
    return lax.ppermute(value, AXES, pairs)


def swap_core(value):
    return lax.ppermute(value, "core", [(0, 1), (1, 0)])


def places():
    return tuple(lax.axis_index(name) for name in AXES)


def lane_orbitals(shape):
    lane = lax.broadcasted_iota(jnp.int32, shape, 1)
    a = jnp.floor((lane.astype(F32) + 0.5) * (1.0 / 36.0)).astype(jnp.int32)
    return a, lane - 36 * a


def window_copies(integrals, ref, first, sems, base):
    copies = []
    for t in range(SPAN):
        start = pl.multiple_of((base + t) * LANES, LANES)
        copies.append(
            pltpu.make_async_copy(integrals.at[:, :, pl.ds(start, LANES)], ref.at[first + t, 0:81], sems.at[t])
        )
    return copies


def open_step(occ_ref, vir_ref, amp_ref, integrals, keep_out, send_out, first_out, second_out, home_out,
              wide, amp, occ, vir, keep, send, first_v, second_v, home, sems, cut_sems, out_sems):
    x, z, y, core = places()
    copies = [
        pltpu.make_async_copy(source, target, sems.at[at])
        for at, (source, target) in enumerate(((occ_ref, occ), (vir_ref, vir), (amp_ref, amp)))
    ]
    groups = [
        window_copies(integrals, first_v, 0, cut_sems.at[0], ((y + 1 + 2 * core) & 3) * 20),
        window_copies(integrals, second_v, 0, cut_sems.at[1], ((y + 3 - 2 * core) & 3) * 20),
        window_copies(integrals, home, 0, cut_sems.at[2], y * 20),
        window_copies(integrals, home, SPAN, cut_sems.at[3], ((y + 2) & 3) * 20),
    ]
    outs = [
        pltpu.make_async_copy(source, target, out_sems.at[at])
        for at, (source, target) in enumerate(
            (
                (first_v, first_out),
                (second_v, second_out),
                (home.at[0:SPAN], home_out.at[0:SPAN]),
                (home.at[SPAN : 2 * SPAN], home_out.at[SPAN : 2 * SPAN]),
                (keep, keep_out),
                (send, send_out),
            )
        )
    ]
    for copy in copies:
        copy.start()
    for group in groups:
        for copy in group:
            copy.start()
    wide[...] = jnp.zeros_like(wide)
    for copy in copies:
        copy.wait()
    for row in range(18):
        wide[row : row + 1, 0:1296] = amp[row // 6, row % 6]
    row_place = x * 4 + z
    occ_here = occ[row_place >> 1]
    first = 3 * (row_place & 1)
    irrep = 2 * y + core
    vir_here = vir[irrep]
    a, b = lane_orbitals(wide.shape)
    row = lax.broadcasted_iota(jnp.int32, wide.shape, 0)
    i_low = (row * 43) >> 8
    j = row - 6 * i_low
    live = (a < vir_here) & (b < vir_here) & (i_low + first < occ_here) & (j < occ_here)
    moved = pltpu.roll(jnp.where(live, wide[...], 0.0), 16 * irrep, 1)

    def write(ref, half):
        for t in range(TILES):
            columns = slice(t * LANES, (t + 1) * LANES)
            ref[8 * t : 8 * t + 8, :] = moved[8 * half : 8 * half + 8, columns]
            ref[MAIN + t : MAIN + t + 1, :] = moved[16 + half : 17 + half, columns]
        ref[MAIN + TILES : SHARD, :] = jnp.zeros((SHARD - MAIN - TILES, LANES), F32)

    @pl.when(core == 0)
    def _():
        write(keep, 0)
        write(send, 1)

    @pl.when(core == 1)
    def _():
        write(keep, 1)
        write(send, 0)

    for copy in outs[4:]:
        copy.start()
    for group, out in zip(groups, outs):
        for copy in group:
            copy.wait()
        out.start()
    for copy in outs:
        copy.wait()


def merge_irreps(even, odd, out, at):
    gap = SPAN - TILES
    out[at : at + 8 * gap, :] = even[0 : 8 * gap, :]
    out[at + 8 * gap : at + MAIN, :] = even[8 * gap : MAIN, :] + odd[0:8, :]
    out[at + MAIN : at + PMAIN, :] = odd[8:MAIN, :]
    extra = at + PMAIN
    out[extra : extra + gap, :] = even[MAIN : MAIN + gap, :]
    out[extra + gap : extra + TILES, :] = even[MAIN + gap : MAIN + TILES, :] + odd[MAIN : MAIN + 1, :]
    out[extra + TILES : extra + SPAN, :] = odd[MAIN + 1 : MAIN + TILES, :]
    out[extra + SPAN : at + PAIR, :] = jnp.zeros((PAIR - PMAIN - SPAN, LANES), F32)


def merge_pair(keep, got, home, out, home_out):
    core = lax.axis_index("core")

    @pl.when(core == 0)
    def _():
        merge_irreps(keep, got, out, 0)

    @pl.when(core == 1)
    def _():
        merge_irreps(got, keep, out, 0)


def join_pairs(near, far, home_other, out):
    out[0:PAIR, :] = near[...]
    out[PAIR:QUAD, :] = far[...]


def gather_four(b0, b1, b2, b3, near, far):
    for at, block in enumerate((b0, b1, b2, b3)):
        near[at * PAIR : (at + 1) * PAIR, :] = block[0:PAIR, :]
        far[at * PAIR : (at + 1) * PAIR, :] = block[PAIR:QUAD, :]


def nothing(*refs):
    pass


def hold(values, *witnesses):
    kept = range(len(values))
    return pl.pallas_call(
        nothing,
        out_shape=[jax.ShapeDtypeStruct(value.shape, value.dtype) for value in values],
        in_specs=[ANY] * (len(values) + len(witnesses)),
        out_specs=[ANY] * len(values),
        input_output_aliases={at: at for at in kept},
        compiler_params=SMALL,
    )(*values, *witnesses)


def left_side(blocks, extra):
    for t in range(SPAN):
        for d, block in enumerate(blocks):
            extra[4 * d : 4 * d + 4, t * LANES : (t + 1) * LANES] = block[pl.ds(PMAIN + t, 4, stride=PAIR), :]
    rows = []
    for block in blocks:
        for e in range(4):
            rows.append(
                jnp.concatenate(
                    [block[e * PAIR + 8 * t : e * PAIR + 8 * t + 8, :] for t in range(SPAN)], axis=1
                )
            )
    return split(jnp.concatenate(rows + [extra[...]], axis=0))


def split(value):
    high = value.astype(BF16)
    return high, (value - high.astype(F32)).astype(BF16)


def tiles_side(ref, first):
    return jnp.concatenate(
        [ref[(first + t) * PSLOT : (first + t + 1) * PSLOT, :] for t in range(SPAN)], axis=1
    )


def last_by_last(p, q):
    return lax.dot_general(p, q, (((1,), (1,)), ((), ())), preferred_element_type=F32)


def split_home(home, home_other, witness, near_high, near_low, far_high, far_low):
    for side, ref in enumerate((home, home_other)):
        high, low = split(tiles_side(ref, 0))
        rows = slice(side * PSLOT, (side + 1) * PSLOT)
        near_high[rows, :] = high
        near_low[rows, :] = low
        high, low = split(tiles_side(ref, SPAN))
        pad = jnp.zeros((LANES - PSLOT, DEPTH), BF16)
        rows = slice(side * LANES, (side + 1) * LANES)
        far_high[rows, :] = jnp.concatenate([high, pad], axis=0)
        far_low[rows, :] = jnp.concatenate([low, pad], axis=0)


def multiply_near(b0, b1, b2, b3, near_high, near_low, below, below_other, above, above_other,
                  here_sum, below_sum, above_sum, extra, turned):
    high, low = left_side((b0, b1, b2, b3), extra)
    sides = [tiles_side(ref, 0) for ref in (below, below_other, above, above_other)]
    v_high, v_low = split(jnp.concatenate(sides, axis=0))
    v_high = jnp.concatenate([near_high[...], v_high], axis=0)
    v_low = jnp.concatenate([near_low[...], v_low], axis=0)
    total = last_by_last(v_high, high) + (last_by_last(v_low, high) + last_by_last(v_high, low))
    turned[...] = jnp.zeros_like(turned)
    for at, ref in enumerate((here_sum, below_sum, above_sum)):
        for side in range(2):
            rows = slice((2 * at + side) * PSLOT, (2 * at + side + 1) * PSLOT)
            turned[0:PSLOT, 0:144] = total[rows, :]
            ref[:, side * LANES : (side + 1) * LANES] = turned[...].T[0:144, :]


def multiply_far(b0, b1, b2, b3, v_high, v_low, here_sum, back_a, back_b, out, extra):
    x, z, y, core = places()
    high, low = left_side((b0, b1, b2, b3), extra)
    partial = here_sum[...] + back_a[...] + back_b[...]
    row = lax.broadcasted_iota(jnp.int32, (8, LANES), 0)
    lane = lax.broadcasted_iota(jnp.int32, (8, LANES), 1)
    total = partial + (
        last_by_last(high, v_high[...]) + (last_by_last(low, v_high[...]) + last_by_last(high, v_low[...]))
    )
    for side in range(2):
        columns = slice(side * LANES, (side + 1) * LANES)
        last = total[128:144, columns]
        last_a = pltpu.roll(last, 81, 1)
        last_b = pltpu.roll(last, 34, 1)
        core_there = core if side == 0 else 1 - core
        for d in range(4):
            for e in range(4):
                s = 4 * d + e
                x_step = jnp.where(core == 0, STEPS[e], STEPS[d])
                z_step = jnp.where(core == 0, STEPS[d], STEPS[e])
                there = ((x - x_step) & 3) * 4 + ((z - z_step) & 3)
                main = total[8 * s : 8 * s + 8, columns]
                tail = jnp.where(row == 0, last_a[s : s + 1, :], last_b[s : s + 1, :])
                out[there * 2 + core_there] = jnp.where(lane < 81, main, tail)


def local_step(occ_ref, vir_ref, eps_occ_ref, eps_vir_ref, amp_ref, ovov, partner,
               scale, cycle, amp, occ, vir, eps_occ, eps_vir, left_a, left_b, panel_a, panel_b, sems):
    x, z, y, core = places()
    copies = [
        pltpu.make_async_copy(source, target, sems.at[at])
        for at, (source, target) in enumerate(
            ((occ_ref, occ), (vir_ref, vir), (eps_occ_ref, eps_occ), (eps_vir_ref, eps_vir), (amp_ref, amp))
        )
    ]
    for copy in copies:
        copy.start()
    panel_a[...] = jnp.zeros_like(panel_a)
    panel_b[...] = jnp.zeros_like(panel_b)
    left_a[...] = jnp.zeros_like(left_a)
    left_b[...] = jnp.zeros_like(left_b)
    lower = (z & 1) == 0
    for r in range(108):
        own, other = ovov[r], partner[r]
        panel_a[r : r + 1, 0:216] = jnp.where(lower, own, other)
        panel_b[r : r + 1, 0:216] = jnp.where(lower, other, own)
    for copy in copies:
        copy.wait()
    row_place = x * 4 + z
    shell = row_place >> 1
    first = 3 * (row_place & 1)
    irrep = 2 * y + core
    a, b = lane_orbitals((1, 1296))
    energy_a = jnp.zeros((1, 1296), F32)
    energy_b = jnp.zeros((1, 1296), F32)
    for slot in range(36):
        value = eps_vir[irrep, slot]
        energy_a = jnp.where(a == slot, value, energy_a)
        energy_b = jnp.where(b == slot, value, energy_b)
    lane_live = (a < vir[irrep]) & (b < vir[irrep])
    occ_here = occ[shell]
    for r in range(18):
        low, k = r // 6, r % 6
        i = first + low
        here = lane_live & (i < occ_here) & (k < occ_here)
        gap = eps_occ[shell, i] + eps_occ[shell, k] - energy_a - energy_b
        scale[r : r + 1, :] = jnp.where(here, 1.0, 0.0) / gap
        live = jnp.where(here, amp[low, k], 0.0)
        left, column = (left_a, 36 * k) if k < 3 else (left_b, 36 * (k - 3))
        for slot in range(36):
            left[36 * low + slot : 36 * low + slot + 1, column : column + 36] = live[
                :, 36 * slot : 36 * slot + 36
            ]
    dot = lambda p, q: jnp.dot(p, q, preferred_element_type=F32)
    total = None
    for left, panel in ((left_a, panel_a), (left_b, panel_b)):
        p_high, p_low = split(left[:, 0:112])
        q_high, q_low = split(panel[...])
        part = dot(p_high, q_high) + (dot(p_low, q_high) + dot(p_high, q_low))
        total = part if total is None else total + part
    for low in range(3):
        for j in range(6):
            r = 6 * low + j
            for slot in range(36):
                cycle[r : r + 1, 36 * slot : 36 * slot + 36] = total[
                    36 * low + slot : 36 * low + slot + 1, 36 * j : 36 * j + 36
                ]


def finish(sums, scale, cycle, out, wide):
    wide[...] = jnp.zeros_like(wide)
    lane8 = lax.broadcasted_iota(jnp.int32, (1, LANES), 1)
    lane = lax.broadcasted_iota(jnp.int32, (24, LANES), 1)
    for r in range(16):
        mains, lasts = [], []
        for core in range(2):
            block = sums[2 * r + core]
            mains.append(block)
            lasts.append(
                jnp.where(lane8 < 47, pltpu.roll(block, 47, 1)[0:1, :], pltpu.roll(block, 94, 1)[1:2, :])
            )
        stack = jnp.concatenate(mains + lasts + [jnp.zeros((6, LANES), F32)], axis=0)
        tile, start = divmod(81 * r, LANES)
        turned = pltpu.roll(stack, start, 1) if start else stack
        here = slice(tile * LANES, (tile + 1) * LANES)
        wide[:, here] = jnp.where((lane >= start) & (lane < start + 81), turned, wide[:, here])
        if start + 81 > LANES:
            after = slice((tile + 1) * LANES, (tile + 2) * LANES)
            wide[:, after] = jnp.where(lane < start + 81 - LANES, turned, wide[:, after])
    total = (wide[0:18, 0:1296] + cycle[...]) * scale[...]
    for r in range(18):
        out[r // 6, r % 6] = total[r : r + 1, :]


def on_device(amplitudes, vvvv, ovov, eps_occ, eps_vir, occ_count, vir_count):
    x, z, y, core = places()
    shape = jax.ShapeDtypeStruct
    integrals = vvvv.reshape(81, 1, 10368)
    window = shape((SPAN, PSLOT, 1, LANES), F32)
    flat = lambda value: value.reshape(PROWS, LANES)
    keep, send, first_v, second_v, home = pl.pallas_call(
        open_step,
        out_shape=[shape((SHARD, LANES), F32)] * 2 + [window] * 2
        + [shape((2 * SPAN, PSLOT, 1, LANES), F32)],
        in_specs=[HBM] * 4,
        out_specs=[ANY] * 5,
        scratch_shapes=[
            pltpu.VMEM((24, WINDOW), F32),
            pltpu.VMEM((3, 6, 1, 1296), F32),
            pltpu.SMEM((8,), jnp.int32),
            pltpu.SMEM((8,), jnp.int32),
            pltpu.VMEM((SHARD, LANES), F32),
            pltpu.VMEM((SHARD, LANES), F32),
            pltpu.VMEM((SPAN, PSLOT, 1, LANES), F32),
            pltpu.VMEM((SPAN, PSLOT, 1, LANES), F32),
            pltpu.VMEM((2 * SPAN, PSLOT, 1, LANES), F32),
            pltpu.SemaphoreType.DMA((3,)),
            pltpu.SemaphoreType.DMA((4, SPAN)),
            pltpu.SemaphoreType.DMA((6,)),
        ],
        compiler_params=HUGE,
    )(occ_count, vir_count, amplitudes, integrals)
    got = swap_core(send)
    moved_a = ring(flat(first_v), "yy", (1, -1))
    partner = lax.ppermute(ovov, "z", [(0, 1), (1, 0), (2, 3), (3, 2)])
    home = home.reshape(2 * PROWS, LANES)
    pair, home = pl.pallas_call(
        merge_pair,
        out_shape=[shape((PAIR, LANES), F32), shape(home.shape, F32)],
        in_specs=[VMEM] * 2 + [ANY],
        out_specs=[VMEM, ANY],
        input_output_aliases={2: 1},
        compiler_params=SMALL,
    )(keep, got, home)
    home_other = swap_core(home)
    far_pair = ring(pair, "yy", (2, 2))
    quad = pl.pallas_call(
        join_pairs,
        out_shape=shape((QUAD, LANES), F32),
        in_specs=[VMEM] * 2 + [ANY],
        out_specs=VMEM,
        compiler_params=SMALL,
    )(pair, far_pair, home_other)
    (second_v,) = hold([flat(second_v)], far_pair)
    moved_b = ring(second_v, "yy", (-1, 1))

    near, far = pl.pallas_call(
        gather_four,
        out_shape=[shape((4 * PAIR, LANES), F32)] * 2,
        in_specs=[VMEM] * 4,
        out_specs=[VMEM] * 2,
        compiler_params=SMALL,
    )(quad, *[ring(quad, "xz", step) for step in SHIFTS])
    near_high, near_low, far_high, far_low = pl.pallas_call(
        split_home,
        out_shape=[shape((2 * PSLOT, DEPTH), BF16)] * 2 + [shape((2 * LANES, DEPTH), BF16)] * 2,
        in_specs=[VMEM] * 2 + [ANY],
        out_specs=[VMEM] * 4,
        compiler_params=LARGE,
        cost_estimate=pl.CostEstimate(flops=1, bytes_accessed=1, transcendentals=0),
    )(home, home_other, near)
    near_blocks = [near] + [ring(near, "zx", step) for step in SHIFTS]
    far_blocks = [far] + [ring(far, "zx", step) for step in SHIFTS]

    moved_a, moved_b = hold([moved_a, moved_b], *near_blocks[1:], near_high, partner)
    swapped_a, swapped_b = swap_core(moved_a), swap_core(moved_b)

    scale, cycle = pl.pallas_call(
        local_step,
        out_shape=[shape((18, 1296), F32)] * 2,
        in_specs=[HBM] * 5 + [VMEM] * 2,
        out_specs=[VMEM] * 2,
        scratch_shapes=[
            pltpu.VMEM((3, 6, 1, 1296), F32),
            pltpu.SMEM((8,), jnp.int32),
            pltpu.SMEM((8,), jnp.int32),
            pltpu.SMEM((8, 6), F32),
            pltpu.SMEM((8, 36), F32),
            pltpu.VMEM((112, 256), F32),
            pltpu.VMEM((112, 256), F32),
            pltpu.VMEM((112, 256), F32),
            pltpu.VMEM((112, 256), F32),
            pltpu.SemaphoreType.DMA((5,)),
        ],
        compiler_params=SMALL,
        cost_estimate=pl.CostEstimate(flops=100000000, bytes_accessed=1000000, transcendentals=0),
    )(occ_count, vir_count, eps_occ, eps_vir, amplitudes, ovov, partner)

    sums = [shape((144, 2 * LANES), F32)] * 3
    here_sum, below_sum, above_sum = pl.pallas_call(
        multiply_near,
        out_shape=sums,
        in_specs=[VMEM] * 10,
        out_specs=[VMEM] * 3,
        scratch_shapes=[pltpu.VMEM((16, DEPTH), F32), pltpu.VMEM((LANES, 2 * LANES), F32)],
        compiler_params=LARGE,
    )(*near_blocks, near_high, near_low, moved_a, swapped_b, moved_b, swapped_a)
    back_a = ring(below_sum, "yy", (-1, 1))
    back_b = ring(above_sum, "yy", (1, -1))
    packed = pl.pallas_call(
        multiply_far,
        out_shape=shape((32, 8, LANES), F32),
        in_specs=[VMEM] * 9,
        out_specs=VMEM,
        scratch_shapes=[pltpu.VMEM((16, DEPTH), F32)],
        compiler_params=LARGE,
    )(*far_blocks, far_high, far_low, here_sum, back_a, back_b)
    ladder = lax.all_to_all(packed, ("x", "z", "core"), 0, 0, tiled=True)
    return pl.pallas_call(
        finish,
        out_shape=shape((3, 6, 1, 1296), F32),
        in_specs=[VMEM] * 3,
        out_specs=VMEM,
        scratch_shapes=[pltpu.VMEM((24, WINDOW), F32)],
        compiler_params=SMALL,
    )(ladder, scale, cycle)


def solution(mesh):
    fine = Mesh(mesh.devices.reshape(4, 4, 4, 2), AXES)
    rows, cols = ("x", "z"), ("y", "core")
    return jax.shard_map(
        on_device,
        mesh=fine,
        in_specs=(P(rows, None, cols, None), P(cols, rows, None), P(rows, cols, None), P(), P(), P(), P()),
        out_specs=P(rows, None, cols, None),
        check_vma=False,
    )
```

```python
import jax
import jax.numpy as jnp
from jax import lax
from jax.experimental import pallas as pl
from jax.experimental.pallas import tpu as pltpu
from jax.sharding import Mesh, PartitionSpec as P

AXES = ("x", "z", "y", "core")
SHIFTS = ((1, 1), (-1, -1), (2, 2))
STEPS = (0, 1, -1, 2)
LANES = 128
TILES = 11
WINDOW = TILES * LANES
SPAN = 21
DEPTH = SPAN * LANES
MAIN = 8 * TILES
SHARD = 104
PMAIN = 8 * SPAN
PAIR = 192
QUAD = 2 * PAIR
PSLOT = 88
PROWS = SPAN * PSLOT
F32 = jnp.float32
BF16 = jnp.bfloat16
ANY = pl.BlockSpec(memory_space=pl.ANY)
HBM = pl.BlockSpec(memory_space=pltpu.HBM)
VMEM = pl.BlockSpec(memory_space=pltpu.VMEM)
HUGE = pltpu.CompilerParams(vmem_limit_bytes=56 * 1024 * 1024)
TIGHT = pltpu.CompilerParams(vmem_limit_bytes=(65536 - 900) * 1024)
SMALL = pltpu.CompilerParams(vmem_limit_bytes=8 * 1024 * 1024)
LARGE = pltpu.CompilerParams(vmem_limit_bytes=28 * 1024 * 1024)


def ring(value, axes, steps):
    pairs = []
    for x in range(4):
        for z in range(4):
            for y in range(4):
                for core in range(2):
                    here = {"x": x, "z": z, "y": y, "core": core}
                    there = dict(here)
                    there[axes[core]] = (there[axes[core]] + steps[core]) % 4
                    pairs.append(
                        tuple(((p["x"] * 4 + p["z"]) * 4 + p["y"]) * 2 + p["core"] for p in (here, there))
                    )
    return lax.ppermute(value, AXES, pairs)


def swap_core(value):
    return lax.ppermute(value, "core", [(0, 1), (1, 0)])


def places():
    return tuple(lax.axis_index(name) for name in AXES)


def lane_orbitals(shape):
    lane = lax.broadcasted_iota(jnp.int32, shape, 1)
    a = jnp.floor((lane.astype(F32) + 0.5) * (1.0 / 36.0)).astype(jnp.int32)
    return a, lane - 36 * a


def window_copies(integrals, ref, sems, base):
    copies = []
    for t in range(SPAN):
        start = pl.multiple_of((base + t) * LANES, LANES)
        copies.append(
            pltpu.make_async_copy(integrals.at[:, :, pl.ds(start, LANES)], ref.at[t, 0:81], sems.at[t])
        )
    return copies


def cut_step(integrals, witness, second_out, home_out, second_v, home, cut_sems, home_sems, out_sems):
    y, core = lax.axis_index("y"), lax.axis_index("core")
    cuts = window_copies(integrals, second_v, cut_sems, ((y + 3 - 2 * core) & 3) * 20)
    homes = []
    for at in range(2):
        start = pl.multiple_of(((y + 2 * at) & 3) * 2560, LANES)
        homes.append(
            pltpu.make_async_copy(
                integrals.at[:, :, pl.ds(start, DEPTH)], home.at[at, 0:81], home_sems.at[at]
            )
        )
    for copy in cuts + homes:
        copy.start()
    outs = [pltpu.make_async_copy(second_v, second_out, out_sems.at[0])]
    outs += [pltpu.make_async_copy(home.at[at], home_out.at[at], out_sems.at[1 + at]) for at in range(2)]
    for copy in cuts:
        copy.wait()
    outs[0].start()
    for copy, out in zip(homes, outs[1:]):
        copy.wait()
        out.start()
    for out in outs:
        out.wait()


def open_step(occ_ref, vir_ref, amp_ref, integrals, keep_out, send_out, first_out,
              wide, amp, occ, vir, keep, send, first_v, sems, cut_sems, out_sems):
    x, z, y, core = places()
    copies = [
        pltpu.make_async_copy(source, target, sems.at[at])
        for at, (source, target) in enumerate(((occ_ref, occ), (vir_ref, vir), (amp_ref, amp)))
    ]
    cuts = window_copies(integrals, first_v, cut_sems, ((y + 1 + 2 * core) & 3) * 20)
    outs = [
        pltpu.make_async_copy(source, target, out_sems.at[at])
        for at, (source, target) in enumerate(((keep, keep_out), (send, send_out), (first_v, first_out)))
    ]
    for copy in copies + cuts:
        copy.start()
    wide[...] = jnp.zeros_like(wide)
    for copy in copies:
        copy.wait()
    for row in range(18):
        wide[row : row + 1, 0:1296] = amp[row // 6, row % 6]
    row_place = x * 4 + z
    occ_here = occ[row_place >> 1]
    first = 3 * (row_place & 1)
    irrep = 2 * y + core
    vir_here = vir[irrep]
    a, b = lane_orbitals(wide.shape)
    row = lax.broadcasted_iota(jnp.int32, wide.shape, 0)
    i_low = (row * 43) >> 8
    j = row - 6 * i_low
    live = (a < vir_here) & (b < vir_here) & (i_low + first < occ_here) & (j < occ_here)
    moved = pltpu.roll(jnp.where(live, wide[...], 0.0), 16 * irrep, 1)

    def write(ref, half):
        for t in range(TILES):
            columns = slice(t * LANES, (t + 1) * LANES)
            ref[8 * t : 8 * t + 8, :] = moved[8 * half : 8 * half + 8, columns]
            ref[MAIN + t : MAIN + t + 1, :] = moved[16 + half : 17 + half, columns]
        ref[MAIN + TILES : SHARD, :] = jnp.zeros((SHARD - MAIN - TILES, LANES), F32)

    @pl.when(core == 0)
    def _():
        write(keep, 0)
        write(send, 1)

    @pl.when(core == 1)
    def _():
        write(keep, 1)
        write(send, 0)

    for copy in outs[:2]:
        copy.start()
    for copy in cuts:
        copy.wait()
    outs[2].start()
    for copy in outs:
        copy.wait()


def merge_irreps(even, odd, out, at):
    gap = SPAN - TILES
    out[at : at + 8 * gap, :] = even[0 : 8 * gap, :]
    out[at + 8 * gap : at + MAIN, :] = even[8 * gap : MAIN, :] + odd[0:8, :]
    out[at + MAIN : at + PMAIN, :] = odd[8:MAIN, :]
    extra = at + PMAIN
    out[extra : extra + gap, :] = even[MAIN : MAIN + gap, :]
    out[extra + gap : extra + TILES, :] = even[MAIN + gap : MAIN + TILES, :] + odd[MAIN : MAIN + 1, :]
    out[extra + TILES : extra + SPAN, :] = odd[MAIN + 1 : MAIN + TILES, :]
    out[extra + SPAN : at + PAIR, :] = jnp.zeros((PAIR - PMAIN - SPAN, LANES), F32)


def merge_pair(keep, got, out):
    core = lax.axis_index("core")

    @pl.when(core == 0)
    def _():
        merge_irreps(keep, got, out, 0)

    @pl.when(core == 1)
    def _():
        merge_irreps(got, keep, out, 0)


def join_pairs(near, far, out):
    out[0:PAIR, :] = near[...]
    out[PAIR:QUAD, :] = far[...]


def gather_four(b0, b1, b2, b3, witness, near, far):
    for at, block in enumerate((b0, b1, b2, b3)):
        near[at * PAIR : (at + 1) * PAIR, :] = block[0:PAIR, :]
        far[at * PAIR : (at + 1) * PAIR, :] = block[PAIR:QUAD, :]


def nothing(*refs):
    pass


def hold(values, *witnesses, params=SMALL):
    kept = range(len(values))
    return pl.pallas_call(
        nothing,
        out_shape=[jax.ShapeDtypeStruct(value.shape, value.dtype) for value in values],
        in_specs=[ANY] * (len(values) + len(witnesses)),
        out_specs=[ANY] * len(values),
        input_output_aliases={at: at for at in kept},
        compiler_params=params,
    )(*values, *witnesses)


def left_side(blocks, extra):
    for t in range(SPAN):
        for d, block in enumerate(blocks):
            extra[4 * d : 4 * d + 4, t * LANES : (t + 1) * LANES] = block[pl.ds(PMAIN + t, 4, stride=PAIR), :]
    rows = []
    for block in blocks:
        for e in range(4):
            rows.append(
                jnp.concatenate(
                    [block[e * PAIR + 8 * t : e * PAIR + 8 * t + 8, :] for t in range(SPAN)], axis=1
                )
            )
    return split(jnp.concatenate(rows + [extra[...]], axis=0))


def split(value):
    high = value.astype(BF16)
    return high, (value - high.astype(F32)).astype(BF16)


def tiles_side(ref, first):
    return jnp.concatenate(
        [ref[(first + t) * PSLOT : (first + t + 1) * PSLOT, :] for t in range(SPAN)], axis=1
    )


def rows_side(ref, first):
    return jnp.concatenate([ref[pl.ds(first + t, PSLOT, stride=SPAN), :] for t in range(SPAN)], axis=1)


def last_by_last(p, q):
    return lax.dot_general(p, q, (((1,), (1,)), ((), ())), preferred_element_type=F32)


def split_home(home, home_other, witness, near_high, near_low, far_high, far_low):
    for side, ref in enumerate((home, home_other)):
        high, low = split(rows_side(ref, 0))
        rows = slice(side * PSLOT, (side + 1) * PSLOT)
        near_high[rows, :] = high
        near_low[rows, :] = low
        high, low = split(rows_side(ref, PROWS))
        pad = jnp.zeros((LANES - PSLOT, DEPTH), BF16)
        rows = slice(side * LANES, (side + 1) * LANES)
        far_high[rows, :] = jnp.concatenate([high, pad], axis=0)
        far_low[rows, :] = jnp.concatenate([low, pad], axis=0)


def multiply_near(b0, b1, b2, b3, near_high, near_low, below, below_other, above, above_other,
                  here_sum, below_sum, above_sum, extra, turned):
    high, low = left_side((b0, b1, b2, b3), extra)
    sides = [tiles_side(ref, 0) for ref in (below, below_other, above, above_other)]
    v_high, v_low = split(jnp.concatenate(sides, axis=0))
    v_high = jnp.concatenate([near_high[...], v_high], axis=0)
    v_low = jnp.concatenate([near_low[...], v_low], axis=0)
    total = last_by_last(v_high, high) + (last_by_last(v_low, high) + last_by_last(v_high, low))
    turned[...] = jnp.zeros_like(turned)
    for at, ref in enumerate((here_sum, below_sum, above_sum)):
        for side in range(2):
            rows = slice((2 * at + side) * PSLOT, (2 * at + side + 1) * PSLOT)
            turned[0:PSLOT, 0:144] = total[rows, :]
            ref[:, side * LANES : (side + 1) * LANES] = turned[...].T[0:144, :]


def multiply_far(b0, b1, b2, b3, v_high, v_low, here_sum, back_a, back_b, out, extra):
    x, z, y, core = places()
    high, low = left_side((b0, b1, b2, b3), extra)
    partial = here_sum[...] + back_a[...] + back_b[...]
    row = lax.broadcasted_iota(jnp.int32, (8, LANES), 0)
    lane = lax.broadcasted_iota(jnp.int32, (8, LANES), 1)
    total = partial + (
        last_by_last(high, v_high[...]) + (last_by_last(low, v_high[...]) + last_by_last(high, v_low[...]))
    )
    for side in range(2):
        columns = slice(side * LANES, (side + 1) * LANES)
        last = total[128:144, columns]
        last_a = pltpu.roll(last, 81, 1)
        last_b = pltpu.roll(last, 34, 1)
        core_there = core if side == 0 else 1 - core
        for d in range(4):
            for e in range(4):
                s = 4 * d + e
                x_step = jnp.where(core == 0, STEPS[e], STEPS[d])
                z_step = jnp.where(core == 0, STEPS[d], STEPS[e])
                there = ((x - x_step) & 3) * 4 + ((z - z_step) & 3)
                main = total[8 * s : 8 * s + 8, columns]
                tail = jnp.where(row == 0, last_a[s : s + 1, :], last_b[s : s + 1, :])
                out[there * 2 + core_there] = jnp.where(lane < 81, main, tail)


def local_step(occ_ref, vir_ref, eps_occ_ref, eps_vir_ref, amp_ref, ovov, partner,
               scale, cycle, amp, occ, vir, eps_occ, eps_vir, left_a, left_b, panel_a, panel_b, sems):
    x, z, y, core = places()
    copies = [
        pltpu.make_async_copy(source, target, sems.at[at])
        for at, (source, target) in enumerate(
            ((occ_ref, occ), (vir_ref, vir), (eps_occ_ref, eps_occ), (eps_vir_ref, eps_vir), (amp_ref, amp))
        )
    ]
    for copy in copies:
        copy.start()
    panel_a[...] = jnp.zeros_like(panel_a)
    panel_b[...] = jnp.zeros_like(panel_b)
    left_a[...] = jnp.zeros_like(left_a)
    left_b[...] = jnp.zeros_like(left_b)
    lower = (z & 1) == 0
    for r in range(108):
        own, other = ovov[r], partner[r]
        panel_a[r : r + 1, 0:216] = jnp.where(lower, own, other)
        panel_b[r : r + 1, 0:216] = jnp.where(lower, other, own)
    for copy in copies:
        copy.wait()
    row_place = x * 4 + z
    shell = row_place >> 1
    first = 3 * (row_place & 1)
    irrep = 2 * y + core
    a, b = lane_orbitals((1, 1296))
    energy_a = jnp.zeros((1, 1296), F32)
    energy_b = jnp.zeros((1, 1296), F32)
    for slot in range(36):
        value = eps_vir[irrep, slot]
        energy_a = jnp.where(a == slot, value, energy_a)
        energy_b = jnp.where(b == slot, value, energy_b)
    lane_live = (a < vir[irrep]) & (b < vir[irrep])
    occ_here = occ[shell]
    for r in range(18):
        low, k = r // 6, r % 6
        i = first + low
        here = lane_live & (i < occ_here) & (k < occ_here)
        gap = eps_occ[shell, i] + eps_occ[shell, k] - energy_a - energy_b
        scale[r : r + 1, :] = jnp.where(here, 1.0, 0.0) / gap
        live = jnp.where(here, amp[low, k], 0.0)
        left, column = (left_a, 36 * k) if k < 3 else (left_b, 36 * (k - 3))
        for slot in range(36):
            left[36 * low + slot : 36 * low + slot + 1, column : column + 36] = live[
                :, 36 * slot : 36 * slot + 36
            ]
    dot = lambda p, q: jnp.dot(p, q, preferred_element_type=F32)
    total = None
    for left, panel in ((left_a, panel_a), (left_b, panel_b)):
        p_high, p_low = split(left[:, 0:112])
        q_high, q_low = split(panel[...])
        part = dot(p_high, q_high) + (dot(p_low, q_high) + dot(p_high, q_low))
        total = part if total is None else total + part
    for low in range(3):
        for j in range(6):
            r = 6 * low + j
            for slot in range(36):
                cycle[r : r + 1, 36 * slot : 36 * slot + 36] = total[
                    36 * low + slot : 36 * low + slot + 1, 36 * j : 36 * j + 36
                ]


def finish(sums, scale, cycle, out, wide):
    wide[...] = jnp.zeros_like(wide)
    lane8 = lax.broadcasted_iota(jnp.int32, (1, LANES), 1)
    lane = lax.broadcasted_iota(jnp.int32, (24, LANES), 1)
    for r in range(16):
        mains, lasts = [], []
        for core in range(2):
            block = sums[2 * r + core]
            mains.append(block)
            lasts.append(
                jnp.where(lane8 < 47, pltpu.roll(block, 47, 1)[0:1, :], pltpu.roll(block, 94, 1)[1:2, :])
            )
        stack = jnp.concatenate(mains + lasts + [jnp.zeros((6, LANES), F32)], axis=0)
        tile, start = divmod(81 * r, LANES)
        turned = pltpu.roll(stack, start, 1) if start else stack
        here = slice(tile * LANES, (tile + 1) * LANES)
        wide[:, here] = jnp.where((lane >= start) & (lane < start + 81), turned, wide[:, here])
        if start + 81 > LANES:
            after = slice((tile + 1) * LANES, (tile + 2) * LANES)
            wide[:, after] = jnp.where(lane < start + 81 - LANES, turned, wide[:, after])
    total = (wide[0:18, 0:1296] + cycle[...]) * scale[...]
    for r in range(18):
        out[r // 6, r % 6] = total[r : r + 1, :]


def on_device(amplitudes, vvvv, ovov, eps_occ, eps_vir, occ_count, vir_count):
    x, z, y, core = places()
    shape = jax.ShapeDtypeStruct
    integrals = vvvv.reshape(81, 1, 10368)
    window = shape((SPAN, PSLOT, 1, LANES), F32)
    flat = lambda value: value.reshape(PROWS, LANES)
    keep, send, first_v = pl.pallas_call(
        open_step,
        out_shape=[shape((SHARD, LANES), F32)] * 2 + [window],
        in_specs=[HBM] * 4,
        out_specs=[ANY] * 3,
        scratch_shapes=[
            pltpu.VMEM((24, WINDOW), F32),
            pltpu.VMEM((3, 6, 1, 1296), F32),
            pltpu.SMEM((8,), jnp.int32),
            pltpu.SMEM((8,), jnp.int32),
            pltpu.VMEM((SHARD, LANES), F32),
            pltpu.VMEM((SHARD, LANES), F32),
            pltpu.VMEM((SPAN, PSLOT, 1, LANES), F32),
            pltpu.SemaphoreType.DMA((3,)),
            pltpu.SemaphoreType.DMA((SPAN,)),
            pltpu.SemaphoreType.DMA((3,)),
        ],
        compiler_params=HUGE,
    )(occ_count, vir_count, amplitudes, integrals)
    got = swap_core(send)
    moved_a = ring(flat(first_v), "yy", (1, -1))
    partner = lax.ppermute(ovov, "z", [(0, 1), (1, 0), (2, 3), (3, 2)])
    pair = pl.pallas_call(
        merge_pair,
        out_shape=shape((PAIR, LANES), F32),
        in_specs=[VMEM] * 2,
        out_specs=VMEM,
        compiler_params=SMALL,
    )(keep, got)
    second_v, home = pl.pallas_call(
        cut_step,
        out_shape=[window, shape((2, PSLOT, 1, DEPTH), F32)],
        in_specs=[HBM, ANY],
        out_specs=[ANY] * 2,
        scratch_shapes=[
            pltpu.VMEM((SPAN, PSLOT, 1, LANES), F32),
            pltpu.VMEM((2, PSLOT, 1, DEPTH), F32),
            pltpu.SemaphoreType.DMA((SPAN,)),
            pltpu.SemaphoreType.DMA((2,)),
            pltpu.SemaphoreType.DMA((3,)),
        ],
        compiler_params=TIGHT,
        cost_estimate=pl.CostEstimate(flops=0, bytes_accessed=7000000, transcendentals=0),
    )(integrals, pair)
    home = home.reshape(2 * PROWS, LANES)
    far_pair = ring(pair, "yy", (2, 2))
    quad = pl.pallas_call(
        join_pairs,
        out_shape=shape((QUAD, LANES), F32),
        in_specs=[VMEM] * 2,
        out_specs=VMEM,
        compiler_params=SMALL,
    )(pair, far_pair)
    second_v, home = hold([flat(second_v), home], far_pair, params=TIGHT)
    home_other = swap_core(home)
    moved_b = ring(second_v, "yy", (-1, 1))

    near, far = pl.pallas_call(
        gather_four,
        out_shape=[shape((4 * PAIR, LANES), F32)] * 2,
        in_specs=[VMEM] * 4 + [ANY],
        out_specs=[VMEM] * 2,
        compiler_params=SMALL,
    )(quad, *[ring(quad, "xz", step) for step in SHIFTS], home_other)
    near_high, near_low, far_high, far_low = pl.pallas_call(
        split_home,
        out_shape=[shape((2 * PSLOT, DEPTH), BF16)] * 2 + [shape((2 * LANES, DEPTH), BF16)] * 2,
        in_specs=[VMEM] * 2 + [ANY],
        out_specs=[VMEM] * 4,
        compiler_params=LARGE,
        cost_estimate=pl.CostEstimate(flops=1, bytes_accessed=1, transcendentals=0),
    )(home, home_other, near)
    near_blocks = [near] + [ring(near, "zx", step) for step in SHIFTS]
    far_blocks = [far] + [ring(far, "zx", step) for step in SHIFTS]

    moved_a, moved_b = hold([moved_a, moved_b], *near_blocks[1:], near_high, partner)
    swapped_a, swapped_b = swap_core(moved_a), swap_core(moved_b)

    scale, cycle = pl.pallas_call(
        local_step,
        out_shape=[shape((18, 1296), F32)] * 2,
        in_specs=[HBM] * 5 + [VMEM] * 2,
        out_specs=[VMEM] * 2,
        scratch_shapes=[
            pltpu.VMEM((3, 6, 1, 1296), F32),
            pltpu.SMEM((8,), jnp.int32),
            pltpu.SMEM((8,), jnp.int32),
            pltpu.SMEM((8, 6), F32),
            pltpu.SMEM((8, 36), F32),
            pltpu.VMEM((112, 256), F32),
            pltpu.VMEM((112, 256), F32),
            pltpu.VMEM((112, 256), F32),
            pltpu.VMEM((112, 256), F32),
            pltpu.SemaphoreType.DMA((5,)),
        ],
        compiler_params=SMALL,
        cost_estimate=pl.CostEstimate(flops=100000000, bytes_accessed=1000000, transcendentals=0),
    )(occ_count, vir_count, eps_occ, eps_vir, amplitudes, ovov, partner)

    sums = [shape((144, 2 * LANES), F32)] * 3
    here_sum, below_sum, above_sum = pl.pallas_call(
        multiply_near,
        out_shape=sums,
        in_specs=[VMEM] * 10,
        out_specs=[VMEM] * 3,
        scratch_shapes=[pltpu.VMEM((16, DEPTH), F32), pltpu.VMEM((LANES, 2 * LANES), F32)],
        compiler_params=LARGE,
    )(*near_blocks, near_high, near_low, moved_a, swapped_b, moved_b, swapped_a)
    back_a = ring(below_sum, "yy", (-1, 1))
    back_b = ring(above_sum, "yy", (1, -1))
    packed = pl.pallas_call(
        multiply_far,
        out_shape=shape((32, 8, LANES), F32),
        in_specs=[VMEM] * 9,
        out_specs=VMEM,
        scratch_shapes=[pltpu.VMEM((16, DEPTH), F32)],
        compiler_params=LARGE,
    )(*far_blocks, far_high, far_low, here_sum, back_a, back_b)
    ladder = lax.all_to_all(packed, ("x", "z", "core"), 0, 0, tiled=True)
    return pl.pallas_call(
        finish,
        out_shape=shape((3, 6, 1, 1296), F32),
        in_specs=[VMEM] * 3,
        out_specs=VMEM,
        scratch_shapes=[pltpu.VMEM((24, WINDOW), F32)],
        compiler_params=SMALL,
    )(ladder, scale, cycle)


def solution(mesh):
    fine = Mesh(mesh.devices.reshape(4, 4, 4, 2), AXES)
    rows, cols = ("x", "z"), ("y", "core")
    return jax.shard_map(
        on_device,
        mesh=fine,
        in_specs=(P(rows, None, cols, None), P(cols, rows, None), P(rows, cols, None), P(), P(), P(), P()),
        out_specs=P(rows, None, cols, None),
        check_vma=False,
    )
```

```python
import jax
import jax.numpy as jnp
from jax import lax
from jax.experimental import pallas as pl
from jax.experimental.pallas import tpu as pltpu
from jax.sharding import Mesh, PartitionSpec as P

AXES = ("x", "z", "y", "core")
SHIFTS = ((1, 1), (-1, -1), (2, 2))
STEPS = (0, 1, -1, 2)
LANES = 128
TILES = 11
WINDOW = TILES * LANES
SPAN = 21
DEPTH = SPAN * LANES
MAIN = 8 * TILES
SHARD = 104
PMAIN = 8 * SPAN
PAIR = 192
QUAD = 2 * PAIR
PSLOT = 88
PROWS = SPAN * PSLOT
F32 = jnp.float32
BF16 = jnp.bfloat16
ANY = pl.BlockSpec(memory_space=pl.ANY)
HBM = pl.BlockSpec(memory_space=pltpu.HBM)
VMEM = pl.BlockSpec(memory_space=pltpu.VMEM)
HUGE = pltpu.CompilerParams(vmem_limit_bytes=56 * 1024 * 1024)
SMALL = pltpu.CompilerParams(vmem_limit_bytes=8 * 1024 * 1024)
LARGE = pltpu.CompilerParams(vmem_limit_bytes=28 * 1024 * 1024)


def ring(value, axes, steps):
    pairs = []
    for x in range(4):
        for z in range(4):
            for y in range(4):
                for core in range(2):
                    here = {"x": x, "z": z, "y": y, "core": core}
                    there = dict(here)
                    there[axes[core]] = (there[axes[core]] + steps[core]) % 4
                    pairs.append(
                        tuple(((p["x"] * 4 + p["z"]) * 4 + p["y"]) * 2 + p["core"] for p in (here, there))
                    )
    return lax.ppermute(value, AXES, pairs)


def swap_core(value):
    return lax.ppermute(value, "core", [(0, 1), (1, 0)])


def places():
    return tuple(lax.axis_index(name) for name in AXES)


def lane_orbitals(shape):
    lane = lax.broadcasted_iota(jnp.int32, shape, 1)
    a = jnp.floor((lane.astype(F32) + 0.5) * (1.0 / 36.0)).astype(jnp.int32)
    return a, lane - 36 * a


def window_copy(integrals, target, sem, chip):
    start = pl.multiple_of((chip & 3) * 2560, LANES)
    return pltpu.make_async_copy(integrals.at[:, :, pl.ds(start, DEPTH)], target.at[0:81], sem)


def open_step(occ_ref, vir_ref, amp_ref, integrals, keep_out, send_out, first_out, second_out, home_out,
              wide, amp, occ, vir, keep, send, first_v, second_v, home, sems, cut_sems, out_sems):
    x, z, y, core = places()
    copies = [
        pltpu.make_async_copy(source, target, sems.at[at])
        for at, (source, target) in enumerate(((occ_ref, occ), (vir_ref, vir), (amp_ref, amp)))
    ]
    cuts = [
        window_copy(integrals, first_v, cut_sems.at[0], y + 1 + 2 * core),
        window_copy(integrals, second_v, cut_sems.at[1], y + 3 - 2 * core),
        window_copy(integrals, home.at[0], cut_sems.at[2], y),
        window_copy(integrals, home.at[1], cut_sems.at[3], y + 2),
    ]
    outs = [
        pltpu.make_async_copy(source, target, out_sems.at[at])
        for at, (source, target) in enumerate(
            (
                (first_v, first_out),
                (second_v, second_out),
                (home.at[0], home_out.at[0]),
                (home.at[1], home_out.at[1]),
                (keep, keep_out),
                (send, send_out),
            )
        )
    ]
    for copy in copies + cuts:
        copy.start()
    wide[...] = jnp.zeros_like(wide)
    for copy in copies:
        copy.wait()
    for row in range(18):
        wide[row : row + 1, 0:1296] = amp[row // 6, row % 6]
    row_place = x * 4 + z
    occ_here = occ[row_place >> 1]
    first = 3 * (row_place & 1)
    irrep = 2 * y + core
    vir_here = vir[irrep]
    a, b = lane_orbitals(wide.shape)
    row = lax.broadcasted_iota(jnp.int32, wide.shape, 0)
    i_low = (row * 43) >> 8
    j = row - 6 * i_low
    live = (a < vir_here) & (b < vir_here) & (i_low + first < occ_here) & (j < occ_here)
    moved = pltpu.roll(jnp.where(live, wide[...], 0.0), 16 * irrep, 1)

    def write(ref, half):
        for t in range(TILES):
            columns = slice(t * LANES, (t + 1) * LANES)
            ref[8 * t : 8 * t + 8, :] = moved[8 * half : 8 * half + 8, columns]
            ref[MAIN + t : MAIN + t + 1, :] = moved[16 + half : 17 + half, columns]
        ref[MAIN + TILES : SHARD, :] = jnp.zeros((SHARD - MAIN - TILES, LANES), F32)

    @pl.when(core == 0)
    def _():
        write(keep, 0)
        write(send, 1)

    @pl.when(core == 1)
    def _():
        write(keep, 1)
        write(send, 0)

    for copy in outs[4:]:
        copy.start()
    for copy, out in zip(cuts, outs):
        copy.wait()
        out.start()
    for copy in outs:
        copy.wait()


def merge_irreps(even, odd, out, at):
    gap = SPAN - TILES
    out[at : at + 8 * gap, :] = even[0 : 8 * gap, :]
    out[at + 8 * gap : at + MAIN, :] = even[8 * gap : MAIN, :] + odd[0:8, :]
    out[at + MAIN : at + PMAIN, :] = odd[8:MAIN, :]
    extra = at + PMAIN
    out[extra : extra + gap, :] = even[MAIN : MAIN + gap, :]
    out[extra + gap : extra + TILES, :] = even[MAIN + gap : MAIN + TILES, :] + odd[MAIN : MAIN + 1, :]
    out[extra + TILES : extra + SPAN, :] = odd[MAIN + 1 : MAIN + TILES, :]
    out[extra + SPAN : at + PAIR, :] = jnp.zeros((PAIR - PMAIN - SPAN, LANES), F32)


def merge_pair(keep, got, home, out, home_out):
    core = lax.axis_index("core")

    @pl.when(core == 0)
    def _():
        merge_irreps(keep, got, out, 0)

    @pl.when(core == 1)
    def _():
        merge_irreps(got, keep, out, 0)


def join_pairs(near, far, home_other, out):
    out[0:PAIR, :] = near[...]
    out[PAIR:QUAD, :] = far[...]


def gather_four(b0, b1, b2, b3, near, far):
    for at, block in enumerate((b0, b1, b2, b3)):
        near[at * PAIR : (at + 1) * PAIR, :] = block[0:PAIR, :]
        far[at * PAIR : (at + 1) * PAIR, :] = block[PAIR:QUAD, :]


def nothing(*refs):
    pass


def hold(values, *witnesses):
    kept = range(len(values))
    return pl.pallas_call(
        nothing,
        out_shape=[jax.ShapeDtypeStruct(value.shape, value.dtype) for value in values],
        in_specs=[ANY] * (len(values) + len(witnesses)),
        out_specs=[ANY] * len(values),
        input_output_aliases={at: at for at in kept},
        compiler_params=SMALL,
    )(*values, *witnesses)


def left_side(blocks, extra):
    for t in range(SPAN):
        for d, block in enumerate(blocks):
            extra[4 * d : 4 * d + 4, t * LANES : (t + 1) * LANES] = block[pl.ds(PMAIN + t, 4, stride=PAIR), :]
    rows = []
    for block in blocks:
        for e in range(4):
            rows.append(
                jnp.concatenate(
                    [block[e * PAIR + 8 * t : e * PAIR + 8 * t + 8, :] for t in range(SPAN)], axis=1
                )
            )
    return split(jnp.concatenate(rows + [extra[...]], axis=0))


def split(value):
    high = value.astype(BF16)
    return high, (value - high.astype(F32)).astype(BF16)


def rows_side(ref, first):
    return jnp.concatenate([ref[pl.ds(first + t, PSLOT, stride=SPAN), :] for t in range(SPAN)], axis=1)


def last_by_last(p, q):
    return lax.dot_general(p, q, (((1,), (1,)), ((), ())), preferred_element_type=F32)


def split_home(home, home_other, witness, near_high, near_low, far_high, far_low):
    for side, ref in enumerate((home, home_other)):
        high, low = split(rows_side(ref, 0))
        rows = slice(side * PSLOT, (side + 1) * PSLOT)
        near_high[rows, :] = high
        near_low[rows, :] = low
        high, low = split(rows_side(ref, PROWS))
        pad = jnp.zeros((LANES - PSLOT, DEPTH), BF16)
        rows = slice(side * LANES, (side + 1) * LANES)
        far_high[rows, :] = jnp.concatenate([high, pad], axis=0)
        far_low[rows, :] = jnp.concatenate([low, pad], axis=0)


def multiply_near(b0, b1, b2, b3, near_high, near_low, below, below_other, above, above_other,
                  here_sum, below_sum, above_sum, extra, turned):
    high, low = left_side((b0, b1, b2, b3), extra)
    sides = [rows_side(ref, 0) for ref in (below, below_other, above, above_other)]
    v_high, v_low = split(jnp.concatenate(sides, axis=0))
    v_high = jnp.concatenate([near_high[...], v_high], axis=0)
    v_low = jnp.concatenate([near_low[...], v_low], axis=0)
    total = last_by_last(v_high, high) + (last_by_last(v_low, high) + last_by_last(v_high, low))
    turned[...] = jnp.zeros_like(turned)
    for at, ref in enumerate((here_sum, below_sum, above_sum)):
        for side in range(2):
            rows = slice((2 * at + side) * PSLOT, (2 * at + side + 1) * PSLOT)
            turned[0:PSLOT, 0:144] = total[rows, :]
            ref[:, side * LANES : (side + 1) * LANES] = turned[...].T[0:144, :]


def multiply_far(b0, b1, b2, b3, v_high, v_low, here_sum, back_a, back_b, out, extra):
    x, z, y, core = places()
    high, low = left_side((b0, b1, b2, b3), extra)
    partial = here_sum[...] + back_a[...] + back_b[...]
    row = lax.broadcasted_iota(jnp.int32, (8, LANES), 0)
    lane = lax.broadcasted_iota(jnp.int32, (8, LANES), 1)
    total = partial + (
        last_by_last(high, v_high[...]) + (last_by_last(low, v_high[...]) + last_by_last(high, v_low[...]))
    )
    for side in range(2):
        columns = slice(side * LANES, (side + 1) * LANES)
        last = total[128:144, columns]
        last_a = pltpu.roll(last, 81, 1)
        last_b = pltpu.roll(last, 34, 1)
        core_there = core if side == 0 else 1 - core
        for d in range(4):
            for e in range(4):
                s = 4 * d + e
                x_step = jnp.where(core == 0, STEPS[e], STEPS[d])
                z_step = jnp.where(core == 0, STEPS[d], STEPS[e])
                there = ((x - x_step) & 3) * 4 + ((z - z_step) & 3)
                main = total[8 * s : 8 * s + 8, columns]
                tail = jnp.where(row == 0, last_a[s : s + 1, :], last_b[s : s + 1, :])
                out[there * 2 + core_there] = jnp.where(lane < 81, main, tail)


def local_step(occ_ref, vir_ref, eps_occ_ref, eps_vir_ref, amp_ref, ovov, partner,
               scale, cycle, amp, occ, vir, eps_occ, eps_vir, left_a, left_b, panel_a, panel_b, sems):
    x, z, y, core = places()
    copies = [
        pltpu.make_async_copy(source, target, sems.at[at])
        for at, (source, target) in enumerate(
            ((occ_ref, occ), (vir_ref, vir), (eps_occ_ref, eps_occ), (eps_vir_ref, eps_vir), (amp_ref, amp))
        )
    ]
    for copy in copies:
        copy.start()
    panel_a[...] = jnp.zeros_like(panel_a)
    panel_b[...] = jnp.zeros_like(panel_b)
    left_a[...] = jnp.zeros_like(left_a)
    left_b[...] = jnp.zeros_like(left_b)
    lower = (z & 1) == 0
    for r in range(108):
        own, other = ovov[r], partner[r]
        panel_a[r : r + 1, 0:216] = jnp.where(lower, own, other)
        panel_b[r : r + 1, 0:216] = jnp.where(lower, other, own)
    for copy in copies:
        copy.wait()
    row_place = x * 4 + z
    shell = row_place >> 1
    first = 3 * (row_place & 1)
    irrep = 2 * y + core
    a, b = lane_orbitals((1, 1296))
    energy_a = jnp.zeros((1, 1296), F32)
    energy_b = jnp.zeros((1, 1296), F32)
    for slot in range(36):
        value = eps_vir[irrep, slot]
        energy_a = jnp.where(a == slot, value, energy_a)
        energy_b = jnp.where(b == slot, value, energy_b)
    lane_live = (a < vir[irrep]) & (b < vir[irrep])
    occ_here = occ[shell]
    for r in range(18):
        low, k = r // 6, r % 6
        i = first + low
        here = lane_live & (i < occ_here) & (k < occ_here)
        gap = eps_occ[shell, i] + eps_occ[shell, k] - energy_a - energy_b
        scale[r : r + 1, :] = jnp.where(here, 1.0, 0.0) / gap
        live = jnp.where(here, amp[low, k], 0.0)
        left, column = (left_a, 36 * k) if k < 3 else (left_b, 36 * (k - 3))
        for slot in range(36):
            left[36 * low + slot : 36 * low + slot + 1, column : column + 36] = live[
                :, 36 * slot : 36 * slot + 36
            ]
    dot = lambda p, q: jnp.dot(p, q, preferred_element_type=F32)
    total = None
    for left, panel in ((left_a, panel_a), (left_b, panel_b)):
        p_high, p_low = split(left[:, 0:112])
        q_high, q_low = split(panel[...])
        part = dot(p_high, q_high) + (dot(p_low, q_high) + dot(p_high, q_low))
        total = part if total is None else total + part
    for low in range(3):
        for j in range(6):
            r = 6 * low + j
            for slot in range(36):
                cycle[r : r + 1, 36 * slot : 36 * slot + 36] = total[
                    36 * low + slot : 36 * low + slot + 1, 36 * j : 36 * j + 36
                ]


def finish(sums, scale, cycle, out, wide):
    wide[...] = jnp.zeros_like(wide)
    lane8 = lax.broadcasted_iota(jnp.int32, (1, LANES), 1)
    lane = lax.broadcasted_iota(jnp.int32, (24, LANES), 1)
    for r in range(16):
        mains, lasts = [], []
        for core in range(2):
            block = sums[2 * r + core]
            mains.append(block)
            lasts.append(
                jnp.where(lane8 < 47, pltpu.roll(block, 47, 1)[0:1, :], pltpu.roll(block, 94, 1)[1:2, :])
            )
        stack = jnp.concatenate(mains + lasts + [jnp.zeros((6, LANES), F32)], axis=0)
        tile, start = divmod(81 * r, LANES)
        turned = pltpu.roll(stack, start, 1) if start else stack
        here = slice(tile * LANES, (tile + 1) * LANES)
        wide[:, here] = jnp.where((lane >= start) & (lane < start + 81), turned, wide[:, here])
        if start + 81 > LANES:
            after = slice((tile + 1) * LANES, (tile + 2) * LANES)
            wide[:, after] = jnp.where(lane < start + 81 - LANES, turned, wide[:, after])
    total = (wide[0:18, 0:1296] + cycle[...]) * scale[...]
    for r in range(18):
        out[r // 6, r % 6] = total[r : r + 1, :]


def on_device(amplitudes, vvvv, ovov, eps_occ, eps_vir, occ_count, vir_count):
    x, z, y, core = places()
    shape = jax.ShapeDtypeStruct
    integrals = vvvv.reshape(81, 1, 10368)
    window = shape((PSLOT, 1, DEPTH), F32)
    flat = lambda value: value.reshape(PROWS, LANES)
    keep, send, first_v, second_v, home = pl.pallas_call(
        open_step,
        out_shape=[shape((SHARD, LANES), F32)] * 2 + [window] * 2
        + [shape((2, PSLOT, 1, DEPTH), F32)],
        in_specs=[HBM] * 4,
        out_specs=[ANY] * 5,
        scratch_shapes=[
            pltpu.VMEM((24, WINDOW), F32),
            pltpu.VMEM((3, 6, 1, 1296), F32),
            pltpu.SMEM((8,), jnp.int32),
            pltpu.SMEM((8,), jnp.int32),
            pltpu.VMEM((SHARD, LANES), F32),
            pltpu.VMEM((SHARD, LANES), F32),
            pltpu.VMEM((PSLOT, 1, DEPTH), F32),
            pltpu.VMEM((PSLOT, 1, DEPTH), F32),
            pltpu.VMEM((2, PSLOT, 1, DEPTH), F32),
            pltpu.SemaphoreType.DMA((3,)),
            pltpu.SemaphoreType.DMA((4,)),
            pltpu.SemaphoreType.DMA((6,)),
        ],
        compiler_params=HUGE,
    )(occ_count, vir_count, amplitudes, integrals)
    got = swap_core(send)
    moved_a = ring(flat(first_v), "yy", (1, -1))
    partner = lax.ppermute(ovov, "z", [(0, 1), (1, 0), (2, 3), (3, 2)])
    home = home.reshape(2 * PROWS, LANES)
    pair, home = pl.pallas_call(
        merge_pair,
        out_shape=[shape((PAIR, LANES), F32), shape(home.shape, F32)],
        in_specs=[VMEM] * 2 + [ANY],
        out_specs=[VMEM, ANY],
        input_output_aliases={2: 1},
        compiler_params=SMALL,
    )(keep, got, home)
    home_other = swap_core(home)
    far_pair = ring(pair, "yy", (2, 2))
    quad = pl.pallas_call(
        join_pairs,
        out_shape=shape((QUAD, LANES), F32),
        in_specs=[VMEM] * 2 + [ANY],
        out_specs=VMEM,
        compiler_params=SMALL,
    )(pair, far_pair, home_other)
    (second_v,) = hold([flat(second_v)], far_pair)
    moved_b = ring(second_v, "yy", (-1, 1))

    near, far = pl.pallas_call(
        gather_four,
        out_shape=[shape((4 * PAIR, LANES), F32)] * 2,
        in_specs=[VMEM] * 4,
        out_specs=[VMEM] * 2,
        compiler_params=SMALL,
    )(quad, *[ring(quad, "xz", step) for step in SHIFTS])
    near_high, near_low, far_high, far_low = pl.pallas_call(
        split_home,
        out_shape=[shape((2 * PSLOT, DEPTH), BF16)] * 2 + [shape((2 * LANES, DEPTH), BF16)] * 2,
        in_specs=[VMEM] * 2 + [ANY],
        out_specs=[VMEM] * 4,
        compiler_params=LARGE,
        cost_estimate=pl.CostEstimate(flops=1, bytes_accessed=1, transcendentals=0),
    )(home, home_other, near)
    near_blocks = [near] + [ring(near, "zx", step) for step in SHIFTS]
    far_blocks = [far] + [ring(far, "zx", step) for step in SHIFTS]

    moved_a, moved_b = hold([moved_a, moved_b], *near_blocks[1:], near_high, partner)
    swapped_a, swapped_b = swap_core(moved_a), swap_core(moved_b)

    scale, cycle = pl.pallas_call(
        local_step,
        out_shape=[shape((18, 1296), F32)] * 2,
        in_specs=[HBM] * 5 + [VMEM] * 2,
        out_specs=[VMEM] * 2,
        scratch_shapes=[
            pltpu.VMEM((3, 6, 1, 1296), F32),
            pltpu.SMEM((8,), jnp.int32),
            pltpu.SMEM((8,), jnp.int32),
            pltpu.SMEM((8, 6), F32),
            pltpu.SMEM((8, 36), F32),
            pltpu.VMEM((112, 256), F32),
            pltpu.VMEM((112, 256), F32),
            pltpu.VMEM((112, 256), F32),
            pltpu.VMEM((112, 256), F32),
            pltpu.SemaphoreType.DMA((5,)),
        ],
        compiler_params=SMALL,
        cost_estimate=pl.CostEstimate(flops=100000000, bytes_accessed=1000000, transcendentals=0),
    )(occ_count, vir_count, eps_occ, eps_vir, amplitudes, ovov, partner)

    sums = [shape((144, 2 * LANES), F32)] * 3
    here_sum, below_sum, above_sum = pl.pallas_call(
        multiply_near,
        out_shape=sums,
        in_specs=[VMEM] * 10,
        out_specs=[VMEM] * 3,
        scratch_shapes=[pltpu.VMEM((16, DEPTH), F32), pltpu.VMEM((LANES, 2 * LANES), F32)],
        compiler_params=LARGE,
    )(*near_blocks, near_high, near_low, moved_a, swapped_b, moved_b, swapped_a)
    back_a = ring(below_sum, "yy", (-1, 1))
    back_b = ring(above_sum, "yy", (1, -1))
    packed = pl.pallas_call(
        multiply_far,
        out_shape=shape((32, 8, LANES), F32),
        in_specs=[VMEM] * 9,
        out_specs=VMEM,
        scratch_shapes=[pltpu.VMEM((16, DEPTH), F32)],
        compiler_params=LARGE,
    )(*far_blocks, far_high, far_low, here_sum, back_a, back_b)
    ladder = lax.all_to_all(packed, ("x", "z", "core"), 0, 0, tiled=True)
    return pl.pallas_call(
        finish,
        out_shape=shape((3, 6, 1, 1296), F32),
        in_specs=[VMEM] * 3,
        out_specs=VMEM,
        scratch_shapes=[pltpu.VMEM((24, WINDOW), F32)],
        compiler_params=SMALL,
    )(ladder, scale, cycle)


def solution(mesh):
    fine = Mesh(mesh.devices.reshape(4, 4, 4, 2), AXES)
    rows, cols = ("x", "z"), ("y", "core")
    return jax.shard_map(
        on_device,
        mesh=fine,
        in_specs=(P(rows, None, cols, None), P(cols, rows, None), P(rows, cols, None), P(), P(), P(), P()),
        out_specs=P(rows, None, cols, None),
        check_vma=False,
    )
```

```python
import jax
import jax.numpy as jnp
from jax import lax
from jax.experimental import pallas as pl
from jax.experimental.pallas import tpu as pltpu
from jax.sharding import Mesh, PartitionSpec as P

AXES = ("x", "z", "y", "core")
SHIFTS = ((2, 2), (1, 1), (-1, -1))
STEPS = (0, 2, 1, -1)
LANES = 128
TILES = 11
WINDOW = TILES * LANES
SPAN = 21
DEPTH = SPAN * LANES
MAIN = 8 * TILES
SHARD = 104
PMAIN = 8 * SPAN
PAIR = 192
QUAD = 2 * PAIR
PSLOT = 88
PROWS = SPAN * PSLOT
F32 = jnp.float32
BF16 = jnp.bfloat16
ANY = pl.BlockSpec(memory_space=pl.ANY)
HBM = pl.BlockSpec(memory_space=pltpu.HBM)
VMEM = pl.BlockSpec(memory_space=pltpu.VMEM)
HUGE = pltpu.CompilerParams(vmem_limit_bytes=56 * 1024 * 1024)
SMALL = pltpu.CompilerParams(vmem_limit_bytes=8 * 1024 * 1024)
LARGE = pltpu.CompilerParams(vmem_limit_bytes=28 * 1024 * 1024)


def ring(value, axes, steps):
    pairs = []
    for x in range(4):
        for z in range(4):
            for y in range(4):
                for core in range(2):
                    here = {"x": x, "z": z, "y": y, "core": core}
                    there = dict(here)
                    there[axes[core]] = (there[axes[core]] + steps[core]) % 4
                    pairs.append(
                        tuple(((p["x"] * 4 + p["z"]) * 4 + p["y"]) * 2 + p["core"] for p in (here, there))
                    )
    return lax.ppermute(value, AXES, pairs)


def swap_core(value):
    return lax.ppermute(value, "core", [(0, 1), (1, 0)])


def places():
    return tuple(lax.axis_index(name) for name in AXES)


def lane_orbitals(shape):
    lane = lax.broadcasted_iota(jnp.int32, shape, 1)
    a = jnp.floor((lane.astype(F32) + 0.5) * (1.0 / 36.0)).astype(jnp.int32)
    return a, lane - 36 * a


def window_copy(integrals, target, sem, chip):
    start = pl.multiple_of((chip & 3) * 2560, LANES)
    return pltpu.make_async_copy(integrals.at[:, :, pl.ds(start, DEPTH)], target.at[0:81], sem)


def open_step(occ_ref, vir_ref, amp_ref, integrals, keep_out, send_out, first_out, second_out, home_out,
              wide, amp, occ, vir, keep, send, first_v, second_v, home, sems, cut_sems, out_sems):
    x, z, y, core = places()
    copies = [
        pltpu.make_async_copy(source, target, sems.at[at])
        for at, (source, target) in enumerate(((occ_ref, occ), (vir_ref, vir), (amp_ref, amp)))
    ]
    cuts = [
        window_copy(integrals, first_v, cut_sems.at[0], y + 1 + 2 * core),
        window_copy(integrals, second_v, cut_sems.at[1], y + 3 - 2 * core),
        window_copy(integrals, home.at[0], cut_sems.at[2], y),
        window_copy(integrals, home.at[1], cut_sems.at[3], y + 2),
    ]
    outs = [
        pltpu.make_async_copy(source, target, out_sems.at[at])
        for at, (source, target) in enumerate(
            (
                (first_v, first_out),
                (second_v, second_out),
                (home.at[0], home_out.at[0]),
                (home.at[1], home_out.at[1]),
                (keep, keep_out),
                (send, send_out),
            )
        )
    ]
    for copy in copies + cuts:
        copy.start()
    wide[...] = jnp.zeros_like(wide)
    for copy in copies:
        copy.wait()
    for row in range(18):
        wide[row : row + 1, 0:1296] = amp[row // 6, row % 6]
    row_place = x * 4 + z
    occ_here = occ[row_place >> 1]
    first = 3 * (row_place & 1)
    irrep = 2 * y + core
    vir_here = vir[irrep]
    a, b = lane_orbitals(wide.shape)
    row = lax.broadcasted_iota(jnp.int32, wide.shape, 0)
    i_low = (row * 43) >> 8
    j = row - 6 * i_low
    live = (a < vir_here) & (b < vir_here) & (i_low + first < occ_here) & (j < occ_here)
    moved = pltpu.roll(jnp.where(live, wide[...], 0.0), 16 * irrep, 1)

    def write(ref, half):
        for t in range(TILES):
            columns = slice(t * LANES, (t + 1) * LANES)
            ref[8 * t : 8 * t + 8, :] = moved[8 * half : 8 * half + 8, columns]
            ref[MAIN + t : MAIN + t + 1, :] = moved[16 + half : 17 + half, columns]
        ref[MAIN + TILES : SHARD, :] = jnp.zeros((SHARD - MAIN - TILES, LANES), F32)

    @pl.when(core == 0)
    def _():
        write(keep, 0)
        write(send, 1)

    @pl.when(core == 1)
    def _():
        write(keep, 1)
        write(send, 0)

    for copy in outs[4:]:
        copy.start()
    for copy, out in zip(cuts, outs):
        copy.wait()
        out.start()
    for copy in outs:
        copy.wait()


def merge_irreps(even, odd, out, at):
    gap = SPAN - TILES
    out[at : at + 8 * gap, :] = even[0 : 8 * gap, :]
    out[at + 8 * gap : at + MAIN, :] = even[8 * gap : MAIN, :] + odd[0:8, :]
    out[at + MAIN : at + PMAIN, :] = odd[8:MAIN, :]
    extra = at + PMAIN
    out[extra : extra + gap, :] = even[MAIN : MAIN + gap, :]
    out[extra + gap : extra + TILES, :] = even[MAIN + gap : MAIN + TILES, :] + odd[MAIN : MAIN + 1, :]
    out[extra + TILES : extra + SPAN, :] = odd[MAIN + 1 : MAIN + TILES, :]
    out[extra + SPAN : at + PAIR, :] = jnp.zeros((PAIR - PMAIN - SPAN, LANES), F32)


def merge_pair(keep, got, home, out, home_out):
    core = lax.axis_index("core")

    @pl.when(core == 0)
    def _():
        merge_irreps(keep, got, out, 0)

    @pl.when(core == 1)
    def _():
        merge_irreps(got, keep, out, 0)


def join_pairs(near, far, home_other, out):
    out[0:PAIR, :] = near[...]
    out[PAIR:QUAD, :] = far[...]


def gather_four(b0, b1, b2, b3, near, far):
    for at, block in enumerate((b0, b1, b2, b3)):
        near[at * PAIR : (at + 1) * PAIR, :] = block[0:PAIR, :]
        far[at * PAIR : (at + 1) * PAIR, :] = block[PAIR:QUAD, :]


def nothing(*refs):
    pass


def hold(values, *witnesses):
    kept = range(len(values))
    return pl.pallas_call(
        nothing,
        out_shape=[jax.ShapeDtypeStruct(value.shape, value.dtype) for value in values],
        in_specs=[ANY] * (len(values) + len(witnesses)),
        out_specs=[ANY] * len(values),
        input_output_aliases={at: at for at in kept},
        compiler_params=SMALL,
    )(*values, *witnesses)


def left_side(blocks, extra):
    for t in range(SPAN):
        for d, block in enumerate(blocks):
            extra[4 * d : 4 * d + 4, t * LANES : (t + 1) * LANES] = block[pl.ds(PMAIN + t, 4, stride=PAIR), :]
    rows = []
    for block in blocks:
        for e in range(4):
            rows.append(
                jnp.concatenate(
                    [block[e * PAIR + 8 * t : e * PAIR + 8 * t + 8, :] for t in range(SPAN)], axis=1
                )
            )
    return split(jnp.concatenate(rows + [extra[...]], axis=0))


def split(value):
    high = value.astype(BF16)
    return high, (value - high.astype(F32)).astype(BF16)


def rows_side(ref, first):
    return jnp.concatenate([ref[pl.ds(first + t, PSLOT, stride=SPAN), :] for t in range(SPAN)], axis=1)


def last_by_last(p, q):
    return lax.dot_general(p, q, (((1,), (1,)), ((), ())), preferred_element_type=F32)


def split_home(home, home_other, witness, near_high, near_low, far_high, far_low):
    for side, ref in enumerate((home, home_other)):
        high, low = split(rows_side(ref, 0))
        rows = slice(side * PSLOT, (side + 1) * PSLOT)
        near_high[rows, :] = high
        near_low[rows, :] = low
        high, low = split(rows_side(ref, PROWS))
        pad = jnp.zeros((LANES - PSLOT, DEPTH), BF16)
        rows = slice(side * LANES, (side + 1) * LANES)
        far_high[rows, :] = jnp.concatenate([high, pad], axis=0)
        far_low[rows, :] = jnp.concatenate([low, pad], axis=0)


def multiply_near(b0, b1, b2, b3, near_high, near_low, below, below_other, above, above_other,
                  here_sum, below_sum, above_sum, extra, turned):
    high, low = left_side((b0, b1, b2, b3), extra)
    sides = [rows_side(ref, 0) for ref in (below, below_other, above, above_other)]
    v_high, v_low = split(jnp.concatenate(sides, axis=0))
    v_high = jnp.concatenate([near_high[...], v_high], axis=0)
    v_low = jnp.concatenate([near_low[...], v_low], axis=0)
    total = last_by_last(v_high, high) + (last_by_last(v_low, high) + last_by_last(v_high, low))
    turned[...] = jnp.zeros_like(turned)
    for at, ref in enumerate((here_sum, below_sum, above_sum)):
        for side in range(2):
            rows = slice((2 * at + side) * PSLOT, (2 * at + side + 1) * PSLOT)
            turned[0:PSLOT, 0:144] = total[rows, :]
            ref[:, side * LANES : (side + 1) * LANES] = turned[...].T[0:144, :]


def multiply_far(b0, b1, b2, b3, v_high, v_low, here_sum, back_a, back_b, out, extra):
    x, z, y, core = places()
    high, low = left_side((b0, b1, b2, b3), extra)
    partial = here_sum[...] + back_a[...] + back_b[...]
    row = lax.broadcasted_iota(jnp.int32, (8, LANES), 0)
    lane = lax.broadcasted_iota(jnp.int32, (8, LANES), 1)
    total = partial + (
        last_by_last(high, v_high[...]) + (last_by_last(low, v_high[...]) + last_by_last(high, v_low[...]))
    )
    for side in range(2):
        columns = slice(side * LANES, (side + 1) * LANES)
        last = total[128:144, columns]
        last_a = pltpu.roll(last, 81, 1)
        last_b = pltpu.roll(last, 34, 1)
        core_there = core if side == 0 else 1 - core
        for d in range(4):
            for e in range(4):
                s = 4 * d + e
                x_step = jnp.where(core == 0, STEPS[e], STEPS[d])
                z_step = jnp.where(core == 0, STEPS[d], STEPS[e])
                there = ((x - x_step) & 3) * 4 + ((z - z_step) & 3)
                main = total[8 * s : 8 * s + 8, columns]
                tail = jnp.where(row == 0, last_a[s : s + 1, :], last_b[s : s + 1, :])
                out[there * 2 + core_there] = jnp.where(lane < 81, main, tail)


def local_step(occ_ref, vir_ref, eps_occ_ref, eps_vir_ref, amp_ref, ovov, partner,
               scale, cycle, amp, occ, vir, eps_occ, eps_vir, left_a, left_b, panel_a, panel_b, sems):
    x, z, y, core = places()
    copies = [
        pltpu.make_async_copy(source, target, sems.at[at])
        for at, (source, target) in enumerate(
            ((occ_ref, occ), (vir_ref, vir), (eps_occ_ref, eps_occ), (eps_vir_ref, eps_vir), (amp_ref, amp))
        )
    ]
    for copy in copies:
        copy.start()
    panel_a[...] = jnp.zeros_like(panel_a)
    panel_b[...] = jnp.zeros_like(panel_b)
    left_a[...] = jnp.zeros_like(left_a)
    left_b[...] = jnp.zeros_like(left_b)
    lower = (z & 1) == 0
    for r in range(108):
        own, other = ovov[r], partner[r]
        panel_a[r : r + 1, 0:216] = jnp.where(lower, own, other)
        panel_b[r : r + 1, 0:216] = jnp.where(lower, other, own)
    for copy in copies:
        copy.wait()
    row_place = x * 4 + z
    shell = row_place >> 1
    first = 3 * (row_place & 1)
    irrep = 2 * y + core
    a, b = lane_orbitals((1, 1296))
    energy_a = jnp.zeros((1, 1296), F32)
    energy_b = jnp.zeros((1, 1296), F32)
    for slot in range(36):
        value = eps_vir[irrep, slot]
        energy_a = jnp.where(a == slot, value, energy_a)
        energy_b = jnp.where(b == slot, value, energy_b)
    lane_live = (a < vir[irrep]) & (b < vir[irrep])
    occ_here = occ[shell]
    for r in range(18):
        low, k = r // 6, r % 6
        i = first + low
        here = lane_live & (i < occ_here) & (k < occ_here)
        gap = eps_occ[shell, i] + eps_occ[shell, k] - energy_a - energy_b
        scale[r : r + 1, :] = jnp.where(here, 1.0, 0.0) / gap
        live = jnp.where(here, amp[low, k], 0.0)
        left, column = (left_a, 36 * k) if k < 3 else (left_b, 36 * (k - 3))
        for slot in range(36):
            left[36 * low + slot : 36 * low + slot + 1, column : column + 36] = live[
                :, 36 * slot : 36 * slot + 36
            ]
    dot = lambda p, q: jnp.dot(p, q, preferred_element_type=F32)
    total = None
    for left, panel in ((left_a, panel_a), (left_b, panel_b)):
        p_high, p_low = split(left[:, 0:112])
        q_high, q_low = split(panel[...])
        part = dot(p_high, q_high) + (dot(p_low, q_high) + dot(p_high, q_low))
        total = part if total is None else total + part
    for low in range(3):
        for j in range(6):
            r = 6 * low + j
            for slot in range(36):
                cycle[r : r + 1, 36 * slot : 36 * slot + 36] = total[
                    36 * low + slot : 36 * low + slot + 1, 36 * j : 36 * j + 36
                ]


def finish(sums, scale, cycle, out, wide):
    wide[...] = jnp.zeros_like(wide)
    lane8 = lax.broadcasted_iota(jnp.int32, (1, LANES), 1)
    lane = lax.broadcasted_iota(jnp.int32, (24, LANES), 1)
    for r in range(16):
        mains, lasts = [], []
        for core in range(2):
            block = sums[2 * r + core]
            mains.append(block)
            lasts.append(
                jnp.where(lane8 < 47, pltpu.roll(block, 47, 1)[0:1, :], pltpu.roll(block, 94, 1)[1:2, :])
            )
        stack = jnp.concatenate(mains + lasts + [jnp.zeros((6, LANES), F32)], axis=0)
        tile, start = divmod(81 * r, LANES)
        turned = pltpu.roll(stack, start, 1) if start else stack
        here = slice(tile * LANES, (tile + 1) * LANES)
        wide[:, here] = jnp.where((lane >= start) & (lane < start + 81), turned, wide[:, here])
        if start + 81 > LANES:
            after = slice((tile + 1) * LANES, (tile + 2) * LANES)
            wide[:, after] = jnp.where(lane < start + 81 - LANES, turned, wide[:, after])
    total = (wide[0:18, 0:1296] + cycle[...]) * scale[...]
    for r in range(18):
        out[r // 6, r % 6] = total[r : r + 1, :]


def on_device(amplitudes, vvvv, ovov, eps_occ, eps_vir, occ_count, vir_count):
    x, z, y, core = places()
    shape = jax.ShapeDtypeStruct
    integrals = vvvv.reshape(81, 1, 10368)
    window = shape((PSLOT, 1, DEPTH), F32)
    flat = lambda value: value.reshape(PROWS, LANES)
    keep, send, first_v, second_v, home = pl.pallas_call(
        open_step,
        out_shape=[shape((SHARD, LANES), F32)] * 2 + [window] * 2
        + [shape((2, PSLOT, 1, DEPTH), F32)],
        in_specs=[HBM] * 4,
        out_specs=[ANY] * 5,
        scratch_shapes=[
            pltpu.VMEM((24, WINDOW), F32),
            pltpu.VMEM((3, 6, 1, 1296), F32),
            pltpu.SMEM((8,), jnp.int32),
            pltpu.SMEM((8,), jnp.int32),
            pltpu.VMEM((SHARD, LANES), F32),
            pltpu.VMEM((SHARD, LANES), F32),
            pltpu.VMEM((PSLOT, 1, DEPTH), F32),
            pltpu.VMEM((PSLOT, 1, DEPTH), F32),
            pltpu.VMEM((2, PSLOT, 1, DEPTH), F32),
            pltpu.SemaphoreType.DMA((3,)),
            pltpu.SemaphoreType.DMA((4,)),
            pltpu.SemaphoreType.DMA((6,)),
        ],
        compiler_params=HUGE,
    )(occ_count, vir_count, amplitudes, integrals)
    got = swap_core(send)
    moved_a = ring(flat(first_v), "yy", (1, -1))
    partner = lax.ppermute(ovov, "z", [(0, 1), (1, 0), (2, 3), (3, 2)])
    home = home.reshape(2 * PROWS, LANES)
    pair, home = pl.pallas_call(
        merge_pair,
        out_shape=[shape((PAIR, LANES), F32), shape(home.shape, F32)],
        in_specs=[VMEM] * 2 + [ANY],
        out_specs=[VMEM, ANY],
        input_output_aliases={2: 1},
        compiler_params=SMALL,
    )(keep, got, home)
    home_other = swap_core(home)
    far_pair = ring(pair, "yy", (2, 2))
    quad = pl.pallas_call(
        join_pairs,
        out_shape=shape((QUAD, LANES), F32),
        in_specs=[VMEM] * 2 + [ANY],
        out_specs=VMEM,
        compiler_params=SMALL,
    )(pair, far_pair, home_other)
    (second_v,) = hold([flat(second_v)], far_pair)
    moved_b = ring(second_v, "yy", (-1, 1))

    near, far = pl.pallas_call(
        gather_four,
        out_shape=[shape((4 * PAIR, LANES), F32)] * 2,
        in_specs=[VMEM] * 4,
        out_specs=[VMEM] * 2,
        compiler_params=SMALL,
    )(quad, *[ring(quad, "xz", step) for step in SHIFTS])
    near_high, near_low, far_high, far_low = pl.pallas_call(
        split_home,
        out_shape=[shape((2 * PSLOT, DEPTH), BF16)] * 2 + [shape((2 * LANES, DEPTH), BF16)] * 2,
        in_specs=[VMEM] * 2 + [ANY],
        out_specs=[VMEM] * 4,
        compiler_params=LARGE,
        cost_estimate=pl.CostEstimate(flops=1, bytes_accessed=1, transcendentals=0),
    )(home, home_other, near)
    near_blocks = [near] + [ring(near, "zx", step) for step in SHIFTS]
    far_blocks = [far] + [ring(far, "zx", step) for step in SHIFTS]

    moved_a, moved_b = hold([moved_a, moved_b], *near_blocks[1:], near_high, partner)
    swapped_a, swapped_b = swap_core(moved_a), swap_core(moved_b)

    scale, cycle = pl.pallas_call(
        local_step,
        out_shape=[shape((18, 1296), F32)] * 2,
        in_specs=[HBM] * 5 + [VMEM] * 2,
        out_specs=[VMEM] * 2,
        scratch_shapes=[
            pltpu.VMEM((3, 6, 1, 1296), F32),
            pltpu.SMEM((8,), jnp.int32),
            pltpu.SMEM((8,), jnp.int32),
            pltpu.SMEM((8, 6), F32),
            pltpu.SMEM((8, 36), F32),
            pltpu.VMEM((112, 256), F32),
            pltpu.VMEM((112, 256), F32),
            pltpu.VMEM((112, 256), F32),
            pltpu.VMEM((112, 256), F32),
            pltpu.SemaphoreType.DMA((5,)),
        ],
        compiler_params=SMALL,
        cost_estimate=pl.CostEstimate(flops=100000000, bytes_accessed=1000000, transcendentals=0),
    )(occ_count, vir_count, eps_occ, eps_vir, amplitudes, ovov, partner)

    sums = [shape((144, 2 * LANES), F32)] * 3
    here_sum, below_sum, above_sum = pl.pallas_call(
        multiply_near,
        out_shape=sums,
        in_specs=[VMEM] * 10,
        out_specs=[VMEM] * 3,
        scratch_shapes=[pltpu.VMEM((16, DEPTH), F32), pltpu.VMEM((LANES, 2 * LANES), F32)],
        compiler_params=LARGE,
    )(*near_blocks, near_high, near_low, moved_a, swapped_b, moved_b, swapped_a)
    back_a = ring(below_sum, "yy", (-1, 1))
    back_b = ring(above_sum, "yy", (1, -1))
    packed = pl.pallas_call(
        multiply_far,
        out_shape=shape((32, 8, LANES), F32),
        in_specs=[VMEM] * 9,
        out_specs=VMEM,
        scratch_shapes=[pltpu.VMEM((16, DEPTH), F32)],
        compiler_params=LARGE,
    )(*far_blocks, far_high, far_low, here_sum, back_a, back_b)
    ladder = lax.all_to_all(packed, ("x", "z", "core"), 0, 0, tiled=True)
    return pl.pallas_call(
        finish,
        out_shape=shape((3, 6, 1, 1296), F32),
        in_specs=[VMEM] * 3,
        out_specs=VMEM,
        scratch_shapes=[pltpu.VMEM((24, WINDOW), F32)],
        compiler_params=SMALL,
    )(ladder, scale, cycle)


def solution(mesh):
    fine = Mesh(mesh.devices.reshape(4, 4, 4, 2), AXES)
    rows, cols = ("x", "z"), ("y", "core")
    return jax.shard_map(
        on_device,
        mesh=fine,
        in_specs=(P(rows, None, cols, None), P(cols, rows, None), P(rows, cols, None), P(), P(), P(), P()),
        out_specs=P(rows, None, cols, None),
        check_vma=False,
    )
```

```python
import jax
import jax.numpy as jnp
from jax import lax
from jax.experimental import pallas as pl
from jax.experimental.pallas import tpu as pltpu
from jax.sharding import Mesh, PartitionSpec as P

AXES = ("x", "z", "y", "core")
SHIFTS = ((2, 2), (1, 1), (-1, -1))
STEPS = (0, 2, 1, -1)
LANES = 128
TILES = 11
WINDOW = TILES * LANES
SPAN = 21
DEPTH = SPAN * LANES
MAIN = 8 * TILES
SHARD = 104
PMAIN = 8 * SPAN
PAIR = 192
QUAD = 2 * PAIR
PSLOT = 88
PROWS = SPAN * PSLOT
F32 = jnp.float32
BF16 = jnp.bfloat16
ANY = pl.BlockSpec(memory_space=pl.ANY)
HBM = pl.BlockSpec(memory_space=pltpu.HBM)
VMEM = pl.BlockSpec(memory_space=pltpu.VMEM)
HUGE = pltpu.CompilerParams(vmem_limit_bytes=56 * 1024 * 1024)
SMALL = pltpu.CompilerParams(vmem_limit_bytes=8 * 1024 * 1024)
LARGE = pltpu.CompilerParams(vmem_limit_bytes=28 * 1024 * 1024)


def ring(value, axes, steps):
    pairs = []
    for x in range(4):
        for z in range(4):
            for y in range(4):
                for core in range(2):
                    here = {"x": x, "z": z, "y": y, "core": core}
                    there = dict(here)
                    there[axes[core]] = (there[axes[core]] + steps[core]) % 4
                    pairs.append(
                        tuple(((p["x"] * 4 + p["z"]) * 4 + p["y"]) * 2 + p["core"] for p in (here, there))
                    )
    return lax.ppermute(value, AXES, pairs)


def swap_core(value):
    return lax.ppermute(value, "core", [(0, 1), (1, 0)])


def places():
    return tuple(lax.axis_index(name) for name in AXES)


def lane_orbitals(shape):
    lane = lax.broadcasted_iota(jnp.int32, shape, 1)
    a = jnp.floor((lane.astype(F32) + 0.5) * (1.0 / 36.0)).astype(jnp.int32)
    return a, lane - 36 * a


def window_copy(integrals, target, sem, chip):
    start = pl.multiple_of((chip & 3) * 2560, LANES)
    return pltpu.make_async_copy(integrals.at[:, :, pl.ds(start, DEPTH)], target.at[0:81], sem)


def open_step(occ_ref, vir_ref, amp_ref, integrals, keep_out, send_out, first_out, second_out, home_out,
              wide, amp, occ, vir, keep, send, first_v, second_v, home, sems, cut_sems, out_sems):
    x, z, y, core = places()
    copies = [
        pltpu.make_async_copy(source, target, sems.at[at])
        for at, (source, target) in enumerate(((occ_ref, occ), (vir_ref, vir), (amp_ref, amp)))
    ]
    cuts = [
        window_copy(integrals, first_v, cut_sems.at[0], y + 1 + 2 * core),
        window_copy(integrals, second_v, cut_sems.at[1], y + 3 - 2 * core),
        window_copy(integrals, home.at[0], cut_sems.at[2], y),
        window_copy(integrals, home.at[1], cut_sems.at[3], y + 2),
    ]
    outs = [
        pltpu.make_async_copy(source, target, out_sems.at[at])
        for at, (source, target) in enumerate(
            (
                (first_v, first_out),
                (second_v, second_out),
                (home.at[0], home_out.at[0]),
                (home.at[1], home_out.at[1]),
                (keep, keep_out),
                (send, send_out),
            )
        )
    ]
    for copy in copies + cuts:
        copy.start()
    wide[...] = jnp.zeros_like(wide)
    for copy in copies:
        copy.wait()
    for row in range(18):
        wide[row : row + 1, 0:1296] = amp[row // 6, row % 6]
    row_place = x * 4 + z
    occ_here = occ[row_place >> 1]
    first = 3 * (row_place & 1)
    irrep = 2 * y + core
    vir_here = vir[irrep]
    a, b = lane_orbitals(wide.shape)
    row = lax.broadcasted_iota(jnp.int32, wide.shape, 0)
    i_low = (row * 43) >> 8
    j = row - 6 * i_low
    live = (a < vir_here) & (b < vir_here) & (i_low + first < occ_here) & (j < occ_here)
    moved = pltpu.roll(jnp.where(live, wide[...], 0.0), 16 * irrep, 1)

    def write(ref, half):
        for t in range(TILES):
            columns = slice(t * LANES, (t + 1) * LANES)
            ref[8 * t : 8 * t + 8, :] = moved[8 * half : 8 * half + 8, columns]
            ref[MAIN + t : MAIN + t + 1, :] = moved[16 + half : 17 + half, columns]
        ref[MAIN + TILES : SHARD, :] = jnp.zeros((SHARD - MAIN - TILES, LANES), F32)

    @pl.when(core == 0)
    def _():
        write(keep, 0)
        write(send, 1)

    @pl.when(core == 1)
    def _():
        write(keep, 1)
        write(send, 0)

    for copy in outs[4:]:
        copy.start()
    for copy, out in zip(cuts, outs):
        copy.wait()
        out.start()
    for copy in outs:
        copy.wait()


def merge_irreps(even, odd, out, at):
    gap = SPAN - TILES
    out[at : at + 8 * gap, :] = even[0 : 8 * gap, :]
    out[at + 8 * gap : at + MAIN, :] = even[8 * gap : MAIN, :] + odd[0:8, :]
    out[at + MAIN : at + PMAIN, :] = odd[8:MAIN, :]
    extra = at + PMAIN
    out[extra : extra + gap, :] = even[MAIN : MAIN + gap, :]
    out[extra + gap : extra + TILES, :] = even[MAIN + gap : MAIN + TILES, :] + odd[MAIN : MAIN + 1, :]
    out[extra + TILES : extra + SPAN, :] = odd[MAIN + 1 : MAIN + TILES, :]
    out[extra + SPAN : at + PAIR, :] = jnp.zeros((PAIR - PMAIN - SPAN, LANES), F32)


def merge_pair(keep, got, home, out, home_out):
    core = lax.axis_index("core")

    @pl.when(core == 0)
    def _():
        merge_irreps(keep, got, out, 0)

    @pl.when(core == 1)
    def _():
        merge_irreps(got, keep, out, 0)


def join_pairs(near, far, home_other, out):
    out[0:PAIR, :] = near[...]
    out[PAIR:QUAD, :] = far[...]


def gather_four(b0, b1, b2, b3, near, far):
    for at, block in enumerate((b0, b1, b2, b3)):
        near[at * PAIR : (at + 1) * PAIR, :] = block[0:PAIR, :]
        far[at * PAIR : (at + 1) * PAIR, :] = block[PAIR:QUAD, :]


def nothing(*refs):
    pass


def hold(values, *witnesses):
    kept = range(len(values))
    return pl.pallas_call(
        nothing,
        out_shape=[jax.ShapeDtypeStruct(value.shape, value.dtype) for value in values],
        in_specs=[ANY] * (len(values) + len(witnesses)),
        out_specs=[ANY] * len(values),
        input_output_aliases={at: at for at in kept},
        compiler_params=SMALL,
    )(*values, *witnesses)


def left_side(blocks, extra):
    for t in range(SPAN):
        for d, block in enumerate(blocks):
            extra[4 * d : 4 * d + 4, t * LANES : (t + 1) * LANES] = block[pl.ds(PMAIN + t, 4, stride=PAIR), :]
    rows = []
    for block in blocks:
        for e in range(4):
            rows.append(
                jnp.concatenate(
                    [block[e * PAIR + 8 * t : e * PAIR + 8 * t + 8, :] for t in range(SPAN)], axis=1
                )
            )
    return split(jnp.concatenate(rows + [extra[...]], axis=0))


def split(value):
    high = value.astype(BF16)
    return high, (value - high.astype(F32)).astype(BF16)


def rows_side(ref, first):
    return jnp.concatenate([ref[pl.ds(first + t, PSLOT, stride=SPAN), :] for t in range(SPAN)], axis=1)


def last_by_last(p, q):
    return lax.dot_general(p, q, (((1,), (1,)), ((), ())), preferred_element_type=F32)


def split_home(home, home_other, witness, near_high, near_low, far_high, far_low):
    for side, ref in enumerate((home, home_other)):
        high, low = split(rows_side(ref, 0))
        rows = slice(side * PSLOT, (side + 1) * PSLOT)
        near_high[rows, :] = high
        near_low[rows, :] = low
        high, low = split(rows_side(ref, PROWS))
        pad = jnp.zeros((LANES - PSLOT, DEPTH), BF16)
        rows = slice(side * LANES, (side + 1) * LANES)
        far_high[rows, :] = jnp.concatenate([high, pad], axis=0)
        far_low[rows, :] = jnp.concatenate([low, pad], axis=0)


def multiply_near(b0, b2, b1, b3, near_high, near_low, below, below_other, above, above_other,
                  here_sum, below_sum, above_sum, extra, turned):
    high, low = left_side((b0, b1, b2, b3), extra)
    sides = [rows_side(ref, 0) for ref in (below, below_other, above, above_other)]
    v_high, v_low = split(jnp.concatenate(sides, axis=0))
    v_high = jnp.concatenate([near_high[...], v_high], axis=0)
    v_low = jnp.concatenate([near_low[...], v_low], axis=0)
    total = last_by_last(v_high, high) + (last_by_last(v_low, high) + last_by_last(v_high, low))
    turned[...] = jnp.zeros_like(turned)
    for at, ref in enumerate((here_sum, below_sum, above_sum)):
        for side in range(2):
            rows = slice((2 * at + side) * PSLOT, (2 * at + side + 1) * PSLOT)
            turned[0:PSLOT, 0:144] = total[rows, :]
            ref[:, side * LANES : (side + 1) * LANES] = turned[...].T[0:144, :]


def multiply_far(b0, b1, b2, b3, v_high, v_low, here_sum, back_a, back_b, out, extra):
    x, z, y, core = places()
    high, low = left_side((b0, b1, b2, b3), extra)
    partial = here_sum[...] + back_a[...] + back_b[...]
    row = lax.broadcasted_iota(jnp.int32, (8, LANES), 0)
    lane = lax.broadcasted_iota(jnp.int32, (8, LANES), 1)
    total = partial + (
        last_by_last(high, v_high[...]) + (last_by_last(low, v_high[...]) + last_by_last(high, v_low[...]))
    )
    for side in range(2):
        columns = slice(side * LANES, (side + 1) * LANES)
        last = total[128:144, columns]
        last_a = pltpu.roll(last, 81, 1)
        last_b = pltpu.roll(last, 34, 1)
        core_there = core if side == 0 else 1 - core
        for d in range(4):
            for e in range(4):
                s = 4 * d + e
                x_step = jnp.where(core == 0, STEPS[e], STEPS[d])
                z_step = jnp.where(core == 0, STEPS[d], STEPS[e])
                there = ((x - x_step) & 3) * 4 + ((z - z_step) & 3)
                main = total[8 * s : 8 * s + 8, columns]
                tail = jnp.where(row == 0, last_a[s : s + 1, :], last_b[s : s + 1, :])
                out[there * 2 + core_there] = jnp.where(lane < 81, main, tail)


def local_step(occ_ref, vir_ref, eps_occ_ref, eps_vir_ref, amp_ref, ovov, partner,
               scale, cycle, amp, occ, vir, eps_occ, eps_vir, left_a, left_b, panel_a, panel_b, sems):
    x, z, y, core = places()
    copies = [
        pltpu.make_async_copy(source, target, sems.at[at])
        for at, (source, target) in enumerate(
            ((occ_ref, occ), (vir_ref, vir), (eps_occ_ref, eps_occ), (eps_vir_ref, eps_vir), (amp_ref, amp))
        )
    ]
    for copy in copies:
        copy.start()
    panel_a[...] = jnp.zeros_like(panel_a)
    panel_b[...] = jnp.zeros_like(panel_b)
    left_a[...] = jnp.zeros_like(left_a)
    left_b[...] = jnp.zeros_like(left_b)
    lower = (z & 1) == 0
    for r in range(108):
        own, other = ovov[r], partner[r]
        panel_a[r : r + 1, 0:216] = jnp.where(lower, own, other)
        panel_b[r : r + 1, 0:216] = jnp.where(lower, other, own)
    for copy in copies:
        copy.wait()
    row_place = x * 4 + z
    shell = row_place >> 1
    first = 3 * (row_place & 1)
    irrep = 2 * y + core
    a, b = lane_orbitals((1, 1296))
    energy_a = jnp.zeros((1, 1296), F32)
    energy_b = jnp.zeros((1, 1296), F32)
    for slot in range(36):
        value = eps_vir[irrep, slot]
        energy_a = jnp.where(a == slot, value, energy_a)
        energy_b = jnp.where(b == slot, value, energy_b)
    lane_live = (a < vir[irrep]) & (b < vir[irrep])
    occ_here = occ[shell]
    for r in range(18):
        low, k = r // 6, r % 6
        i = first + low
        here = lane_live & (i < occ_here) & (k < occ_here)
        gap = eps_occ[shell, i] + eps_occ[shell, k] - energy_a - energy_b
        scale[r : r + 1, :] = jnp.where(here, 1.0, 0.0) / gap
        live = jnp.where(here, amp[low, k], 0.0)
        left, column = (left_a, 36 * k) if k < 3 else (left_b, 36 * (k - 3))
        for slot in range(36):
            left[36 * low + slot : 36 * low + slot + 1, column : column + 36] = live[
                :, 36 * slot : 36 * slot + 36
            ]
    dot = lambda p, q: jnp.dot(p, q, preferred_element_type=F32)
    total = None
    for left, panel in ((left_a, panel_a), (left_b, panel_b)):
        p_high, p_low = split(left[:, 0:112])
        q_high, q_low = split(panel[...])
        part = dot(p_high, q_high) + (dot(p_low, q_high) + dot(p_high, q_low))
        total = part if total is None else total + part
    for low in range(3):
        for j in range(6):
            r = 6 * low + j
            for slot in range(36):
                cycle[r : r + 1, 36 * slot : 36 * slot + 36] = total[
                    36 * low + slot : 36 * low + slot + 1, 36 * j : 36 * j + 36
                ]


def finish(sums, scale, cycle, out, wide):
    wide[...] = jnp.zeros_like(wide)
    lane8 = lax.broadcasted_iota(jnp.int32, (1, LANES), 1)
    lane = lax.broadcasted_iota(jnp.int32, (24, LANES), 1)
    for r in range(16):
        mains, lasts = [], []
        for core in range(2):
            block = sums[2 * r + core]
            mains.append(block)
            lasts.append(
                jnp.where(lane8 < 47, pltpu.roll(block, 47, 1)[0:1, :], pltpu.roll(block, 94, 1)[1:2, :])
            )
        stack = jnp.concatenate(mains + lasts + [jnp.zeros((6, LANES), F32)], axis=0)
        tile, start = divmod(81 * r, LANES)
        turned = pltpu.roll(stack, start, 1) if start else stack
        here = slice(tile * LANES, (tile + 1) * LANES)
        wide[:, here] = jnp.where((lane >= start) & (lane < start + 81), turned, wide[:, here])
        if start + 81 > LANES:
            after = slice((tile + 1) * LANES, (tile + 2) * LANES)
            wide[:, after] = jnp.where(lane < start + 81 - LANES, turned, wide[:, after])
    total = (wide[0:18, 0:1296] + cycle[...]) * scale[...]
    for r in range(18):
        out[r // 6, r % 6] = total[r : r + 1, :]


def on_device(amplitudes, vvvv, ovov, eps_occ, eps_vir, occ_count, vir_count):
    x, z, y, core = places()
    shape = jax.ShapeDtypeStruct
    integrals = vvvv.reshape(81, 1, 10368)
    window = shape((PSLOT, 1, DEPTH), F32)
    flat = lambda value: value.reshape(PROWS, LANES)
    keep, send, first_v, second_v, home = pl.pallas_call(
        open_step,
        out_shape=[shape((SHARD, LANES), F32)] * 2 + [window] * 2
        + [shape((2, PSLOT, 1, DEPTH), F32)],
        in_specs=[HBM] * 4,
        out_specs=[ANY] * 5,
        scratch_shapes=[
            pltpu.VMEM((24, WINDOW), F32),
            pltpu.VMEM((3, 6, 1, 1296), F32),
            pltpu.SMEM((8,), jnp.int32),
            pltpu.SMEM((8,), jnp.int32),
            pltpu.VMEM((SHARD, LANES), F32),
            pltpu.VMEM((SHARD, LANES), F32),
            pltpu.VMEM((PSLOT, 1, DEPTH), F32),
            pltpu.VMEM((PSLOT, 1, DEPTH), F32),
            pltpu.VMEM((2, PSLOT, 1, DEPTH), F32),
            pltpu.SemaphoreType.DMA((3,)),
            pltpu.SemaphoreType.DMA((4,)),
            pltpu.SemaphoreType.DMA((6,)),
        ],
        compiler_params=HUGE,
    )(occ_count, vir_count, amplitudes, integrals)
    got = swap_core(send)
    moved_a = ring(flat(first_v), "yy", (1, -1))
    partner = lax.ppermute(ovov, "z", [(0, 1), (1, 0), (2, 3), (3, 2)])
    home = home.reshape(2 * PROWS, LANES)
    pair, home = pl.pallas_call(
        merge_pair,
        out_shape=[shape((PAIR, LANES), F32), shape(home.shape, F32)],
        in_specs=[VMEM] * 2 + [ANY],
        out_specs=[VMEM, ANY],
        input_output_aliases={2: 1},
        compiler_params=SMALL,
    )(keep, got, home)
    home_other = swap_core(home)
    far_pair = ring(pair, "yy", (2, 2))
    quad = pl.pallas_call(
        join_pairs,
        out_shape=shape((QUAD, LANES), F32),
        in_specs=[VMEM] * 2 + [ANY],
        out_specs=VMEM,
        compiler_params=SMALL,
    )(pair, far_pair, home_other)
    (second_v,) = hold([flat(second_v)], far_pair)
    moved_b = ring(second_v, "yy", (-1, 1))

    near, far = pl.pallas_call(
        gather_four,
        out_shape=[shape((4 * PAIR, LANES), F32)] * 2,
        in_specs=[VMEM] * 4,
        out_specs=[VMEM] * 2,
        compiler_params=SMALL,
    )(quad, *[ring(quad, "xz", step) for step in SHIFTS])
    near_high, near_low, far_high, far_low = pl.pallas_call(
        split_home,
        out_shape=[shape((2 * PSLOT, DEPTH), BF16)] * 2 + [shape((2 * LANES, DEPTH), BF16)] * 2,
        in_specs=[VMEM] * 2 + [ANY],
        out_specs=[VMEM] * 4,
        compiler_params=LARGE,
        cost_estimate=pl.CostEstimate(flops=1, bytes_accessed=1, transcendentals=0),
    )(home, home_other, near)
    next_one, opposite, last_one = [ring(near, "zx", SHIFTS[at]) for at in (1, 0, 2)]
    near_blocks = [near, next_one, opposite, last_one]
    far_blocks = [far] + [ring(far, "zx", step) for step in SHIFTS]

    moved_a, moved_b = hold([moved_a, moved_b], next_one, opposite, last_one, near_high, partner)
    swapped_a, swapped_b = swap_core(moved_a), swap_core(moved_b)

    scale, cycle = pl.pallas_call(
        local_step,
        out_shape=[shape((18, 1296), F32)] * 2,
        in_specs=[HBM] * 5 + [VMEM] * 2,
        out_specs=[VMEM] * 2,
        scratch_shapes=[
            pltpu.VMEM((3, 6, 1, 1296), F32),
            pltpu.SMEM((8,), jnp.int32),
            pltpu.SMEM((8,), jnp.int32),
            pltpu.SMEM((8, 6), F32),
            pltpu.SMEM((8, 36), F32),
            pltpu.VMEM((112, 256), F32),
            pltpu.VMEM((112, 256), F32),
            pltpu.VMEM((112, 256), F32),
            pltpu.VMEM((112, 256), F32),
            pltpu.SemaphoreType.DMA((5,)),
        ],
        compiler_params=SMALL,
        cost_estimate=pl.CostEstimate(flops=100000000, bytes_accessed=1000000, transcendentals=0),
    )(occ_count, vir_count, eps_occ, eps_vir, amplitudes, ovov, partner)

    sums = [shape((144, 2 * LANES), F32)] * 3
    here_sum, below_sum, above_sum = pl.pallas_call(
        multiply_near,
        out_shape=sums,
        in_specs=[VMEM] * 10,
        out_specs=[VMEM] * 3,
        scratch_shapes=[pltpu.VMEM((16, DEPTH), F32), pltpu.VMEM((LANES, 2 * LANES), F32)],
        compiler_params=LARGE,
    )(*near_blocks, near_high, near_low, moved_a, swapped_b, moved_b, swapped_a)
    back_a = ring(below_sum, "yy", (-1, 1))
    back_b = ring(above_sum, "yy", (1, -1))
    packed = pl.pallas_call(
        multiply_far,
        out_shape=shape((32, 8, LANES), F32),
        in_specs=[VMEM] * 9,
        out_specs=VMEM,
        scratch_shapes=[pltpu.VMEM((16, DEPTH), F32)],
        compiler_params=LARGE,
    )(*far_blocks, far_high, far_low, here_sum, back_a, back_b)
    ladder = lax.all_to_all(packed, ("x", "z", "core"), 0, 0, tiled=True)
    return pl.pallas_call(
        finish,
        out_shape=shape((3, 6, 1, 1296), F32),
        in_specs=[VMEM] * 3,
        out_specs=VMEM,
        scratch_shapes=[pltpu.VMEM((24, WINDOW), F32)],
        compiler_params=SMALL,
    )(ladder, scale, cycle)


def solution(mesh):
    fine = Mesh(mesh.devices.reshape(4, 4, 4, 2), AXES)
    rows, cols = ("x", "z"), ("y", "core")
    return jax.shard_map(
        on_device,
        mesh=fine,
        in_specs=(P(rows, None, cols, None), P(cols, rows, None), P(rows, cols, None), P(), P(), P(), P()),
        out_specs=P(rows, None, cols, None),
        check_vma=False,
    )
```

```python
import jax
import jax.numpy as jnp
from jax import lax
from jax.experimental import pallas as pl
from jax.experimental.pallas import tpu as pltpu
from jax.sharding import Mesh, PartitionSpec as P

AXES = ("x", "z", "y", "core")
FIRST_STEPS = (0, 1, -1, 2)
LAST_STEPS = (0, 2, 1, -1)
LANES = 128
TILES = 11
WINDOW = TILES * LANES
SPAN = 21
DEPTH = SPAN * LANES
MAIN = 8 * TILES
SHARD = 104
PMAIN = 8 * SPAN
PAIR = 192
QUAD = 2 * PAIR
PSLOT = 88
PROWS = SPAN * PSLOT
F32 = jnp.float32
BF16 = jnp.bfloat16
ANY = pl.BlockSpec(memory_space=pl.ANY)
HBM = pl.BlockSpec(memory_space=pltpu.HBM)
VMEM = pl.BlockSpec(memory_space=pltpu.VMEM)
HUGE = pltpu.CompilerParams(vmem_limit_bytes=56 * 1024 * 1024)
SMALL = pltpu.CompilerParams(vmem_limit_bytes=8 * 1024 * 1024)
LARGE = pltpu.CompilerParams(vmem_limit_bytes=28 * 1024 * 1024)


def ring(value, axes, steps):
    pairs = []
    for x in range(4):
        for z in range(4):
            for y in range(4):
                for core in range(2):
                    here = {"x": x, "z": z, "y": y, "core": core}
                    there = dict(here)
                    there[axes[core]] = (there[axes[core]] + steps[core]) % 4
                    pairs.append(
                        tuple(((p["x"] * 4 + p["z"]) * 4 + p["y"]) * 2 + p["core"] for p in (here, there))
                    )
    return lax.ppermute(value, AXES, pairs)


def swap_core(value):
    return lax.ppermute(value, "core", [(0, 1), (1, 0)])


def places():
    return tuple(lax.axis_index(name) for name in AXES)


def lane_orbitals(shape):
    lane = lax.broadcasted_iota(jnp.int32, shape, 1)
    a = jnp.floor((lane.astype(F32) + 0.5) * (1.0 / 36.0)).astype(jnp.int32)
    return a, lane - 36 * a


def window_copy(integrals, target, sem, chip):
    start = pl.multiple_of((chip & 3) * 2560, LANES)
    return pltpu.make_async_copy(integrals.at[:, :, pl.ds(start, DEPTH)], target.at[0:81], sem)


def open_step(occ_ref, vir_ref, amp_ref, integrals, keep_out, send_out, first_out, second_out, home_out,
              wide, amp, occ, vir, keep, send, first_v, second_v, home, sems, cut_sems, out_sems):
    x, z, y, core = places()
    copies = [
        pltpu.make_async_copy(source, target, sems.at[at])
        for at, (source, target) in enumerate(((occ_ref, occ), (vir_ref, vir), (amp_ref, amp)))
    ]
    cuts = [
        window_copy(integrals, first_v, cut_sems.at[0], y + 1 + 2 * core),
        window_copy(integrals, second_v, cut_sems.at[1], y + 3 - 2 * core),
        window_copy(integrals, home.at[0], cut_sems.at[2], y),
        window_copy(integrals, home.at[1], cut_sems.at[3], y + 2),
    ]
    outs = [
        pltpu.make_async_copy(source, target, out_sems.at[at])
        for at, (source, target) in enumerate(
            (
                (first_v, first_out),
                (second_v, second_out),
                (home.at[0], home_out.at[0]),
                (home.at[1], home_out.at[1]),
                (keep, keep_out),
                (send, send_out),
            )
        )
    ]
    for copy in copies + cuts:
        copy.start()
    wide[...] = jnp.zeros_like(wide)
    for copy in copies:
        copy.wait()
    for row in range(18):
        wide[row : row + 1, 0:1296] = amp[row // 6, row % 6]
    row_place = x * 4 + z
    occ_here = occ[row_place >> 1]
    first = 3 * (row_place & 1)
    irrep = 2 * y + core
    vir_here = vir[irrep]
    a, b = lane_orbitals(wide.shape)
    row = lax.broadcasted_iota(jnp.int32, wide.shape, 0)
    i_low = (row * 43) >> 8
    j = row - 6 * i_low
    live = (a < vir_here) & (b < vir_here) & (i_low + first < occ_here) & (j < occ_here)
    moved = pltpu.roll(jnp.where(live, wide[...], 0.0), 16 * irrep, 1)

    def write(ref, half):
        for t in range(TILES):
            columns = slice(t * LANES, (t + 1) * LANES)
            ref[8 * t : 8 * t + 8, :] = moved[8 * half : 8 * half + 8, columns]
            ref[MAIN + t : MAIN + t + 1, :] = moved[16 + half : 17 + half, columns]
        ref[MAIN + TILES : SHARD, :] = jnp.zeros((SHARD - MAIN - TILES, LANES), F32)

    @pl.when(core == 0)
    def _():
        write(keep, 0)
        write(send, 1)

    @pl.when(core == 1)
    def _():
        write(keep, 1)
        write(send, 0)

    for copy in outs[4:]:
        copy.start()
    for copy, out in zip(cuts, outs):
        copy.wait()
        out.start()
    for copy in outs:
        copy.wait()


def merge_irreps(even, odd, out, at):
    gap = SPAN - TILES
    out[at : at + 8 * gap, :] = even[0 : 8 * gap, :]
    out[at + 8 * gap : at + MAIN, :] = even[8 * gap : MAIN, :] + odd[0:8, :]
    out[at + MAIN : at + PMAIN, :] = odd[8:MAIN, :]
    extra = at + PMAIN
    out[extra : extra + gap, :] = even[MAIN : MAIN + gap, :]
    out[extra + gap : extra + TILES, :] = even[MAIN + gap : MAIN + TILES, :] + odd[MAIN : MAIN + 1, :]
    out[extra + TILES : extra + SPAN, :] = odd[MAIN + 1 : MAIN + TILES, :]
    out[extra + SPAN : at + PAIR, :] = jnp.zeros((PAIR - PMAIN - SPAN, LANES), F32)


def merge_pair(keep, got, home, out, home_out):
    core = lax.axis_index("core")

    @pl.when(core == 0)
    def _():
        merge_irreps(keep, got, out, 0)

    @pl.when(core == 1)
    def _():
        merge_irreps(got, keep, out, 0)


def join_pairs(near, far, home_other, out):
    out[0:PAIR, :] = near[...]
    out[PAIR:QUAD, :] = far[...]


def gather_four(b0, b1, b2, b3, near, far):
    for at, block in enumerate((b0, b1, b2, b3)):
        near[at * PAIR : (at + 1) * PAIR, :] = block[0:PAIR, :]
        far[at * PAIR : (at + 1) * PAIR, :] = block[PAIR:QUAD, :]


def nothing(*refs):
    pass


def hold(values, *witnesses):
    kept = range(len(values))
    return pl.pallas_call(
        nothing,
        out_shape=[jax.ShapeDtypeStruct(value.shape, value.dtype) for value in values],
        in_specs=[ANY] * (len(values) + len(witnesses)),
        out_specs=[ANY] * len(values),
        input_output_aliases={at: at for at in kept},
        compiler_params=SMALL,
    )(*values, *witnesses)


def left_side(blocks, extra):
    for t in range(SPAN):
        for d, block in enumerate(blocks):
            extra[4 * d : 4 * d + 4, t * LANES : (t + 1) * LANES] = block[pl.ds(PMAIN + t, 4, stride=PAIR), :]
    rows = []
    for block in blocks:
        for e in range(4):
            rows.append(
                jnp.concatenate(
                    [block[e * PAIR + 8 * t : e * PAIR + 8 * t + 8, :] for t in range(SPAN)], axis=1
                )
            )
    return split(jnp.concatenate(rows + [extra[...]], axis=0))


def split(value):
    high = value.astype(BF16)
    return high, (value - high.astype(F32)).astype(BF16)


def rows_side(ref, first):
    return jnp.concatenate([ref[pl.ds(first + t, PSLOT, stride=SPAN), :] for t in range(SPAN)], axis=1)


def last_by_last(p, q):
    return lax.dot_general(p, q, (((1,), (1,)), ((), ())), preferred_element_type=F32)


def split_home(home, home_other, witness, near_high, near_low, far_high, far_low):
    for side, ref in enumerate((home, home_other)):
        high, low = split(rows_side(ref, 0))
        rows = slice(side * PSLOT, (side + 1) * PSLOT)
        near_high[rows, :] = high
        near_low[rows, :] = low
        high, low = split(rows_side(ref, PROWS))
        pad = jnp.zeros((LANES - PSLOT, DEPTH), BF16)
        rows = slice(side * LANES, (side + 1) * LANES)
        far_high[rows, :] = jnp.concatenate([high, pad], axis=0)
        far_low[rows, :] = jnp.concatenate([low, pad], axis=0)


def turn_sums(total, refs, turned):
    turned[...] = jnp.zeros_like(turned)
    for at, ref in enumerate(refs):
        for side in range(2):
            rows = slice((2 * at + side) * PSLOT, (2 * at + side + 1) * PSLOT)
            turned[0:PSLOT, 0:144] = total[rows, :]
            ref[:, side * LANES : (side + 1) * LANES] = turned[...].T[0:144, :]


def multiply_moved(b0, b1, b2, b3, below, below_other, above, above_other,
                   below_sum, above_sum, high_out, low_out, extra, turned):
    high, low = left_side((b0, b1, b2, b3), extra)
    high_out[...] = high
    low_out[...] = low
    sides = [rows_side(ref, 0) for ref in (below, below_other, above, above_other)]
    v_high, v_low = split(jnp.concatenate(sides, axis=0))
    total = last_by_last(v_high, high) + (last_by_last(v_low, high) + last_by_last(v_high, low))
    turn_sums(total, (below_sum, above_sum), turned)


def multiply_home(high, low, v_high, v_low, below_sum, here_sum, turned):
    total = last_by_last(v_high[...], high[...]) + (
        last_by_last(v_low[...], high[...]) + last_by_last(v_high[...], low[...])
    )
    turn_sums(total, (here_sum,), turned)


def multiply_far(b0, b1, b2, b3, v_high, v_low, here_sum, back_a, back_b, out, extra):
    x, z, y, core = places()
    high, low = left_side((b0, b1, b2, b3), extra)
    partial = here_sum[...] + back_a[...] + back_b[...]
    row = lax.broadcasted_iota(jnp.int32, (8, LANES), 0)
    lane = lax.broadcasted_iota(jnp.int32, (8, LANES), 1)
    total = partial + (
        last_by_last(high, v_high[...]) + (last_by_last(low, v_high[...]) + last_by_last(high, v_low[...]))
    )
    for side in range(2):
        columns = slice(side * LANES, (side + 1) * LANES)
        last = total[128:144, columns]
        last_a = pltpu.roll(last, 81, 1)
        last_b = pltpu.roll(last, 34, 1)
        core_there = core if side == 0 else 1 - core
        for d in range(4):
            for e in range(4):
                s = 4 * d + e
                x_step = jnp.where(core == 0, FIRST_STEPS[e], LAST_STEPS[d])
                z_step = jnp.where(core == 0, LAST_STEPS[d], FIRST_STEPS[e])
                there = ((x - x_step) & 3) * 4 + ((z - z_step) & 3)
                main = total[8 * s : 8 * s + 8, columns]
                tail = jnp.where(row == 0, last_a[s : s + 1, :], last_b[s : s + 1, :])
                out[there * 2 + core_there] = jnp.where(lane < 81, main, tail)


def local_step(occ_ref, vir_ref, eps_occ_ref, eps_vir_ref, amp_ref, ovov, partner,
               scale, cycle, amp, occ, vir, eps_occ, eps_vir, left_a, left_b, panel_a, panel_b, sems):
    x, z, y, core = places()
    copies = [
        pltpu.make_async_copy(source, target, sems.at[at])
        for at, (source, target) in enumerate(
            ((occ_ref, occ), (vir_ref, vir), (eps_occ_ref, eps_occ), (eps_vir_ref, eps_vir), (amp_ref, amp))
        )
    ]
    for copy in copies:
        copy.start()
    panel_a[...] = jnp.zeros_like(panel_a)
    panel_b[...] = jnp.zeros_like(panel_b)
    left_a[...] = jnp.zeros_like(left_a)
    left_b[...] = jnp.zeros_like(left_b)
    lower = (z & 1) == 0
    for r in range(108):
        own, other = ovov[r], partner[r]
        panel_a[r : r + 1, 0:216] = jnp.where(lower, own, other)
        panel_b[r : r + 1, 0:216] = jnp.where(lower, other, own)
    for copy in copies:
        copy.wait()
    row_place = x * 4 + z
    shell = row_place >> 1
    first = 3 * (row_place & 1)
    irrep = 2 * y + core
    a, b = lane_orbitals((1, 1296))
    energy_a = jnp.zeros((1, 1296), F32)
    energy_b = jnp.zeros((1, 1296), F32)
    for slot in range(36):
        value = eps_vir[irrep, slot]
        energy_a = jnp.where(a == slot, value, energy_a)
        energy_b = jnp.where(b == slot, value, energy_b)
    lane_live = (a < vir[irrep]) & (b < vir[irrep])
    occ_here = occ[shell]
    for r in range(18):
        low, k = r // 6, r % 6
        i = first + low
        here = lane_live & (i < occ_here) & (k < occ_here)
        gap = eps_occ[shell, i] + eps_occ[shell, k] - energy_a - energy_b
        scale[r : r + 1, :] = jnp.where(here, 1.0, 0.0) / gap
        live = jnp.where(here, amp[low, k], 0.0)
        left, column = (left_a, 36 * k) if k < 3 else (left_b, 36 * (k - 3))
        for slot in range(36):
            left[36 * low + slot : 36 * low + slot + 1, column : column + 36] = live[
                :, 36 * slot : 36 * slot + 36
            ]
    dot = lambda p, q: jnp.dot(p, q, preferred_element_type=F32)
    total = None
    for left, panel in ((left_a, panel_a), (left_b, panel_b)):
        p_high, p_low = split(left[:, 0:112])
        q_high, q_low = split(panel[...])
        part = dot(p_high, q_high) + (dot(p_low, q_high) + dot(p_high, q_low))
        total = part if total is None else total + part
    for low in range(3):
        for j in range(6):
            r = 6 * low + j
            for slot in range(36):
                cycle[r : r + 1, 36 * slot : 36 * slot + 36] = total[
                    36 * low + slot : 36 * low + slot + 1, 36 * j : 36 * j + 36
                ]


def finish(sums, scale, cycle, out, wide):
    wide[...] = jnp.zeros_like(wide)
    lane8 = lax.broadcasted_iota(jnp.int32, (1, LANES), 1)
    lane = lax.broadcasted_iota(jnp.int32, (24, LANES), 1)
    for r in range(16):
        mains, lasts = [], []
        for core in range(2):
            block = sums[2 * r + core]
            mains.append(block)
            lasts.append(
                jnp.where(lane8 < 47, pltpu.roll(block, 47, 1)[0:1, :], pltpu.roll(block, 94, 1)[1:2, :])
            )
        stack = jnp.concatenate(mains + lasts + [jnp.zeros((6, LANES), F32)], axis=0)
        tile, start = divmod(81 * r, LANES)
        turned = pltpu.roll(stack, start, 1) if start else stack
        here = slice(tile * LANES, (tile + 1) * LANES)
        wide[:, here] = jnp.where((lane >= start) & (lane < start + 81), turned, wide[:, here])
        if start + 81 > LANES:
            after = slice((tile + 1) * LANES, (tile + 2) * LANES)
            wide[:, after] = jnp.where(lane < start + 81 - LANES, turned, wide[:, after])
    total = (wide[0:18, 0:1296] + cycle[...]) * scale[...]
    for r in range(18):
        out[r // 6, r % 6] = total[r : r + 1, :]


def on_device(amplitudes, vvvv, ovov, eps_occ, eps_vir, occ_count, vir_count):
    x, z, y, core = places()
    shape = jax.ShapeDtypeStruct
    integrals = vvvv.reshape(81, 1, 10368)
    window = shape((PSLOT, 1, DEPTH), F32)
    flat = lambda value: value.reshape(PROWS, LANES)
    keep, send, first_v, second_v, home = pl.pallas_call(
        open_step,
        out_shape=[shape((SHARD, LANES), F32)] * 2 + [window] * 2
        + [shape((2, PSLOT, 1, DEPTH), F32)],
        in_specs=[HBM] * 4,
        out_specs=[ANY] * 5,
        scratch_shapes=[
            pltpu.VMEM((24, WINDOW), F32),
            pltpu.VMEM((3, 6, 1, 1296), F32),
            pltpu.SMEM((8,), jnp.int32),
            pltpu.SMEM((8,), jnp.int32),
            pltpu.VMEM((SHARD, LANES), F32),
            pltpu.VMEM((SHARD, LANES), F32),
            pltpu.VMEM((PSLOT, 1, DEPTH), F32),
            pltpu.VMEM((PSLOT, 1, DEPTH), F32),
            pltpu.VMEM((2, PSLOT, 1, DEPTH), F32),
            pltpu.SemaphoreType.DMA((3,)),
            pltpu.SemaphoreType.DMA((4,)),
            pltpu.SemaphoreType.DMA((6,)),
        ],
        compiler_params=HUGE,
    )(occ_count, vir_count, amplitudes, integrals)
    got = swap_core(send)
    moved_a = ring(flat(first_v), "yy", (1, -1))
    partner = lax.ppermute(ovov, "z", [(0, 1), (1, 0), (2, 3), (3, 2)])
    home = home.reshape(2 * PROWS, LANES)
    pair, home = pl.pallas_call(
        merge_pair,
        out_shape=[shape((PAIR, LANES), F32), shape(home.shape, F32)],
        in_specs=[VMEM] * 2 + [ANY],
        out_specs=[VMEM, ANY],
        input_output_aliases={2: 1},
        compiler_params=SMALL,
    )(keep, got, home)
    home_other = swap_core(home)
    far_pair = ring(pair, "yy", (2, 2))
    quad = pl.pallas_call(
        join_pairs,
        out_shape=shape((QUAD, LANES), F32),
        in_specs=[VMEM] * 2 + [ANY],
        out_specs=VMEM,
        compiler_params=SMALL,
    )(pair, far_pair, home_other)
    (second_v,) = hold([flat(second_v)], far_pair)
    moved_b = ring(second_v, "yy", (-1, 1))

    near, far = pl.pallas_call(
        gather_four,
        out_shape=[shape((4 * PAIR, LANES), F32)] * 2,
        in_specs=[VMEM] * 4,
        out_specs=[VMEM] * 2,
        compiler_params=SMALL,
    )(quad, *[ring(quad, "xz", (step, step)) for step in FIRST_STEPS[1:]])
    near_high, near_low, far_high, far_low = pl.pallas_call(
        split_home,
        out_shape=[shape((2 * PSLOT, DEPTH), BF16)] * 2 + [shape((2 * LANES, DEPTH), BF16)] * 2,
        in_specs=[VMEM] * 2 + [ANY],
        out_specs=[VMEM] * 4,
        compiler_params=LARGE,
        cost_estimate=pl.CostEstimate(flops=1, bytes_accessed=1, transcendentals=0),
    )(home, home_other, near)
    near_blocks = [near] + [ring(near, "zx", (step, step)) for step in LAST_STEPS[1:]]
    far_blocks = [far] + [ring(far, "zx", (step, step)) for step in LAST_STEPS[1:]]

    moved_a, moved_b = hold([moved_a, moved_b], *near_blocks[1:], near_high, partner)
    swapped_a, swapped_b = swap_core(moved_a), swap_core(moved_b)

    scale, cycle = pl.pallas_call(
        local_step,
        out_shape=[shape((18, 1296), F32)] * 2,
        in_specs=[HBM] * 5 + [VMEM] * 2,
        out_specs=[VMEM] * 2,
        scratch_shapes=[
            pltpu.VMEM((3, 6, 1, 1296), F32),
            pltpu.SMEM((8,), jnp.int32),
            pltpu.SMEM((8,), jnp.int32),
            pltpu.SMEM((8, 6), F32),
            pltpu.SMEM((8, 36), F32),
            pltpu.VMEM((112, 256), F32),
            pltpu.VMEM((112, 256), F32),
            pltpu.VMEM((112, 256), F32),
            pltpu.VMEM((112, 256), F32),
            pltpu.SemaphoreType.DMA((5,)),
        ],
        compiler_params=SMALL,
        cost_estimate=pl.CostEstimate(flops=100000000, bytes_accessed=1000000, transcendentals=0),
    )(occ_count, vir_count, eps_occ, eps_vir, amplitudes, ovov, partner)

    sums = shape((144, 2 * LANES), F32)
    left = shape((144, DEPTH), BF16)
    below_sum, above_sum, high, low = pl.pallas_call(
        multiply_moved,
        out_shape=[sums, sums, left, left],
        in_specs=[VMEM] * 8,
        out_specs=[VMEM] * 4,
        scratch_shapes=[pltpu.VMEM((16, DEPTH), F32), pltpu.VMEM((LANES, 2 * LANES), F32)],
        compiler_params=LARGE,
    )(*near_blocks, moved_a, swapped_b, moved_b, swapped_a)
    back_a = ring(below_sum, "yy", (-1, 1))
    back_b = ring(above_sum, "yy", (1, -1))
    here_sum = pl.pallas_call(
        multiply_home,
        out_shape=sums,
        in_specs=[VMEM] * 4 + [ANY],
        out_specs=VMEM,
        scratch_shapes=[pltpu.VMEM((LANES, 2 * LANES), F32)],
        compiler_params=LARGE,
    )(high, low, near_high, near_low, below_sum)
    packed = pl.pallas_call(
        multiply_far,
        out_shape=shape((32, 8, LANES), F32),
        in_specs=[VMEM] * 9,
        out_specs=VMEM,
        scratch_shapes=[pltpu.VMEM((16, DEPTH), F32)],
        compiler_params=LARGE,
    )(*far_blocks, far_high, far_low, here_sum, back_a, back_b)
    ladder = lax.all_to_all(packed, ("x", "z", "core"), 0, 0, tiled=True)
    return pl.pallas_call(
        finish,
        out_shape=shape((3, 6, 1, 1296), F32),
        in_specs=[VMEM] * 3,
        out_specs=VMEM,
        scratch_shapes=[pltpu.VMEM((24, WINDOW), F32)],
        compiler_params=SMALL,
    )(ladder, scale, cycle)


def solution(mesh):
    fine = Mesh(mesh.devices.reshape(4, 4, 4, 2), AXES)
    rows, cols = ("x", "z"), ("y", "core")
    return jax.shard_map(
        on_device,
        mesh=fine,
        in_specs=(P(rows, None, cols, None), P(cols, rows, None), P(rows, cols, None), P(), P(), P(), P()),
        out_specs=P(rows, None, cols, None),
        check_vma=False,
    )
```

```python
import jax
import jax.numpy as jnp
from jax import lax
from jax.experimental import pallas as pl
from jax.experimental.pallas import tpu as pltpu
from jax.sharding import Mesh, PartitionSpec as P

AXES = ("x", "z", "y", "core")
FIRST_STEPS = (0, 1, -1, 2)
LAST_STEPS = (0, 2, 1, -1)
LANES = 128
TILES = 11
WINDOW = TILES * LANES
SPAN = 21
DEPTH = SPAN * LANES
MAIN = 8 * TILES
SHARD = 104
PMAIN = 8 * SPAN
PAIR = 192
QUAD = 2 * PAIR
PSLOT = 88
PROWS = SPAN * PSLOT
F32 = jnp.float32
BF16 = jnp.bfloat16
ANY = pl.BlockSpec(memory_space=pl.ANY)
HBM = pl.BlockSpec(memory_space=pltpu.HBM)
VMEM = pl.BlockSpec(memory_space=pltpu.VMEM)
HUGE = pltpu.CompilerParams(vmem_limit_bytes=56 * 1024 * 1024)
SMALL = pltpu.CompilerParams(vmem_limit_bytes=8 * 1024 * 1024)
LARGE = pltpu.CompilerParams(vmem_limit_bytes=28 * 1024 * 1024)


def ring(value, axes, steps):
    pairs = []
    for x in range(4):
        for z in range(4):
            for y in range(4):
                for core in range(2):
                    here = {"x": x, "z": z, "y": y, "core": core}
                    there = dict(here)
                    there[axes[core]] = (there[axes[core]] + steps[core]) % 4
                    pairs.append(
                        tuple(((p["x"] * 4 + p["z"]) * 4 + p["y"]) * 2 + p["core"] for p in (here, there))
                    )
    return lax.ppermute(value, AXES, pairs)


def swap_core(value):
    return lax.ppermute(value, "core", [(0, 1), (1, 0)])


def places():
    return tuple(lax.axis_index(name) for name in AXES)


def lane_orbitals(shape):
    lane = lax.broadcasted_iota(jnp.int32, shape, 1)
    a = jnp.floor((lane.astype(F32) + 0.5) * (1.0 / 36.0)).astype(jnp.int32)
    return a, lane - 36 * a


def window_copy(integrals, target, sem, chip):
    start = pl.multiple_of((chip & 3) * 2560, LANES)
    return pltpu.make_async_copy(integrals.at[:, :, pl.ds(start, DEPTH)], target.at[0:81], sem)


def open_step(occ_ref, vir_ref, amp_ref, integrals, keep_out, send_out, first_out, second_out, home_out,
              wide, amp, occ, vir, keep, send, first_v, second_v, home, sems, cut_sems, out_sems):
    x, z, y, core = places()
    copies = [
        pltpu.make_async_copy(source, target, sems.at[at])
        for at, (source, target) in enumerate(((occ_ref, occ), (vir_ref, vir), (amp_ref, amp)))
    ]
    cuts = [
        window_copy(integrals, first_v, cut_sems.at[0], y + 1 + 2 * core),
        window_copy(integrals, second_v, cut_sems.at[1], y + 3 - 2 * core),
        window_copy(integrals, home.at[0], cut_sems.at[2], y),
        window_copy(integrals, home.at[1], cut_sems.at[3], y + 2),
    ]
    outs = [
        pltpu.make_async_copy(source, target, out_sems.at[at])
        for at, (source, target) in enumerate(
            (
                (first_v, first_out),
                (second_v, second_out),
                (home.at[0], home_out.at[0]),
                (home.at[1], home_out.at[1]),
                (keep, keep_out),
                (send, send_out),
            )
        )
    ]
    for copy in copies + cuts:
        copy.start()
    wide[...] = jnp.zeros_like(wide)
    for copy in copies:
        copy.wait()
    for row in range(18):
        wide[row : row + 1, 0:1296] = amp[row // 6, row % 6]
    row_place = x * 4 + z
    occ_here = occ[row_place >> 1]
    first = 3 * (row_place & 1)
    irrep = 2 * y + core
    vir_here = vir[irrep]
    a, b = lane_orbitals(wide.shape)
    row = lax.broadcasted_iota(jnp.int32, wide.shape, 0)
    i_low = (row * 43) >> 8
    j = row - 6 * i_low
    live = (a < vir_here) & (b < vir_here) & (i_low + first < occ_here) & (j < occ_here)
    moved = pltpu.roll(jnp.where(live, wide[...], 0.0), 16 * irrep, 1)

    def write(ref, half):
        for t in range(TILES):
            columns = slice(t * LANES, (t + 1) * LANES)
            ref[8 * t : 8 * t + 8, :] = moved[8 * half : 8 * half + 8, columns]
            ref[MAIN + t : MAIN + t + 1, :] = moved[16 + half : 17 + half, columns]
        ref[MAIN + TILES : SHARD, :] = jnp.zeros((SHARD - MAIN - TILES, LANES), F32)

    @pl.when(core == 0)
    def _():
        write(keep, 0)
        write(send, 1)

    @pl.when(core == 1)
    def _():
        write(keep, 1)
        write(send, 0)

    for copy in outs[4:]:
        copy.start()
    for copy, out in zip(cuts, outs):
        copy.wait()
        out.start()
    for copy in outs:
        copy.wait()


def merge_irreps(even, odd, out, at):
    gap = SPAN - TILES
    out[at : at + 8 * gap, :] = even[0 : 8 * gap, :]
    out[at + 8 * gap : at + MAIN, :] = even[8 * gap : MAIN, :] + odd[0:8, :]
    out[at + MAIN : at + PMAIN, :] = odd[8:MAIN, :]
    extra = at + PMAIN
    out[extra : extra + gap, :] = even[MAIN : MAIN + gap, :]
    out[extra + gap : extra + TILES, :] = even[MAIN + gap : MAIN + TILES, :] + odd[MAIN : MAIN + 1, :]
    out[extra + TILES : extra + SPAN, :] = odd[MAIN + 1 : MAIN + TILES, :]
    out[extra + SPAN : at + PAIR, :] = jnp.zeros((PAIR - PMAIN - SPAN, LANES), F32)


def merge_pair(keep, got, home, out, home_out):
    core = lax.axis_index("core")

    @pl.when(core == 0)
    def _():
        merge_irreps(keep, got, out, 0)

    @pl.when(core == 1)
    def _():
        merge_irreps(got, keep, out, 0)


def join_pairs(near, far, home_other, out):
    out[0:PAIR, :] = near[...]
    out[PAIR:QUAD, :] = far[...]


def gather_four(b0, b1, b2, b3, near, far):
    for at, block in enumerate((b0, b1, b2, b3)):
        near[at * PAIR : (at + 1) * PAIR, :] = block[0:PAIR, :]
        far[at * PAIR : (at + 1) * PAIR, :] = block[PAIR:QUAD, :]


def nothing(*refs):
    pass


def relay(value, witness, out):
    out[...] = value[...]


def hold(values, *witnesses):
    kept = range(len(values))
    return pl.pallas_call(
        nothing,
        out_shape=[jax.ShapeDtypeStruct(value.shape, value.dtype) for value in values],
        in_specs=[ANY] * (len(values) + len(witnesses)),
        out_specs=[ANY] * len(values),
        input_output_aliases={at: at for at in kept},
        compiler_params=SMALL,
    )(*values, *witnesses)


def left_side(blocks, extra):
    for t in range(SPAN):
        for d, block in enumerate(blocks):
            extra[4 * d : 4 * d + 4, t * LANES : (t + 1) * LANES] = block[pl.ds(PMAIN + t, 4, stride=PAIR), :]
    rows = []
    for block in blocks:
        for e in range(4):
            rows.append(
                jnp.concatenate(
                    [block[e * PAIR + 8 * t : e * PAIR + 8 * t + 8, :] for t in range(SPAN)], axis=1
                )
            )
    return split(jnp.concatenate(rows + [extra[...]], axis=0))


def split(value):
    high = value.astype(BF16)
    return high, (value - high.astype(F32)).astype(BF16)


def rows_side(ref, first):
    return jnp.concatenate([ref[pl.ds(first + t, PSLOT, stride=SPAN), :] for t in range(SPAN)], axis=1)


def last_by_last(p, q):
    return lax.dot_general(p, q, (((1,), (1,)), ((), ())), preferred_element_type=F32)


def split_home(home, home_other, witness, near_high, near_low, far_high, far_low):
    for side, ref in enumerate((home, home_other)):
        high, low = split(rows_side(ref, 0))
        rows = slice(side * PSLOT, (side + 1) * PSLOT)
        near_high[rows, :] = high
        near_low[rows, :] = low
        high, low = split(rows_side(ref, PROWS))
        pad = jnp.zeros((LANES - PSLOT, DEPTH), BF16)
        rows = slice(side * LANES, (side + 1) * LANES)
        far_high[rows, :] = jnp.concatenate([high, pad], axis=0)
        far_low[rows, :] = jnp.concatenate([low, pad], axis=0)


def turn_sums(total, refs, turned):
    turned[...] = jnp.zeros_like(turned)
    for at, ref in enumerate(refs):
        for side in range(2):
            rows = slice((2 * at + side) * PSLOT, (2 * at + side + 1) * PSLOT)
            turned[0:PSLOT, 0:144] = total[rows, :]
            ref[:, side * LANES : (side + 1) * LANES] = turned[...].T[0:144, :]


def multiply_moved(b0, b1, b2, b3, below, below_other, above, above_other,
                   below_sum, above_sum, high_out, low_out, extra, turned):
    high, low = left_side((b0, b1, b2, b3), extra)
    high_out[...] = high
    low_out[...] = low
    sides = [rows_side(ref, 0) for ref in (below, below_other, above, above_other)]
    v_high, v_low = split(jnp.concatenate(sides, axis=0))
    total = last_by_last(v_high, high) + (last_by_last(v_low, high) + last_by_last(v_high, low))
    turn_sums(total, (below_sum, above_sum), turned)


def multiply_home(high, low, v_high, v_low, below_sum, here_sum, turned):
    total = last_by_last(v_high[...], high[...]) + (
        last_by_last(v_low[...], high[...]) + last_by_last(v_high[...], low[...])
    )
    turn_sums(total, (here_sum,), turned)


def multiply_far(b0, b1, b2, b3, v_high, v_low, here_sum, back_a, back_b, out, extra):
    x, z, y, core = places()
    high, low = left_side((b0, b1, b2, b3), extra)
    partial = here_sum[...] + back_a[...] + back_b[...]
    row = lax.broadcasted_iota(jnp.int32, (8, LANES), 0)
    lane = lax.broadcasted_iota(jnp.int32, (8, LANES), 1)
    total = partial + (
        last_by_last(high, v_high[...]) + (last_by_last(low, v_high[...]) + last_by_last(high, v_low[...]))
    )
    for side in range(2):
        columns = slice(side * LANES, (side + 1) * LANES)
        last = total[128:144, columns]
        last_a = pltpu.roll(last, 81, 1)
        last_b = pltpu.roll(last, 34, 1)
        core_there = core if side == 0 else 1 - core
        for d in range(4):
            for e in range(4):
                s = 4 * d + e
                x_step = jnp.where(core == 0, FIRST_STEPS[e], LAST_STEPS[d])
                z_step = jnp.where(core == 0, LAST_STEPS[d], FIRST_STEPS[e])
                there = ((x - x_step) & 3) * 4 + ((z - z_step) & 3)
                main = total[8 * s : 8 * s + 8, columns]
                tail = jnp.where(row == 0, last_a[s : s + 1, :], last_b[s : s + 1, :])
                out[there * 2 + core_there] = jnp.where(lane < 81, main, tail)


def local_step(occ_ref, vir_ref, eps_occ_ref, eps_vir_ref, amp_ref, ovov, partner,
               scale, cycle, amp, occ, vir, eps_occ, eps_vir, left_a, left_b, panel_a, panel_b, sems):
    x, z, y, core = places()
    copies = [
        pltpu.make_async_copy(source, target, sems.at[at])
        for at, (source, target) in enumerate(
            ((occ_ref, occ), (vir_ref, vir), (eps_occ_ref, eps_occ), (eps_vir_ref, eps_vir), (amp_ref, amp))
        )
    ]
    for copy in copies:
        copy.start()
    panel_a[...] = jnp.zeros_like(panel_a)
    panel_b[...] = jnp.zeros_like(panel_b)
    left_a[...] = jnp.zeros_like(left_a)
    left_b[...] = jnp.zeros_like(left_b)
    lower = (z & 1) == 0
    for r in range(108):
        own, other = ovov[r], partner[r]
        panel_a[r : r + 1, 0:216] = jnp.where(lower, own, other)
        panel_b[r : r + 1, 0:216] = jnp.where(lower, other, own)
    for copy in copies:
        copy.wait()
    row_place = x * 4 + z
    shell = row_place >> 1
    first = 3 * (row_place & 1)
    irrep = 2 * y + core
    a, b = lane_orbitals((1, 1296))
    energy_a = jnp.zeros((1, 1296), F32)
    energy_b = jnp.zeros((1, 1296), F32)
    for slot in range(36):
        value = eps_vir[irrep, slot]
        energy_a = jnp.where(a == slot, value, energy_a)
        energy_b = jnp.where(b == slot, value, energy_b)
    lane_live = (a < vir[irrep]) & (b < vir[irrep])
    occ_here = occ[shell]
    for r in range(18):
        low, k = r // 6, r % 6
        i = first + low
        here = lane_live & (i < occ_here) & (k < occ_here)
        gap = eps_occ[shell, i] + eps_occ[shell, k] - energy_a - energy_b
        scale[r : r + 1, :] = jnp.where(here, 1.0, 0.0) / gap
        live = jnp.where(here, amp[low, k], 0.0)
        left, column = (left_a, 36 * k) if k < 3 else (left_b, 36 * (k - 3))
        for slot in range(36):
            left[36 * low + slot : 36 * low + slot + 1, column : column + 36] = live[
                :, 36 * slot : 36 * slot + 36
            ]
    dot = lambda p, q: jnp.dot(p, q, preferred_element_type=F32)
    total = None
    for left, panel in ((left_a, panel_a), (left_b, panel_b)):
        p_high, p_low = split(left[:, 0:112])
        q_high, q_low = split(panel[...])
        part = dot(p_high, q_high) + (dot(p_low, q_high) + dot(p_high, q_low))
        total = part if total is None else total + part
    for low in range(3):
        for j in range(6):
            r = 6 * low + j
            for slot in range(36):
                cycle[r : r + 1, 36 * slot : 36 * slot + 36] = total[
                    36 * low + slot : 36 * low + slot + 1, 36 * j : 36 * j + 36
                ]


def finish(sums, scale, cycle, out, wide):
    wide[...] = jnp.zeros_like(wide)
    lane8 = lax.broadcasted_iota(jnp.int32, (1, LANES), 1)
    lane = lax.broadcasted_iota(jnp.int32, (24, LANES), 1)
    for r in range(16):
        mains, lasts = [], []
        for core in range(2):
            block = sums[2 * r + core]
            mains.append(block)
            lasts.append(
                jnp.where(lane8 < 47, pltpu.roll(block, 47, 1)[0:1, :], pltpu.roll(block, 94, 1)[1:2, :])
            )
        stack = jnp.concatenate(mains + lasts + [jnp.zeros((6, LANES), F32)], axis=0)
        tile, start = divmod(81 * r, LANES)
        turned = pltpu.roll(stack, start, 1) if start else stack
        here = slice(tile * LANES, (tile + 1) * LANES)
        wide[:, here] = jnp.where((lane >= start) & (lane < start + 81), turned, wide[:, here])
        if start + 81 > LANES:
            after = slice((tile + 1) * LANES, (tile + 2) * LANES)
            wide[:, after] = jnp.where(lane < start + 81 - LANES, turned, wide[:, after])
    total = (wide[0:18, 0:1296] + cycle[...]) * scale[...]
    for r in range(18):
        out[r // 6, r % 6] = total[r : r + 1, :]


def on_device(amplitudes, vvvv, ovov, eps_occ, eps_vir, occ_count, vir_count):
    x, z, y, core = places()
    shape = jax.ShapeDtypeStruct
    integrals = vvvv.reshape(81, 1, 10368)
    window = shape((PSLOT, 1, DEPTH), F32)
    flat = lambda value: value.reshape(PROWS, LANES)
    keep, send, first_v, second_v, home = pl.pallas_call(
        open_step,
        out_shape=[shape((SHARD, LANES), F32)] * 2 + [window] * 2
        + [shape((2, PSLOT, 1, DEPTH), F32)],
        in_specs=[HBM] * 4,
        out_specs=[ANY] * 5,
        scratch_shapes=[
            pltpu.VMEM((24, WINDOW), F32),
            pltpu.VMEM((3, 6, 1, 1296), F32),
            pltpu.SMEM((8,), jnp.int32),
            pltpu.SMEM((8,), jnp.int32),
            pltpu.VMEM((SHARD, LANES), F32),
            pltpu.VMEM((SHARD, LANES), F32),
            pltpu.VMEM((PSLOT, 1, DEPTH), F32),
            pltpu.VMEM((PSLOT, 1, DEPTH), F32),
            pltpu.VMEM((2, PSLOT, 1, DEPTH), F32),
            pltpu.SemaphoreType.DMA((3,)),
            pltpu.SemaphoreType.DMA((4,)),
            pltpu.SemaphoreType.DMA((6,)),
        ],
        compiler_params=HUGE,
    )(occ_count, vir_count, amplitudes, integrals)
    got = swap_core(send)
    moved_a = ring(flat(first_v), "yy", (1, -1))
    home = home.reshape(2 * PROWS, LANES)
    pair, home = pl.pallas_call(
        merge_pair,
        out_shape=[shape((PAIR, LANES), F32), shape(home.shape, F32)],
        in_specs=[VMEM] * 2 + [ANY],
        out_specs=[VMEM, ANY],
        input_output_aliases={2: 1},
        compiler_params=SMALL,
    )(keep, got, home)
    home_other = swap_core(home)
    far_pair = ring(pair, "yy", (2, 2))
    quad = pl.pallas_call(
        join_pairs,
        out_shape=shape((QUAD, LANES), F32),
        in_specs=[VMEM] * 2 + [ANY],
        out_specs=VMEM,
        compiler_params=SMALL,
    )(pair, far_pair, home_other)
    (second_v,) = hold([flat(second_v)], far_pair)
    moved_b = ring(second_v, "yy", (-1, 1))

    near, far = pl.pallas_call(
        gather_four,
        out_shape=[shape((4 * PAIR, LANES), F32)] * 2,
        in_specs=[VMEM] * 4,
        out_specs=[VMEM] * 2,
        compiler_params=SMALL,
    )(quad, *[ring(quad, "xz", (step, step)) for step in FIRST_STEPS[1:]])
    near_high, near_low, far_high, far_low = pl.pallas_call(
        split_home,
        out_shape=[shape((2 * PSLOT, DEPTH), BF16)] * 2 + [shape((2 * LANES, DEPTH), BF16)] * 2,
        in_specs=[VMEM] * 2 + [ANY],
        out_specs=[VMEM] * 4,
        compiler_params=LARGE,
        cost_estimate=pl.CostEstimate(flops=1, bytes_accessed=1, transcendentals=0),
    )(home, home_other, near)
    panel = pl.pallas_call(
        relay,
        out_shape=shape(ovov.shape, F32),
        in_specs=[VMEM, ANY],
        out_specs=VMEM,
        compiler_params=SMALL,
        cost_estimate=pl.CostEstimate(flops=1, bytes_accessed=1, transcendentals=0),
    )(ovov, near_high)
    partner = lax.ppermute(panel, "z", [(0, 1), (1, 0), (2, 3), (3, 2)])
    near_blocks = [near] + [ring(near, "zx", (step, step)) for step in LAST_STEPS[1:]]
    far_blocks = [far] + [ring(far, "zx", (step, step)) for step in LAST_STEPS[1:]]

    moved_a, moved_b = hold([moved_a, moved_b], *near_blocks[1:], near_high, partner)
    swapped_a, swapped_b = swap_core(moved_a), swap_core(moved_b)

    scale, cycle = pl.pallas_call(
        local_step,
        out_shape=[shape((18, 1296), F32)] * 2,
        in_specs=[HBM] * 5 + [VMEM] * 2,
        out_specs=[VMEM] * 2,
        scratch_shapes=[
            pltpu.VMEM((3, 6, 1, 1296), F32),
            pltpu.SMEM((8,), jnp.int32),
            pltpu.SMEM((8,), jnp.int32),
            pltpu.SMEM((8, 6), F32),
            pltpu.SMEM((8, 36), F32),
            pltpu.VMEM((112, 256), F32),
            pltpu.VMEM((112, 256), F32),
            pltpu.VMEM((112, 256), F32),
            pltpu.VMEM((112, 256), F32),
            pltpu.SemaphoreType.DMA((5,)),
        ],
        compiler_params=SMALL,
        cost_estimate=pl.CostEstimate(flops=100000000, bytes_accessed=1000000, transcendentals=0),
    )(occ_count, vir_count, eps_occ, eps_vir, amplitudes, panel, partner)

    sums = shape((144, 2 * LANES), F32)
    left = shape((144, DEPTH), BF16)
    below_sum, above_sum, high, low = pl.pallas_call(
        multiply_moved,
        out_shape=[sums, sums, left, left],
        in_specs=[VMEM] * 8,
        out_specs=[VMEM] * 4,
        scratch_shapes=[pltpu.VMEM((16, DEPTH), F32), pltpu.VMEM((LANES, 2 * LANES), F32)],
        compiler_params=LARGE,
    )(*near_blocks, moved_a, swapped_b, moved_b, swapped_a)
    back_a = ring(below_sum, "yy", (-1, 1))
    back_b = ring(above_sum, "yy", (1, -1))
    here_sum = pl.pallas_call(
        multiply_home,
        out_shape=sums,
        in_specs=[VMEM] * 4 + [ANY],
        out_specs=VMEM,
        scratch_shapes=[pltpu.VMEM((LANES, 2 * LANES), F32)],
        compiler_params=LARGE,
    )(high, low, near_high, near_low, below_sum)
    packed = pl.pallas_call(
        multiply_far,
        out_shape=shape((32, 8, LANES), F32),
        in_specs=[VMEM] * 9,
        out_specs=VMEM,
        scratch_shapes=[pltpu.VMEM((16, DEPTH), F32)],
        compiler_params=LARGE,
    )(*far_blocks, far_high, far_low, here_sum, back_a, back_b)
    ladder = lax.all_to_all(packed, ("x", "z", "core"), 0, 0, tiled=True)
    return pl.pallas_call(
        finish,
        out_shape=shape((3, 6, 1, 1296), F32),
        in_specs=[VMEM] * 3,
        out_specs=VMEM,
        scratch_shapes=[pltpu.VMEM((24, WINDOW), F32)],
        compiler_params=SMALL,
    )(ladder, scale, cycle)


def solution(mesh):
    fine = Mesh(mesh.devices.reshape(4, 4, 4, 2), AXES)
    rows, cols = ("x", "z"), ("y", "core")
    return jax.shard_map(
        on_device,
        mesh=fine,
        in_specs=(P(rows, None, cols, None), P(cols, rows, None), P(rows, cols, None), P(), P(), P(), P()),
        out_specs=P(rows, None, cols, None),
        check_vma=False,
    )
```

```python
import jax
import jax.numpy as jnp
from jax import lax
from jax.experimental import pallas as pl
from jax.experimental.pallas import tpu as pltpu
from jax.sharding import Mesh, PartitionSpec as P

AXES = ("x", "z", "y", "core")
FIRST_STEPS = (0, 1, -1, 2)
LAST_STEPS = (0, 2, 1, -1)
LANES = 128
TILES = 11
WINDOW = TILES * LANES
SPAN = 21
DEPTH = SPAN * LANES
MAIN = 8 * TILES
SHARD = 104
PMAIN = 8 * SPAN
PAIR = 192
QUAD = 2 * PAIR
PSLOT = 88
PROWS = SPAN * PSLOT
F32 = jnp.float32
BF16 = jnp.bfloat16
ANY = pl.BlockSpec(memory_space=pl.ANY)
HBM = pl.BlockSpec(memory_space=pltpu.HBM)
VMEM = pl.BlockSpec(memory_space=pltpu.VMEM)
HUGE = pltpu.CompilerParams(vmem_limit_bytes=56 * 1024 * 1024)
SMALL = pltpu.CompilerParams(vmem_limit_bytes=8 * 1024 * 1024)
LARGE = pltpu.CompilerParams(vmem_limit_bytes=28 * 1024 * 1024)


def ring(value, axes, steps):
    pairs = []
    for x in range(4):
        for z in range(4):
            for y in range(4):
                for core in range(2):
                    here = {"x": x, "z": z, "y": y, "core": core}
                    there = dict(here)
                    there[axes[core]] = (there[axes[core]] + steps[core]) % 4
                    pairs.append(
                        tuple(((p["x"] * 4 + p["z"]) * 4 + p["y"]) * 2 + p["core"] for p in (here, there))
                    )
    return lax.ppermute(value, AXES, pairs)


def swap_core(value):
    return lax.ppermute(value, "core", [(0, 1), (1, 0)])


def places():
    return tuple(lax.axis_index(name) for name in AXES)


def lane_orbitals(shape):
    lane = lax.broadcasted_iota(jnp.int32, shape, 1)
    a = jnp.floor((lane.astype(F32) + 0.5) * (1.0 / 36.0)).astype(jnp.int32)
    return a, lane - 36 * a


def window_copy(integrals, target, sem, chip):
    start = pl.multiple_of((chip & 3) * 2560, LANES)
    return pltpu.make_async_copy(integrals.at[:, :, pl.ds(start, DEPTH)], target.at[0:81], sem)


def open_step(occ_ref, vir_ref, amp_ref, integrals, keep_out, send_out, first_out, second_out, home_out,
              wide, amp, occ, vir, keep, send, first_v, second_v, home, sems, cut_sems, out_sems):
    x, z, y, core = places()
    copies = [
        pltpu.make_async_copy(source, target, sems.at[at])
        for at, (source, target) in enumerate(((occ_ref, occ), (vir_ref, vir), (amp_ref, amp)))
    ]
    cuts = [
        window_copy(integrals, first_v, cut_sems.at[0], y + 1 + 2 * core),
        window_copy(integrals, second_v, cut_sems.at[1], y + 3 - 2 * core),
        window_copy(integrals, home.at[0], cut_sems.at[2], y),
        window_copy(integrals, home.at[1], cut_sems.at[3], y + 2),
    ]
    outs = [
        pltpu.make_async_copy(source, target, out_sems.at[at])
        for at, (source, target) in enumerate(
            (
                (first_v, first_out),
                (second_v, second_out),
                (home.at[0], home_out.at[0]),
                (home.at[1], home_out.at[1]),
                (keep, keep_out),
                (send, send_out),
            )
        )
    ]
    for copy in copies + cuts:
        copy.start()
    wide[...] = jnp.zeros_like(wide)
    for copy in copies:
        copy.wait()
    for row in range(18):
        wide[row : row + 1, 0:1296] = amp[row // 6, row % 6]
    row_place = x * 4 + z
    occ_here = occ[row_place >> 1]
    first = 3 * (row_place & 1)
    irrep = 2 * y + core
    vir_here = vir[irrep]
    a, b = lane_orbitals(wide.shape)
    row = lax.broadcasted_iota(jnp.int32, wide.shape, 0)
    i_low = (row * 43) >> 8
    j = row - 6 * i_low
    live = (a < vir_here) & (b < vir_here) & (i_low + first < occ_here) & (j < occ_here)
    moved = pltpu.roll(jnp.where(live, wide[...], 0.0), 16 * irrep, 1)

    def write(ref, half):
        for t in range(TILES):
            columns = slice(t * LANES, (t + 1) * LANES)
            ref[8 * t : 8 * t + 8, :] = moved[8 * half : 8 * half + 8, columns]
            ref[MAIN + t : MAIN + t + 1, :] = moved[16 + half : 17 + half, columns]
        ref[MAIN + TILES : SHARD, :] = jnp.zeros((SHARD - MAIN - TILES, LANES), F32)

    @pl.when(core == 0)
    def _():
        write(keep, 0)
        write(send, 1)

    @pl.when(core == 1)
    def _():
        write(keep, 1)
        write(send, 0)

    for copy in outs[4:]:
        copy.start()
    for copy, out in zip(cuts, outs):
        copy.wait()
        out.start()
    for copy in outs:
        copy.wait()


def merge_irreps(even, odd, out, at):
    gap = SPAN - TILES
    out[at : at + 8 * gap, :] = even[0 : 8 * gap, :]
    out[at + 8 * gap : at + MAIN, :] = even[8 * gap : MAIN, :] + odd[0:8, :]
    out[at + MAIN : at + PMAIN, :] = odd[8:MAIN, :]
    extra = at + PMAIN
    out[extra : extra + gap, :] = even[MAIN : MAIN + gap, :]
    out[extra + gap : extra + TILES, :] = even[MAIN + gap : MAIN + TILES, :] + odd[MAIN : MAIN + 1, :]
    out[extra + TILES : extra + SPAN, :] = odd[MAIN + 1 : MAIN + TILES, :]
    out[extra + SPAN : at + PAIR, :] = jnp.zeros((PAIR - PMAIN - SPAN, LANES), F32)


def merge_pair(keep, got, home, out, home_out):
    core = lax.axis_index("core")

    @pl.when(core == 0)
    def _():
        merge_irreps(keep, got, out, 0)

    @pl.when(core == 1)
    def _():
        merge_irreps(got, keep, out, 0)


def join_pairs(near, far, home_other, out):
    out[0:PAIR, :] = near[...]
    out[PAIR:QUAD, :] = far[...]


def gather_four(b0, b1, b2, b3, near, far):
    for at, block in enumerate((b0, b1, b2, b3)):
        near[at * PAIR : (at + 1) * PAIR, :] = block[0:PAIR, :]
        far[at * PAIR : (at + 1) * PAIR, :] = block[PAIR:QUAD, :]


def nothing(*refs):
    pass


def hold(values, *witnesses):
    kept = range(len(values))
    return pl.pallas_call(
        nothing,
        out_shape=[jax.ShapeDtypeStruct(value.shape, value.dtype) for value in values],
        in_specs=[ANY] * (len(values) + len(witnesses)),
        out_specs=[ANY] * len(values),
        input_output_aliases={at: at for at in kept},
        compiler_params=SMALL,
    )(*values, *witnesses)


def left_side(blocks, extra):
    for t in range(SPAN):
        for d, block in enumerate(blocks):
            extra[4 * d : 4 * d + 4, t * LANES : (t + 1) * LANES] = block[pl.ds(PMAIN + t, 4, stride=PAIR), :]
    rows = []
    for block in blocks:
        for e in range(4):
            rows.append(
                jnp.concatenate(
                    [block[e * PAIR + 8 * t : e * PAIR + 8 * t + 8, :] for t in range(SPAN)], axis=1
                )
            )
    return split(jnp.concatenate(rows + [extra[...]], axis=0))


def split(value):
    high = value.astype(BF16)
    return high, (value - high.astype(F32)).astype(BF16)


def rows_side(ref, first):
    return jnp.concatenate([ref[pl.ds(first + t, PSLOT, stride=SPAN), :] for t in range(SPAN)], axis=1)


def last_by_last(p, q):
    return lax.dot_general(p, q, (((1,), (1,)), ((), ())), preferred_element_type=F32)


def split_home(home, home_other, witness, near_high, near_low, far_high, far_low):
    for side, ref in enumerate((home, home_other)):
        high, low = split(rows_side(ref, 0))
        rows = slice(side * PSLOT, (side + 1) * PSLOT)
        near_high[rows, :] = high
        near_low[rows, :] = low
        high, low = split(rows_side(ref, PROWS))
        pad = jnp.zeros((LANES - PSLOT, DEPTH), BF16)
        rows = slice(side * LANES, (side + 1) * LANES)
        far_high[rows, :] = jnp.concatenate([high, pad], axis=0)
        far_low[rows, :] = jnp.concatenate([low, pad], axis=0)


def turn_sums(total, refs, turned):
    turned[...] = jnp.zeros_like(turned)
    for at, ref in enumerate(refs):
        for side in range(2):
            rows = slice((2 * at + side) * PSLOT, (2 * at + side + 1) * PSLOT)
            turned[0:PSLOT, 0:144] = total[rows, :]
            ref[:, side * LANES : (side + 1) * LANES] = turned[...].T[0:144, :]


def pack_sides(first, second):
    lane = lax.broadcasted_iota(jnp.int32, (144, LANES), 1)
    turned = pltpu.roll(second, 81, 1)
    main = jnp.where(lane < 81, first, turned)
    low = lane[0:48]
    rest = jnp.where(
        low < 34,
        turned[0:48],
        jnp.where(low < 68, pltpu.roll(turned[48:96], 34, 1), pltpu.roll(turned[96:144], 68, 1)),
    )
    return jnp.concatenate([main, rest], axis=0)


def unpack_sides(packed):
    lane = lax.broadcasted_iota(jnp.int32, (144, LANES), 1)
    main, rest = packed[0:144], packed[144:192]
    tail = jnp.concatenate([pltpu.roll(rest, at, 1) for at in (47, 13, 107)], axis=0)
    second = jnp.where(lane < 47, pltpu.roll(main, 47, 1), tail)
    return jnp.concatenate([main, second], axis=1)


def multiply_moved(b0, b1, b2, b3, below, below_other, above, above_other,
                   below_sum, above_sum, high_out, low_out, extra, turned):
    high, low = left_side((b0, b1, b2, b3), extra)
    high_out[...] = high
    low_out[...] = low
    sides = [rows_side(ref, 0) for ref in (below, below_other, above, above_other)]
    v_high, v_low = split(jnp.concatenate(sides, axis=0))
    total = last_by_last(v_high, high) + (last_by_last(v_low, high) + last_by_last(v_high, low))
    turned[...] = jnp.zeros_like(turned)
    for at, ref in enumerate((below_sum, above_sum)):
        sides = []
        for side in range(2):
            turned[0:PSLOT, 0:144] = total[(2 * at + side) * PSLOT : (2 * at + side + 1) * PSLOT, :]
            sides.append(turned[...].T[0:144, :])
        ref[...] = pack_sides(*sides)


def multiply_home(high, low, v_high, v_low, below_sum, here_sum, turned):
    total = last_by_last(v_high[...], high[...]) + (
        last_by_last(v_low[...], high[...]) + last_by_last(v_high[...], low[...])
    )
    turn_sums(total, (here_sum,), turned)


def multiply_far(b0, b1, b2, b3, v_high, v_low, here_sum, back_a, back_b, out, extra):
    x, z, y, core = places()
    high, low = left_side((b0, b1, b2, b3), extra)
    partial = here_sum[...] + unpack_sides(back_a[...] + back_b[...])
    row = lax.broadcasted_iota(jnp.int32, (8, LANES), 0)
    lane = lax.broadcasted_iota(jnp.int32, (8, LANES), 1)
    total = partial + (
        last_by_last(high, v_high[...]) + (last_by_last(low, v_high[...]) + last_by_last(high, v_low[...]))
    )
    for side in range(2):
        columns = slice(side * LANES, (side + 1) * LANES)
        last = total[128:144, columns]
        last_a = pltpu.roll(last, 81, 1)
        last_b = pltpu.roll(last, 34, 1)
        core_there = core if side == 0 else 1 - core
        for d in range(4):
            for e in range(4):
                s = 4 * d + e
                x_step = jnp.where(core == 0, FIRST_STEPS[e], LAST_STEPS[d])
                z_step = jnp.where(core == 0, LAST_STEPS[d], FIRST_STEPS[e])
                there = ((x - x_step) & 3) * 4 + ((z - z_step) & 3)
                main = total[8 * s : 8 * s + 8, columns]
                tail = jnp.where(row == 0, last_a[s : s + 1, :], last_b[s : s + 1, :])
                out[there * 2 + core_there] = jnp.where(lane < 81, main, tail)


def local_step(occ_ref, vir_ref, eps_occ_ref, eps_vir_ref, amp_ref, ovov, partner,
               scale, cycle, amp, occ, vir, eps_occ, eps_vir, left_a, left_b, panel_a, panel_b, sems):
    x, z, y, core = places()
    copies = [
        pltpu.make_async_copy(source, target, sems.at[at])
        for at, (source, target) in enumerate(
            ((occ_ref, occ), (vir_ref, vir), (eps_occ_ref, eps_occ), (eps_vir_ref, eps_vir), (amp_ref, amp))
        )
    ]
    for copy in copies:
        copy.start()
    panel_a[...] = jnp.zeros_like(panel_a)
    panel_b[...] = jnp.zeros_like(panel_b)
    left_a[...] = jnp.zeros_like(left_a)
    left_b[...] = jnp.zeros_like(left_b)
    lower = (z & 1) == 0
    for r in range(108):
        own, other = ovov[r], partner[r]
        panel_a[r : r + 1, 0:216] = jnp.where(lower, own, other)
        panel_b[r : r + 1, 0:216] = jnp.where(lower, other, own)
    for copy in copies:
        copy.wait()
    row_place = x * 4 + z
    shell = row_place >> 1
    first = 3 * (row_place & 1)
    irrep = 2 * y + core
    a, b = lane_orbitals((1, 1296))
    energy_a = jnp.zeros((1, 1296), F32)
    energy_b = jnp.zeros((1, 1296), F32)
    for slot in range(36):
        value = eps_vir[irrep, slot]
        energy_a = jnp.where(a == slot, value, energy_a)
        energy_b = jnp.where(b == slot, value, energy_b)
    lane_live = (a < vir[irrep]) & (b < vir[irrep])
    occ_here = occ[shell]
    for r in range(18):
        low, k = r // 6, r % 6
        i = first + low
        here = lane_live & (i < occ_here) & (k < occ_here)
        gap = eps_occ[shell, i] + eps_occ[shell, k] - energy_a - energy_b
        scale[r : r + 1, :] = jnp.where(here, 1.0, 0.0) / gap
        live = jnp.where(here, amp[low, k], 0.0)
        left, column = (left_a, 36 * k) if k < 3 else (left_b, 36 * (k - 3))
        for slot in range(36):
            left[36 * low + slot : 36 * low + slot + 1, column : column + 36] = live[
                :, 36 * slot : 36 * slot + 36
            ]
    dot = lambda p, q: jnp.dot(p, q, preferred_element_type=F32)
    total = None
    for left, panel in ((left_a, panel_a), (left_b, panel_b)):
        p_high, p_low = split(left[:, 0:112])
        q_high, q_low = split(panel[...])
        part = dot(p_high, q_high) + (dot(p_low, q_high) + dot(p_high, q_low))
        total = part if total is None else total + part
    for low in range(3):
        for j in range(6):
            r = 6 * low + j
            for slot in range(36):
                cycle[r : r + 1, 36 * slot : 36 * slot + 36] = total[
                    36 * low + slot : 36 * low + slot + 1, 36 * j : 36 * j + 36
                ]


def finish(sums, scale, cycle, out, wide):
    wide[...] = jnp.zeros_like(wide)
    lane8 = lax.broadcasted_iota(jnp.int32, (1, LANES), 1)
    lane = lax.broadcasted_iota(jnp.int32, (24, LANES), 1)
    for r in range(16):
        mains, lasts = [], []
        for core in range(2):
            block = sums[2 * r + core]
            mains.append(block)
            lasts.append(
                jnp.where(lane8 < 47, pltpu.roll(block, 47, 1)[0:1, :], pltpu.roll(block, 94, 1)[1:2, :])
            )
        stack = jnp.concatenate(mains + lasts + [jnp.zeros((6, LANES), F32)], axis=0)
        tile, start = divmod(81 * r, LANES)
        turned = pltpu.roll(stack, start, 1) if start else stack
        here = slice(tile * LANES, (tile + 1) * LANES)
        wide[:, here] = jnp.where((lane >= start) & (lane < start + 81), turned, wide[:, here])
        if start + 81 > LANES:
            after = slice((tile + 1) * LANES, (tile + 2) * LANES)
            wide[:, after] = jnp.where(lane < start + 81 - LANES, turned, wide[:, after])
    total = (wide[0:18, 0:1296] + cycle[...]) * scale[...]
    for r in range(18):
        out[r // 6, r % 6] = total[r : r + 1, :]


def on_device(amplitudes, vvvv, ovov, eps_occ, eps_vir, occ_count, vir_count):
    x, z, y, core = places()
    shape = jax.ShapeDtypeStruct
    integrals = vvvv.reshape(81, 1, 10368)
    window = shape((PSLOT, 1, DEPTH), F32)
    flat = lambda value: value.reshape(PROWS, LANES)
    keep, send, first_v, second_v, home = pl.pallas_call(
        open_step,
        out_shape=[shape((SHARD, LANES), F32)] * 2 + [window] * 2
        + [shape((2, PSLOT, 1, DEPTH), F32)],
        in_specs=[HBM] * 4,
        out_specs=[ANY] * 5,
        scratch_shapes=[
            pltpu.VMEM((24, WINDOW), F32),
            pltpu.VMEM((3, 6, 1, 1296), F32),
            pltpu.SMEM((8,), jnp.int32),
            pltpu.SMEM((8,), jnp.int32),
            pltpu.VMEM((SHARD, LANES), F32),
            pltpu.VMEM((SHARD, LANES), F32),
            pltpu.VMEM((PSLOT, 1, DEPTH), F32),
            pltpu.VMEM((PSLOT, 1, DEPTH), F32),
            pltpu.VMEM((2, PSLOT, 1, DEPTH), F32),
            pltpu.SemaphoreType.DMA((3,)),
            pltpu.SemaphoreType.DMA((4,)),
            pltpu.SemaphoreType.DMA((6,)),
        ],
        compiler_params=HUGE,
    )(occ_count, vir_count, amplitudes, integrals)
    got = swap_core(send)
    moved_a = ring(flat(first_v), "yy", (1, -1))
    partner = lax.ppermute(ovov, "z", [(0, 1), (1, 0), (2, 3), (3, 2)])
    home = home.reshape(2 * PROWS, LANES)
    pair, home = pl.pallas_call(
        merge_pair,
        out_shape=[shape((PAIR, LANES), F32), shape(home.shape, F32)],
        in_specs=[VMEM] * 2 + [ANY],
        out_specs=[VMEM, ANY],
        input_output_aliases={2: 1},
        compiler_params=SMALL,
    )(keep, got, home)
    home_other = swap_core(home)
    far_pair = ring(pair, "yy", (2, 2))
    quad = pl.pallas_call(
        join_pairs,
        out_shape=shape((QUAD, LANES), F32),
        in_specs=[VMEM] * 2 + [ANY],
        out_specs=VMEM,
        compiler_params=SMALL,
    )(pair, far_pair, home_other)
    (second_v,) = hold([flat(second_v)], far_pair)
    moved_b = ring(second_v, "yy", (-1, 1))

    near, far = pl.pallas_call(
        gather_four,
        out_shape=[shape((4 * PAIR, LANES), F32)] * 2,
        in_specs=[VMEM] * 4,
        out_specs=[VMEM] * 2,
        compiler_params=SMALL,
    )(quad, *[ring(quad, "xz", (step, step)) for step in FIRST_STEPS[1:]])
    near_high, near_low, far_high, far_low = pl.pallas_call(
        split_home,
        out_shape=[shape((2 * PSLOT, DEPTH), BF16)] * 2 + [shape((2 * LANES, DEPTH), BF16)] * 2,
        in_specs=[VMEM] * 2 + [ANY],
        out_specs=[VMEM] * 4,
        compiler_params=LARGE,
        cost_estimate=pl.CostEstimate(flops=1, bytes_accessed=1, transcendentals=0),
    )(home, home_other, near)
    near_blocks = [near] + [ring(near, "zx", (step, step)) for step in LAST_STEPS[1:]]
    far_blocks = [far] + [ring(far, "zx", (step, step)) for step in LAST_STEPS[1:]]

    moved_a, moved_b = hold([moved_a, moved_b], *near_blocks[1:], near_high, partner)
    swapped_a, swapped_b = swap_core(moved_a), swap_core(moved_b)

    scale, cycle = pl.pallas_call(
        local_step,
        out_shape=[shape((18, 1296), F32)] * 2,
        in_specs=[HBM] * 5 + [VMEM] * 2,
        out_specs=[VMEM] * 2,
        scratch_shapes=[
            pltpu.VMEM((3, 6, 1, 1296), F32),
            pltpu.SMEM((8,), jnp.int32),
            pltpu.SMEM((8,), jnp.int32),
            pltpu.SMEM((8, 6), F32),
            pltpu.SMEM((8, 36), F32),
            pltpu.VMEM((112, 256), F32),
            pltpu.VMEM((112, 256), F32),
            pltpu.VMEM((112, 256), F32),
            pltpu.VMEM((112, 256), F32),
            pltpu.SemaphoreType.DMA((5,)),
        ],
        compiler_params=SMALL,
        cost_estimate=pl.CostEstimate(flops=100000000, bytes_accessed=1000000, transcendentals=0),
    )(occ_count, vir_count, eps_occ, eps_vir, amplitudes, ovov, partner)

    sums = shape((144, 2 * LANES), F32)
    left = shape((144, DEPTH), BF16)
    below_sum, above_sum, high, low = pl.pallas_call(
        multiply_moved,
        out_shape=[shape((192, LANES), F32)] * 2 + [left] * 2,
        in_specs=[VMEM] * 8,
        out_specs=[VMEM] * 4,
        scratch_shapes=[pltpu.VMEM((16, DEPTH), F32), pltpu.VMEM((LANES, 2 * LANES), F32)],
        compiler_params=LARGE,
    )(*near_blocks, moved_a, swapped_b, moved_b, swapped_a)
    back_a = ring(below_sum, "yy", (-1, 1))
    back_b = ring(above_sum, "yy", (1, -1))
    here_sum = pl.pallas_call(
        multiply_home,
        out_shape=sums,
        in_specs=[VMEM] * 4 + [ANY],
        out_specs=VMEM,
        scratch_shapes=[pltpu.VMEM((LANES, 2 * LANES), F32)],
        compiler_params=LARGE,
    )(high, low, near_high, near_low, below_sum)
    packed = pl.pallas_call(
        multiply_far,
        out_shape=shape((32, 8, LANES), F32),
        in_specs=[VMEM] * 9,
        out_specs=VMEM,
        scratch_shapes=[pltpu.VMEM((16, DEPTH), F32)],
        compiler_params=LARGE,
    )(*far_blocks, far_high, far_low, here_sum, back_a, back_b)
    ladder = lax.all_to_all(packed, ("x", "z", "core"), 0, 0, tiled=True)
    return pl.pallas_call(
        finish,
        out_shape=shape((3, 6, 1, 1296), F32),
        in_specs=[VMEM] * 3,
        out_specs=VMEM,
        scratch_shapes=[pltpu.VMEM((24, WINDOW), F32)],
        compiler_params=SMALL,
    )(ladder, scale, cycle)


def solution(mesh):
    fine = Mesh(mesh.devices.reshape(4, 4, 4, 2), AXES)
    rows, cols = ("x", "z"), ("y", "core")
    return jax.shard_map(
        on_device,
        mesh=fine,
        in_specs=(P(rows, None, cols, None), P(cols, rows, None), P(rows, cols, None), P(), P(), P(), P()),
        out_specs=P(rows, None, cols, None),
        check_vma=False,
    )
```

```python
import jax
import jax.numpy as jnp
from jax import lax
from jax.experimental import pallas as pl
from jax.experimental.pallas import tpu as pltpu
from jax.sharding import Mesh, PartitionSpec as P

AXES = ("x", "z", "y", "core")
FIRST_STEPS = (0, 1, -1, 2)
LAST_STEPS = (0, 2, 1, -1)
LANES = 128
TILES = 11
WINDOW = TILES * LANES
SPAN = 21
DEPTH = SPAN * LANES
MAIN = 8 * TILES
SHARD = 104
PMAIN = 8 * SPAN
PAIR = 192
QUAD = 2 * PAIR
PSLOT = 88
PROWS = SPAN * PSLOT
F32 = jnp.float32
BF16 = jnp.bfloat16
ANY = pl.BlockSpec(memory_space=pl.ANY)
HBM = pl.BlockSpec(memory_space=pltpu.HBM)
VMEM = pl.BlockSpec(memory_space=pltpu.VMEM)
HUGE = pltpu.CompilerParams(vmem_limit_bytes=56 * 1024 * 1024)
SMALL = pltpu.CompilerParams(vmem_limit_bytes=8 * 1024 * 1024)
LARGE = pltpu.CompilerParams(vmem_limit_bytes=28 * 1024 * 1024)


def ring(value, axes, steps):
    pairs = []
    for x in range(4):
        for z in range(4):
            for y in range(4):
                for core in range(2):
                    here = {"x": x, "z": z, "y": y, "core": core}
                    there = dict(here)
                    there[axes[core]] = (there[axes[core]] + steps[core]) % 4
                    pairs.append(
                        tuple(((p["x"] * 4 + p["z"]) * 4 + p["y"]) * 2 + p["core"] for p in (here, there))
                    )
    return lax.ppermute(value, AXES, pairs)


def swap_core(value):
    return lax.ppermute(value, "core", [(0, 1), (1, 0)])


def places():
    return tuple(lax.axis_index(name) for name in AXES)


def lane_orbitals(shape):
    lane = lax.broadcasted_iota(jnp.int32, shape, 1)
    a = jnp.floor((lane.astype(F32) + 0.5) * (1.0 / 36.0)).astype(jnp.int32)
    return a, lane - 36 * a


def window_copy(integrals, target, sem, chip):
    start = pl.multiple_of((chip & 3) * 2560, LANES)
    return pltpu.make_async_copy(integrals.at[:, :, pl.ds(start, DEPTH)], target.at[0:81], sem)


def open_step(occ_ref, vir_ref, amp_ref, integrals, keep_out, send_out, first_out, second_out, home_out,
              wide, amp, occ, vir, keep, send, first_v, second_v, home, sems, cut_sems, out_sems):
    x, z, y, core = places()
    copies = [
        pltpu.make_async_copy(source, target, sems.at[at])
        for at, (source, target) in enumerate(((occ_ref, occ), (vir_ref, vir), (amp_ref, amp)))
    ]
    cuts = [
        window_copy(integrals, first_v, cut_sems.at[0], y + 3 - 2 * core),
        window_copy(integrals, second_v, cut_sems.at[1], y + 1 + 2 * core),
        window_copy(integrals, home.at[0], cut_sems.at[2], y),
        window_copy(integrals, home.at[1], cut_sems.at[3], y + 2),
    ]
    outs = [
        pltpu.make_async_copy(source, target, out_sems.at[at])
        for at, (source, target) in enumerate(
            (
                (first_v, first_out),
                (second_v, second_out),
                (home.at[0], home_out.at[0]),
                (home.at[1], home_out.at[1]),
                (keep, keep_out),
                (send, send_out),
            )
        )
    ]
    for copy in copies + cuts:
        copy.start()
    wide[...] = jnp.zeros_like(wide)
    for copy in copies:
        copy.wait()
    for row in range(18):
        wide[row : row + 1, 0:1296] = amp[row // 6, row % 6]
    row_place = x * 4 + z
    occ_here = occ[row_place >> 1]
    first = 3 * (row_place & 1)
    irrep = 2 * y + core
    vir_here = vir[irrep]
    a, b = lane_orbitals(wide.shape)
    row = lax.broadcasted_iota(jnp.int32, wide.shape, 0)
    i_low = (row * 43) >> 8
    j = row - 6 * i_low
    live = (a < vir_here) & (b < vir_here) & (i_low + first < occ_here) & (j < occ_here)
    moved = pltpu.roll(jnp.where(live, wide[...], 0.0), 16 * irrep, 1)

    def write(ref, half):
        for t in range(TILES):
            columns = slice(t * LANES, (t + 1) * LANES)
            ref[8 * t : 8 * t + 8, :] = moved[8 * half : 8 * half + 8, columns]
            ref[MAIN + t : MAIN + t + 1, :] = moved[16 + half : 17 + half, columns]
        ref[MAIN + TILES : SHARD, :] = jnp.zeros((SHARD - MAIN - TILES, LANES), F32)

    @pl.when(core == 0)
    def _():
        write(keep, 0)
        write(send, 1)

    @pl.when(core == 1)
    def _():
        write(keep, 1)
        write(send, 0)

    for copy in outs[4:]:
        copy.start()
    for copy, out in zip(cuts, outs):
        copy.wait()
        out.start()
    for copy in outs:
        copy.wait()


def merge_irreps(even, odd, out, at):
    gap = SPAN - TILES
    out[at : at + 8 * gap, :] = even[0 : 8 * gap, :]
    out[at + 8 * gap : at + MAIN, :] = even[8 * gap : MAIN, :] + odd[0:8, :]
    out[at + MAIN : at + PMAIN, :] = odd[8:MAIN, :]
    extra = at + PMAIN
    out[extra : extra + gap, :] = even[MAIN : MAIN + gap, :]
    out[extra + gap : extra + TILES, :] = even[MAIN + gap : MAIN + TILES, :] + odd[MAIN : MAIN + 1, :]
    out[extra + TILES : extra + SPAN, :] = odd[MAIN + 1 : MAIN + TILES, :]
    out[extra + SPAN : at + PAIR, :] = jnp.zeros((PAIR - PMAIN - SPAN, LANES), F32)


def merge_pair(keep, got, home, out, home_out):
    core = lax.axis_index("core")

    @pl.when(core == 0)
    def _():
        merge_irreps(keep, got, out, 0)

    @pl.when(core == 1)
    def _():
        merge_irreps(got, keep, out, 0)


def join_pairs(near, far, home_other, out):
    out[0:PAIR, :] = near[...]
    out[PAIR:QUAD, :] = far[...]


def gather_four(b0, b1, b2, b3, near, far):
    for at, block in enumerate((b0, b1, b2, b3)):
        near[at * PAIR : (at + 1) * PAIR, :] = block[0:PAIR, :]
        far[at * PAIR : (at + 1) * PAIR, :] = block[PAIR:QUAD, :]


def nothing(*refs):
    pass


def hold(values, *witnesses):
    kept = range(len(values))
    return pl.pallas_call(
        nothing,
        out_shape=[jax.ShapeDtypeStruct(value.shape, value.dtype) for value in values],
        in_specs=[ANY] * (len(values) + len(witnesses)),
        out_specs=[ANY] * len(values),
        input_output_aliases={at: at for at in kept},
        compiler_params=SMALL,
    )(*values, *witnesses)


def left_side(blocks, extra):
    for t in range(SPAN):
        for d, block in enumerate(blocks):
            extra[4 * d : 4 * d + 4, t * LANES : (t + 1) * LANES] = block[pl.ds(PMAIN + t, 4, stride=PAIR), :]
    rows = []
    for block in blocks:
        for e in range(4):
            rows.append(
                jnp.concatenate(
                    [block[e * PAIR + 8 * t : e * PAIR + 8 * t + 8, :] for t in range(SPAN)], axis=1
                )
            )
    return split(jnp.concatenate(rows + [extra[...]], axis=0))


def split(value):
    high = value.astype(BF16)
    return high, (value - high.astype(F32)).astype(BF16)


def rows_side(ref, first):
    return jnp.concatenate([ref[pl.ds(first + t, PSLOT, stride=SPAN), :] for t in range(SPAN)], axis=1)


def last_by_last(p, q):
    return lax.dot_general(p, q, (((1,), (1,)), ((), ())), preferred_element_type=F32)


def split_home(home, home_other, witness, near_high, near_low, far_high, far_low):
    for side, ref in enumerate((home, home_other)):
        high, low = split(rows_side(ref, 0))
        rows = slice(side * PSLOT, (side + 1) * PSLOT)
        near_high[rows, :] = high
        near_low[rows, :] = low
        high, low = split(rows_side(ref, PROWS))
        pad = jnp.zeros((LANES - PSLOT, DEPTH), BF16)
        rows = slice(side * LANES, (side + 1) * LANES)
        far_high[rows, :] = jnp.concatenate([high, pad], axis=0)
        far_low[rows, :] = jnp.concatenate([low, pad], axis=0)


def turn_sums(total, refs, turned):
    turned[...] = jnp.zeros_like(turned)
    for at, ref in enumerate(refs):
        for side in range(2):
            rows = slice((2 * at + side) * PSLOT, (2 * at + side + 1) * PSLOT)
            turned[0:PSLOT, 0:144] = total[rows, :]
            ref[:, side * LANES : (side + 1) * LANES] = turned[...].T[0:144, :]


def pack_sides(first, second):
    lane = lax.broadcasted_iota(jnp.int32, (144, LANES), 1)
    turned = pltpu.roll(second, 81, 1)
    main = jnp.where(lane < 81, first, turned)
    low = lane[0:48]
    rest = jnp.where(
        low < 34,
        turned[0:48],
        jnp.where(low < 68, pltpu.roll(turned[48:96], 34, 1), pltpu.roll(turned[96:144], 68, 1)),
    )
    return jnp.concatenate([main, rest], axis=0)


def unpack_sides(packed):
    lane = lax.broadcasted_iota(jnp.int32, (144, LANES), 1)
    main, rest = packed[0:144], packed[144:192]
    tail = jnp.concatenate([pltpu.roll(rest, at, 1) for at in (47, 13, 107)], axis=0)
    second = jnp.where(lane < 47, pltpu.roll(main, 47, 1), tail)
    return jnp.concatenate([main, second], axis=1)


def multiply_moved(b0, b1, b2, b3, below, below_other, above, above_other,
                   below_sum, above_sum, high_out, low_out, extra, turned):
    high, low = left_side((b0, b1, b2, b3), extra)
    high_out[...] = high
    low_out[...] = low
    sides = [rows_side(ref, 0) for ref in (below, below_other, above, above_other)]
    v_high, v_low = split(jnp.concatenate(sides, axis=0))
    total = last_by_last(v_high, high) + (last_by_last(v_low, high) + last_by_last(v_high, low))
    turned[...] = jnp.zeros_like(turned)
    for at, ref in enumerate((below_sum, above_sum)):
        sides = []
        for side in range(2):
            turned[0:PSLOT, 0:144] = total[(2 * at + side) * PSLOT : (2 * at + side + 1) * PSLOT, :]
            sides.append(turned[...].T[0:144, :])
        ref[...] = pack_sides(*sides)


def multiply_home(high, low, v_high, v_low, below_sum, here_sum, turned):
    total = last_by_last(v_high[...], high[...]) + (
        last_by_last(v_low[...], high[...]) + last_by_last(v_high[...], low[...])
    )
    turn_sums(total, (here_sum,), turned)


def multiply_far(b0, b1, b2, b3, v_high, v_low, here_sum, back_a, back_b, out, extra):
    x, z, y, core = places()
    high, low = left_side((b0, b1, b2, b3), extra)
    partial = here_sum[...] + unpack_sides(back_a[...] + back_b[...])
    row = lax.broadcasted_iota(jnp.int32, (8, LANES), 0)
    lane = lax.broadcasted_iota(jnp.int32, (8, LANES), 1)
    total = partial + (
        last_by_last(high, v_high[...]) + (last_by_last(low, v_high[...]) + last_by_last(high, v_low[...]))
    )
    for side in range(2):
        columns = slice(side * LANES, (side + 1) * LANES)
        last = total[128:144, columns]
        last_a = pltpu.roll(last, 81, 1)
        last_b = pltpu.roll(last, 34, 1)
        core_there = core if side == 0 else 1 - core
        for d in range(4):
            for e in range(4):
                s = 4 * d + e
                x_step = jnp.where(core == 0, FIRST_STEPS[e], LAST_STEPS[d])
                z_step = jnp.where(core == 0, LAST_STEPS[d], FIRST_STEPS[e])
                there = ((x - x_step) & 3) * 4 + ((z - z_step) & 3)
                main = total[8 * s : 8 * s + 8, columns]
                tail = jnp.where(row == 0, last_a[s : s + 1, :], last_b[s : s + 1, :])
                out[there * 2 + core_there] = jnp.where(lane < 81, main, tail)


def local_step(occ_ref, vir_ref, eps_occ_ref, eps_vir_ref, amp_ref, ovov, partner,
               scale, cycle, amp, occ, vir, eps_occ, eps_vir, left_a, left_b, panel_a, panel_b, sems):
    x, z, y, core = places()
    copies = [
        pltpu.make_async_copy(source, target, sems.at[at])
        for at, (source, target) in enumerate(
            ((occ_ref, occ), (vir_ref, vir), (eps_occ_ref, eps_occ), (eps_vir_ref, eps_vir), (amp_ref, amp))
        )
    ]
    for copy in copies:
        copy.start()
    panel_a[...] = jnp.zeros_like(panel_a)
    panel_b[...] = jnp.zeros_like(panel_b)
    left_a[...] = jnp.zeros_like(left_a)
    left_b[...] = jnp.zeros_like(left_b)
    lower = (z & 1) == 0
    for r in range(108):
        own, other = ovov[r], partner[r]
        panel_a[r : r + 1, 0:216] = jnp.where(lower, own, other)
        panel_b[r : r + 1, 0:216] = jnp.where(lower, other, own)
    for copy in copies:
        copy.wait()
    row_place = x * 4 + z
    shell = row_place >> 1
    first = 3 * (row_place & 1)
    irrep = 2 * y + core
    a, b = lane_orbitals((1, 1296))
    energy_a = jnp.zeros((1, 1296), F32)
    energy_b = jnp.zeros((1, 1296), F32)
    for slot in range(36):
        value = eps_vir[irrep, slot]
        energy_a = jnp.where(a == slot, value, energy_a)
        energy_b = jnp.where(b == slot, value, energy_b)
    lane_live = (a < vir[irrep]) & (b < vir[irrep])
    occ_here = occ[shell]
    for r in range(18):
        low, k = r // 6, r % 6
        i = first + low
        here = lane_live & (i < occ_here) & (k < occ_here)
        gap = eps_occ[shell, i] + eps_occ[shell, k] - energy_a - energy_b
        scale[r : r + 1, :] = jnp.where(here, 1.0, 0.0) / gap
        live = jnp.where(here, amp[low, k], 0.0)
        left, column = (left_a, 36 * k) if k < 3 else (left_b, 36 * (k - 3))
        for slot in range(36):
            left[36 * low + slot : 36 * low + slot + 1, column : column + 36] = live[
                :, 36 * slot : 36 * slot + 36
            ]
    dot = lambda p, q: jnp.dot(p, q, preferred_element_type=F32)
    total = None
    for left, panel in ((left_a, panel_a), (left_b, panel_b)):
        p_high, p_low = split(left[:, 0:112])
        q_high, q_low = split(panel[...])
        part = dot(p_high, q_high) + (dot(p_low, q_high) + dot(p_high, q_low))
        total = part if total is None else total + part
    for low in range(3):
        for j in range(6):
            r = 6 * low + j
            for slot in range(36):
                cycle[r : r + 1, 36 * slot : 36 * slot + 36] = total[
                    36 * low + slot : 36 * low + slot + 1, 36 * j : 36 * j + 36
                ]


def finish(sums, scale, cycle, out, wide):
    wide[...] = jnp.zeros_like(wide)
    lane8 = lax.broadcasted_iota(jnp.int32, (1, LANES), 1)
    lane = lax.broadcasted_iota(jnp.int32, (24, LANES), 1)
    for r in range(16):
        mains, lasts = [], []
        for core in range(2):
            block = sums[2 * r + core]
            mains.append(block)
            lasts.append(
                jnp.where(lane8 < 47, pltpu.roll(block, 47, 1)[0:1, :], pltpu.roll(block, 94, 1)[1:2, :])
            )
        stack = jnp.concatenate(mains + lasts + [jnp.zeros((6, LANES), F32)], axis=0)
        tile, start = divmod(81 * r, LANES)
        turned = pltpu.roll(stack, start, 1) if start else stack
        here = slice(tile * LANES, (tile + 1) * LANES)
        wide[:, here] = jnp.where((lane >= start) & (lane < start + 81), turned, wide[:, here])
        if start + 81 > LANES:
            after = slice((tile + 1) * LANES, (tile + 2) * LANES)
            wide[:, after] = jnp.where(lane < start + 81 - LANES, turned, wide[:, after])
    total = (wide[0:18, 0:1296] + cycle[...]) * scale[...]
    for r in range(18):
        out[r // 6, r % 6] = total[r : r + 1, :]


def on_device(amplitudes, vvvv, ovov, eps_occ, eps_vir, occ_count, vir_count):
    x, z, y, core = places()
    shape = jax.ShapeDtypeStruct
    integrals = vvvv.reshape(81, 1, 10368)
    window = shape((PSLOT, 1, DEPTH), F32)
    flat = lambda value: value.reshape(PROWS, LANES)
    keep, send, first_v, second_v, home = pl.pallas_call(
        open_step,
        out_shape=[shape((SHARD, LANES), F32)] * 2 + [window] * 2
        + [shape((2, PSLOT, 1, DEPTH), F32)],
        in_specs=[HBM] * 4,
        out_specs=[ANY] * 5,
        scratch_shapes=[
            pltpu.VMEM((24, WINDOW), F32),
            pltpu.VMEM((3, 6, 1, 1296), F32),
            pltpu.SMEM((8,), jnp.int32),
            pltpu.SMEM((8,), jnp.int32),
            pltpu.VMEM((SHARD, LANES), F32),
            pltpu.VMEM((SHARD, LANES), F32),
            pltpu.VMEM((PSLOT, 1, DEPTH), F32),
            pltpu.VMEM((PSLOT, 1, DEPTH), F32),
            pltpu.VMEM((2, PSLOT, 1, DEPTH), F32),
            pltpu.SemaphoreType.DMA((3,)),
            pltpu.SemaphoreType.DMA((4,)),
            pltpu.SemaphoreType.DMA((6,)),
        ],
        compiler_params=HUGE,
    )(occ_count, vir_count, amplitudes, integrals)
    got = swap_core(send)
    moved_a = ring(flat(first_v), "yy", (-1, 1))
    partner = lax.ppermute(ovov, "z", [(0, 1), (1, 0), (2, 3), (3, 2)])
    home = home.reshape(2 * PROWS, LANES)
    pair, home = pl.pallas_call(
        merge_pair,
        out_shape=[shape((PAIR, LANES), F32), shape(home.shape, F32)],
        in_specs=[VMEM] * 2 + [ANY],
        out_specs=[VMEM, ANY],
        input_output_aliases={2: 1},
        compiler_params=SMALL,
    )(keep, got, home)
    home_other = swap_core(home)
    far_pair = ring(pair, "yy", (2, 2))
    quad = pl.pallas_call(
        join_pairs,
        out_shape=shape((QUAD, LANES), F32),
        in_specs=[VMEM] * 2 + [ANY],
        out_specs=VMEM,
        compiler_params=SMALL,
    )(pair, far_pair, home_other)
    (second_v,) = hold([flat(second_v)], far_pair)
    moved_b = ring(second_v, "yy", (1, -1))

    near, far = pl.pallas_call(
        gather_four,
        out_shape=[shape((4 * PAIR, LANES), F32)] * 2,
        in_specs=[VMEM] * 4,
        out_specs=[VMEM] * 2,
        compiler_params=SMALL,
    )(quad, *[ring(quad, "xz", (step, step)) for step in FIRST_STEPS[1:]])
    near_high, near_low, far_high, far_low = pl.pallas_call(
        split_home,
        out_shape=[shape((2 * PSLOT, DEPTH), BF16)] * 2 + [shape((2 * LANES, DEPTH), BF16)] * 2,
        in_specs=[VMEM] * 2 + [ANY],
        out_specs=[VMEM] * 4,
        compiler_params=LARGE,
        cost_estimate=pl.CostEstimate(flops=1, bytes_accessed=1, transcendentals=0),
    )(home, home_other, near)
    near_blocks = [near] + [ring(near, "zx", (step, step)) for step in LAST_STEPS[1:]]
    far_blocks = [far] + [ring(far, "zx", (step, step)) for step in LAST_STEPS[1:]]

    moved_a, moved_b = hold([moved_a, moved_b], *near_blocks[1:], near_high, partner)
    swapped_a, swapped_b = swap_core(moved_a), swap_core(moved_b)

    scale, cycle = pl.pallas_call(
        local_step,
        out_shape=[shape((18, 1296), F32)] * 2,
        in_specs=[HBM] * 5 + [VMEM] * 2,
        out_specs=[VMEM] * 2,
        scratch_shapes=[
            pltpu.VMEM((3, 6, 1, 1296), F32),
            pltpu.SMEM((8,), jnp.int32),
            pltpu.SMEM((8,), jnp.int32),
            pltpu.SMEM((8, 6), F32),
            pltpu.SMEM((8, 36), F32),
            pltpu.VMEM((112, 256), F32),
            pltpu.VMEM((112, 256), F32),
            pltpu.VMEM((112, 256), F32),
            pltpu.VMEM((112, 256), F32),
            pltpu.SemaphoreType.DMA((5,)),
        ],
        compiler_params=SMALL,
        cost_estimate=pl.CostEstimate(flops=100000000, bytes_accessed=1000000, transcendentals=0),
    )(occ_count, vir_count, eps_occ, eps_vir, amplitudes, ovov, partner)

    sums = shape((144, 2 * LANES), F32)
    left = shape((144, DEPTH), BF16)
    below_sum, above_sum, high, low = pl.pallas_call(
        multiply_moved,
        out_shape=[shape((192, LANES), F32)] * 2 + [left] * 2,
        in_specs=[VMEM] * 8,
        out_specs=[VMEM] * 4,
        scratch_shapes=[pltpu.VMEM((16, DEPTH), F32), pltpu.VMEM((LANES, 2 * LANES), F32)],
        compiler_params=LARGE,
    )(*near_blocks, moved_a, swapped_b, moved_b, swapped_a)
    back_a = ring(below_sum, "yy", (1, -1))
    back_b = ring(above_sum, "yy", (-1, 1))
    here_sum = pl.pallas_call(
        multiply_home,
        out_shape=sums,
        in_specs=[VMEM] * 4 + [ANY],
        out_specs=VMEM,
        scratch_shapes=[pltpu.VMEM((LANES, 2 * LANES), F32)],
        compiler_params=LARGE,
    )(high, low, near_high, near_low, below_sum)
    packed = pl.pallas_call(
        multiply_far,
        out_shape=shape((32, 8, LANES), F32),
        in_specs=[VMEM] * 9,
        out_specs=VMEM,
        scratch_shapes=[pltpu.VMEM((16, DEPTH), F32)],
        compiler_params=LARGE,
    )(*far_blocks, far_high, far_low, here_sum, back_a, back_b)
    ladder = lax.all_to_all(packed, ("x", "z", "core"), 0, 0, tiled=True)
    return pl.pallas_call(
        finish,
        out_shape=shape((3, 6, 1, 1296), F32),
        in_specs=[VMEM] * 3,
        out_specs=VMEM,
        scratch_shapes=[pltpu.VMEM((24, WINDOW), F32)],
        compiler_params=SMALL,
    )(ladder, scale, cycle)


def solution(mesh):
    fine = Mesh(mesh.devices.reshape(4, 4, 4, 2), AXES)
    rows, cols = ("x", "z"), ("y", "core")
    return jax.shard_map(
        on_device,
        mesh=fine,
        in_specs=(P(rows, None, cols, None), P(cols, rows, None), P(rows, cols, None), P(), P(), P(), P()),
        out_specs=P(rows, None, cols, None),
        check_vma=False,
    )
```
